32 devices in a mesh: half: 2 (over core), prow: 8 (over z, x), pcol: 2 (over y).
Axes of the slice: x: 2, y: 2, z: 4, core: 2. Of those that a mesh axis runs over, the one named last changes fastest.
Arguments:
- child_update: float32 [2, 8192, 8192], P('half', 'prow', 'pcol'), may hold values from -6 to 6, as said below
- child_panel: float32 [2, 8192, 1024], P('half', 'prow'), may hold values from -3 to 3
- root_front: float32 [12288, 12288], P('prow', ('half', 'pcol')), may hold values from -29 to 6144, as said below
- index_map: int32 [2, 64], replicated, may hold values from 0 to 95, as said below
Outputs:
- root_next: float32 [12288, 12288], P('prow', ('half', 'pcol'))
The draws below stay inside these ranges and needn't reach their ends.
Inputs may be any that keep to these rules, and one draw needn't show every extreme that they name: `child_update`: each child's matrix is symmetric. `root_front`: Symmetric. `index_map`: for each child the entries are distinct, and child 0 names the blocks 0 to 1. Of the 16 blocks of one process row of both children (blocks p * 8 on), at most 2 share one root process row v // 12; of the 32 blocks of one child process column (blocks q * 32 on), at most 8 share one root column group v // 24; both bounds are reached.
All inputs are finite; a program needn't handle non-finite values.
Results may differ from the reference program's by a relative error of at most 0.00016.
Values sent between devices are 32-bit elements; how exact they have to be, the bound alone decides.
No kernel may reach another device: no remote copies, remote signals or barrier semaphores. Data moves between devices by JAX's collectives and lax.ppermute only.
A program may use at most 192 MiB of HBM per device.

```python
import jax
import jax.numpy as jnp
from jax import lax

BLK = 128
MBLK = 64
RBLK = 96
RPB = 2
PANEL = 1024
CHILD = 8192
NR = 12288
RP = 256
N_PROW = 8
N_PCOL = 2


def draw_child_update(key, part):
    values = jax.random.truncated_normal(key, -4.0, 4.0, (2, CHILD, CHILD), jnp.float32)
    return (values + jnp.swapaxes(values, 1, 2)) * 0.7071


def draw_root_front(key, part):
    key_base, key_off, key_diag = jax.random.split(key, 3)
    values = jax.random.truncated_normal(key_base, -4.0, 4.0, (NR, NR), jnp.float32)
    values = (values + values.T) * 0.7071
    values = values.at[RP:, :RP].multiply(5.0).at[:RP, RP:].multiply(5.0)
    coupling = jax.random.uniform(key_off, (RP, RP), jnp.float32, -1.0, 1.0)
    coupling = 0.5 * (coupling + coupling.T)
    diagonal = jax.random.uniform(key_diag, (RP,), jnp.float32, 16.0 * RP, 24.0 * RP)
    identity = jnp.eye(RP, dtype=jnp.float32)
    pivot_block = coupling * (1.0 - identity) + identity * diagonal[None, :]
    return values.at[:RP, :RP].set(pivot_block)


def draw_index_map(key, part):
    child_rows = MBLK // N_PROW
    root_rows = RBLK // N_PROW
    width = N_PROW // (2 * N_PCOL)
    key_off, key_group, key_item, key_slot = jax.random.split(key, 4)
    offset = jax.random.randint(key_off, (), 0, N_PROW)
    group_perm = jax.random.permutation(key_group, 2 * N_PCOL).astype(jnp.int32)
    item_perm = jax.vmap(lambda subkey: jax.random.permutation(subkey, child_rows))(jax.random.split(key_item, 2 * N_PROW)).reshape(2, N_PROW, child_rows)
    blocks = jnp.arange(N_PROW, dtype=jnp.int32)[None, :, None] * child_rows + item_perm.astype(jnp.int32)
    child_shift = jnp.arange(2, dtype=jnp.int32)[:, None, None] * child_rows
    base = (blocks + child_shift + offset) % N_PROW
    owner = (jnp.take(group_perm, base // width) * width + base % width).reshape(2, MBLK).astype(jnp.int32)
    onehot = (owner[:, :, None] == jnp.arange(N_PROW, dtype=jnp.int32)[None, None, :]).astype(jnp.int32)
    ranks = jnp.sum((jnp.cumsum(onehot, axis=1) - 1) * onehot, axis=2)
    slot_orders = jax.vmap(lambda subkey: jax.random.permutation(subkey, root_rows))(jax.random.split(key_slot, 2 * N_PROW)).reshape(2, N_PROW, root_rows).astype(jnp.int32)
    forced = jnp.zeros((2, N_PROW, root_rows), jnp.int32)
    forced = forced.at[0, 0, :RPB].set(1).at[0, N_PROW - 1, root_rows - 1].set(1)
    priority = slot_orders - forced * root_rows
    slot_table = jnp.argsort(priority, axis=2).astype(jnp.int32).reshape(2, N_PROW * root_rows)
    slots = jnp.take_along_axis(slot_table, owner * root_rows + ranks, axis=1)
    return (owner * root_rows + slots).astype(jnp.int32)


def block_levels(key, extent, shards, least, largest):
    factor_of = 1.0
    for axis_at, parts in shards:
        heights = jax.random.uniform(jax.random.fold_in(jax.random.fold_in(key, 6), axis_at), (parts,), jnp.float32, least / len(shards), largest / len(shards))
        factor_of = factor_of * jnp.repeat(jnp.exp(heights), extent[axis_at] // parts).reshape((-1,) + (1,) * (len(extent) - 1 - axis_at))
    return factor_of


def bell_draw(key, dims, spread, reach, pieces=(), kind=jnp.bfloat16):
    array = spread * jax.random.normal(key, dims, jnp.float32)
    if pieces:
        array = array * block_levels(key, dims, pieces, -0.22, 0.18)
    return jnp.clip(array, -reach, reach).astype(kind)


def setup_inputs(seed: int = 0) -> dict:
    key_of = jax.random.split(jax.random.key(seed), 5)
    return {
        "child_update": draw_child_update(jax.random.fold_in(key_of[4], 71), 0),
        "child_panel": bell_draw(key_of[1], (2, CHILD, PANEL), 0.2, 3.0, ((0, 2), (1, 8)), jnp.float32),
        "root_front": draw_root_front(jax.random.fold_in(key_of[4], 71), 0),
        "index_map": draw_index_map(jax.random.fold_in(key_of[4], 71), 0),
    }


def reference(child_update, child_panel, root_front, index_map):
    root_blocks = root_front.reshape(RBLK, BLK, RBLK, BLK)
    for child_index in range(2):
        panel_part = child_panel[child_index]
        product = lax.dot_general(panel_part.astype(jnp.float32), panel_part.astype(jnp.float32), (((1,), (1,)), ((), ())), precision=lax.Precision.HIGHEST, preferred_element_type=jnp.float32)
        schur_part = child_update[child_index] - product
        child_tiles = schur_part.reshape(MBLK, BLK, MBLK, BLK).transpose(0, 2, 1, 3)
        targets = index_map[child_index].astype(jnp.int32)
        root_blocks = root_blocks.at[targets[:, None], :, targets[None, :], :].add(child_tiles)
    assembled = root_blocks.reshape(NR, NR)
    factor = jnp.linalg.cholesky(assembled[:RP, :RP])
    lower = lax.linalg.triangular_solve(factor, assembled[RP:, :RP], left_side=False, lower=True, transpose_a=True)
    update = lax.dot_general(lower.astype(jnp.float32), lower.astype(jnp.float32), (((1,), (1,)), ((), ())), precision=lax.Precision.HIGHEST, preferred_element_type=jnp.float32)
    trailing = assembled[RP:, RP:] - update
    panel_cols = jnp.concatenate([factor, lower], axis=0)
    right_side = jnp.concatenate([assembled[:RP, RP:], trailing], axis=0)
    return jnp.concatenate([panel_cols, right_side], axis=1)
```

```python
import functools

import jax
import jax.numpy as jnp
from jax import lax
from jax.experimental import pallas as pl
from jax.experimental.pallas import tpu as pltpu
from jax.sharding import PartitionSpec as P

BLK = 128
RP = 256
F32 = jnp.float32
BF16 = jnp.bfloat16
HIGHEST = lax.Precision.HIGHEST
NT = (((1,), (1,)), ((), ()))
VMEM_LIMIT = 56 * 1024 * 1024


def split(x):
    hi = x.astype(BF16)
    lo = (x - hi.astype(F32)).astype(BF16)
    return hi, lo


def dot_nt(a, b):
    return lax.dot_general(a, b, NT, preferred_element_type=F32)


def params():
    return pltpu.CompilerParams(vmem_limit_bytes=VMEM_LIMIT)


def cost(flops, nbytes):
    return pl.CostEstimate(flops=int(flops), bytes_accessed=int(nbytes), transcendentals=0)


def pack_columns(update, chosen):
    rows = update.shape[0]
    groups, width = chosen.shape

    def body(chosen_ref, in_ref, out_ref):
        out_ref[0, 0] = in_ref[...]

    return pl.pallas_call(
        body,
        grid_spec=pltpu.PrefetchScalarGridSpec(
            num_scalar_prefetch=1,
            grid=(groups, width),
            in_specs=[pl.BlockSpec((rows, BLK), lambda g, u, s: (0, s[g * width + u]))],
            out_specs=pl.BlockSpec((1, 1, rows, BLK), lambda g, u, s: (g, u, 0, 0)),
        ),
        out_shape=jax.ShapeDtypeStruct((groups, width, rows, BLK), F32),
        compiler_params=params(),
        cost_estimate=cost(0, 8 * groups * width * rows * BLK),
    )(chosen.reshape(-1), update)


def pick_rows(own, other, block, mine):
    count = block.shape[0]
    depth = own.shape[1]

    def body(block_ref, mine_ref, own_ref, other_ref, out_ref):
        s = pl.program_id(0)

        @pl.when(mine_ref[s] == 1)
        def _():
            out_ref[0] = own_ref[...]

        @pl.when(mine_ref[s] == 0)
        def _():
            out_ref[0] = other_ref[...]

    spec = pl.BlockSpec((BLK, depth), lambda s, b, m: (b[s], 0))
    return pl.pallas_call(
        body,
        grid_spec=pltpu.PrefetchScalarGridSpec(
            num_scalar_prefetch=2,
            grid=(count,),
            in_specs=[spec, spec],
            out_specs=pl.BlockSpec((1, BLK, depth), lambda s, b, m: (s, 0, 0)),
        ),
        out_shape=jax.ShapeDtypeStruct((count, BLK, depth), F32),
        compiler_params=params(),
        cost_estimate=cost(0, 12 * count * BLK * depth),
    )(block, mine, own, other)


def schur_rows(own, other, columns, panel_blocks, child, block, mine, places):
    slots = child.shape[0]
    depth = own.shape[1]
    _, col_count, width, rows, _ = columns.shape
    wide = col_count * width * BLK
    per_child = col_count * width

    def body(child_ref, block_ref, mine_ref, place_ref, own_ref, other_ref, col_ref, *rest):
        b_refs = rest[: 2 * per_child]
        out_ref, hi_ref, lo_ref = rest[2 * per_child :]
        s = pl.program_id(0)

        @pl.when(s == 0)
        def _():
            for k in range(2 * per_child):
                at = pl.ds((k % per_child) * BLK, BLK)
                hi, lo = split(b_refs[k][0])
                hi_ref[k // per_child, at, :] = hi
                lo_ref[k // per_child, at, :] = lo

        c = child_ref[s]
        rows_f32 = jnp.where(mine_ref[s] == 1, own_ref[...], other_ref[...])
        a_hi, a_lo = split(rows_f32)
        both = dot_nt(jnp.concatenate([a_hi, a_lo], axis=0), hi_ref[c])
        total = both[:BLK] + both[BLK:] + dot_nt(a_hi, lo_ref[c])
        for q in range(col_count):
            for u in range(width):
                k = q * width + u
                out_ref[0, q, u] = col_ref[0, q, u] - total[:, k * BLK : (k + 1) * BLK]

    row_spec = pl.BlockSpec((BLK, depth), lambda s, c, b, m, p: (b[s], 0))
    b_specs = [
        pl.BlockSpec((1, BLK, depth), functools.partial(lambda k, s, c, b, m, p: (p[k], 0, 0), k))
        for k in range(2 * per_child)
    ]
    return pl.pallas_call(
        body,
        grid_spec=pltpu.PrefetchScalarGridSpec(
            num_scalar_prefetch=4,
            grid=(slots,),
            in_specs=[
                row_spec,
                row_spec,
                pl.BlockSpec(
                    (1, col_count, width, BLK, BLK), lambda s, c, b, m, p: (c[s], 0, 0, b[s], 0)
                ),
            ]
            + b_specs,
            out_specs=pl.BlockSpec(
                (1, col_count, width, BLK, BLK), lambda s, c, b, m, p: (s, 0, 0, 0, 0)
            ),
            scratch_shapes=[
                pltpu.VMEM((2, wide, depth), BF16),
                pltpu.VMEM((2, wide, depth), BF16),
            ],
        ),
        out_shape=jax.ShapeDtypeStruct((slots, col_count, width, BLK, BLK), F32),
        compiler_params=params(),
        cost_estimate=cost(
            6 * slots * BLK * wide * depth, slots * BLK * (2 * depth + 2 * wide) * 4 + 8 * wide * depth
        ),
    )(child, block, mine, places, own, other, columns, *([panel_blocks] * (2 * per_child)))


def first_panel(root, part, row_slot, row_valid, col_place):
    row_blocks = root.shape[0] // BLK
    _, col_count, width, _, _ = part.shape

    def body(slot_ref, valid_ref, place_ref, root_ref, a0_ref, a1_ref, out_ref):
        r = pl.program_id(0)
        out_ref[...] = root_ref[...]
        for c, a_ref in enumerate((a0_ref, a1_ref)):
            for q in range(col_count):
                for u in range(width):
                    col = place_ref[c, q * width + u]
                    ok = (valid_ref[c * row_blocks + r] == 1) & (col >= 0) & (col < RP // BLK)

                    @pl.when(ok)
                    def _():
                        at = pl.ds(pl.multiple_of(col * BLK, BLK), BLK)
                        out_ref[:, at] += a_ref[0, q, u]

    def arrived(c):
        return pl.BlockSpec(
            (1, col_count, width, BLK, BLK), lambda r, s, v, p: (s[c * row_blocks + r], 0, 0, 0, 0)
        )

    return pl.pallas_call(
        body,
        grid_spec=pltpu.PrefetchScalarGridSpec(
            num_scalar_prefetch=3,
            grid=(row_blocks,),
            in_specs=[pl.BlockSpec((BLK, RP), lambda r, s, v, p: (r, 0)), arrived(0), arrived(1)],
            out_specs=pl.BlockSpec((BLK, RP), lambda r, s, v, p: (r, 0)),
        ),
        out_shape=jax.ShapeDtypeStruct((root.shape[0], RP), F32),
        compiler_params=params(),
        cost_estimate=cost(0, 8 * root.shape[0] * RP + 4 * part.size),
    )(row_slot, row_valid, col_place, root, part, part)


def finish(root, parts, own_rows, columns, row_slot, row_valid, col_place, flags):
    rows, cols = root.shape
    row_blocks = rows // BLK
    count = len(parts)
    _, col_count, width, _, _ = parts[0].shape
    step = next(w for w in (512, 384, 256) if cols % w == 0)

    def body(slot_ref, valid_ref, place_ref, flag_ref, root_ref, *rest):
        a_refs = rest[: 2 * count]
        own_ref, col_ref, out_ref, hi_ref, lo_ref = rest[2 * count :]
        r = pl.program_id(0)

        @pl.when(r == 0)
        def _():
            hi, lo = split(col_ref[...])
            hi_ref[...] = hi
            lo_ref[...] = lo

        pivot_rows = (flag_ref[0] == 1) & (r < RP // BLK)

        @pl.when(pivot_rows)
        def _():
            out_ref[...] = root_ref[...]

        @pl.when(jnp.logical_not(pivot_rows))
        def _():
            a_hi, a_lo = split(own_ref[...])
            stacked = jnp.concatenate([a_hi, a_lo], axis=0)
            for n in range(0, cols, step):
                both = dot_nt(stacked, hi_ref[n : n + step, :])
                total = both[:BLK] + both[BLK:] + dot_nt(a_hi, lo_ref[n : n + step, :])
                out_ref[:, n : n + step] = root_ref[:, n : n + step] - total

        for c in range(2):
            for j in range(count):
                for q in range(col_count):
                    for u in range(width):
                        col = place_ref[c, (j * col_count + q) * width + u]

                        @pl.when((valid_ref[c * row_blocks + r] == 1) & (col >= 0))
                        def _():
                            at = pl.ds(pl.multiple_of(col * BLK, BLK), BLK)
                            out_ref[:, at] += a_refs[c * count + j][0, q, u]

        @pl.when(flag_ref[1] == 1)
        def _():
            out_ref[:, :RP] = own_ref[...]

    def arrived(c):
        return pl.BlockSpec(
            (1, col_count, width, BLK, BLK),
            lambda r, s, v, p, f: (s[c * row_blocks + r], 0, 0, 0, 0),
        )

    return pl.pallas_call(
        body,
        grid_spec=pltpu.PrefetchScalarGridSpec(
            num_scalar_prefetch=4,
            grid=(row_blocks,),
            in_specs=[pl.BlockSpec((BLK, cols), lambda r, s, v, p, f: (r, 0))]
            + [arrived(0)] * count
            + [arrived(1)] * count
            + [
                pl.BlockSpec((BLK, RP), lambda r, s, v, p, f: (r, 0)),
                pl.BlockSpec((cols, RP), lambda r, s, v, p, f: (0, 0)),
            ],
            out_specs=pl.BlockSpec((BLK, cols), lambda r, s, v, p, f: (r, 0)),
            scratch_shapes=[pltpu.VMEM((cols, RP), BF16), pltpu.VMEM((cols, RP), BF16)],
        ),
        out_shape=jax.ShapeDtypeStruct((rows, cols), F32),
        compiler_params=params(),
        cost_estimate=cost(6 * rows * cols * RP, 8 * rows * cols + 4 * sum(p.size for p in parts)),
    )(row_slot, row_valid, col_place, flags, root, *parts, *parts, own_rows, columns)


def shards(child_update, child_panel, root_front, index_map):
    col_count = lax.axis_size("pcol")
    row_count = lax.axis_size("prow")
    group_count = 2 * col_count
    half = lax.axis_index("half")
    pcol = lax.axis_index("pcol")
    prow = lax.axis_index("prow")
    group = half * col_count + pcol
    rows_dev = child_update.shape[1]
    root_rows, root_cols = root_front.shape
    child_blocks = rows_dev // BLK
    col_blocks = child_update.shape[2] // BLK
    row_blocks = root_rows // BLK
    group_cols = root_cols // BLK
    ratio = root_cols // root_rows
    cap_col = max(1, col_blocks // group_count)
    cap_row = max(1, 2 * child_blocks // row_count)
    cap_pick = cap_row * ratio
    width = 2 if cap_col % 2 == 0 else 1
    chunks = cap_col // width
    iota = functools.partial(jnp.arange, dtype=jnp.int32)
    own_panel = child_panel[0]
    other_panel = lax.ppermute(own_panel, "half", [(0, 1), (1, 0)])

    by_col = index_map.reshape(2, col_count, col_blocks)
    col_group = by_col // group_cols
    before = (by_col[..., None, :] < by_col[..., :, None]) & (
        col_group[..., None, :] == col_group[..., :, None]
    )
    col_rank = jnp.sum(before.astype(jnp.int32), axis=-1)
    col_key = col_group * cap_col + col_rank
    own_key = lax.dynamic_index_in_dim(
        col_key.reshape(group_count, col_blocks), group, 0, keepdims=False
    )
    chosen = jnp.sum(
        jnp.where(own_key[None, :] == iota(group_count * cap_col)[:, None], iota(col_blocks), 0),
        axis=1,
    ).reshape(group_count, cap_col)

    by_row = index_map.reshape(2, row_count, child_blocks)
    joint = by_row.transpose(1, 0, 2).reshape(row_count, 2 * child_blocks)
    items = 2 * child_blocks
    earlier = iota(items)[None, :] < iota(items)[:, None]
    owner = joint // row_blocks
    row_rank = jnp.sum(
        ((owner[:, None, :] == owner[:, :, None]) & earlier).astype(jnp.int32), axis=-1
    )
    joint_group = joint // group_cols
    pick_rank = jnp.sum(
        ((joint_group[:, None, :] == joint_group[:, :, None]) & earlier).astype(jnp.int32), axis=-1
    )
    here = lax.dynamic_index_in_dim
    own_owner = here(owner, prow, 0, keepdims=False)
    own_row_rank = here(row_rank, prow, 0, keepdims=False)
    own_pick_group = here(joint_group, prow, 0, keepdims=False)
    own_pick_rank = here(pick_rank, prow, 0, keepdims=False)
    pick_item = jnp.sum(
        jnp.where(
            (own_pick_group[None, :] == group) & (own_pick_rank[None, :] == iota(cap_pick)[:, None]),
            iota(items),
            0,
        ),
        axis=1,
    )
    send_item = jnp.sum(
        jnp.where(
            (own_owner * cap_row + own_row_rank)[None, :] == iota(row_count * cap_row)[:, None],
            iota(items),
            0,
        ),
        axis=1,
    )

    def to_child(item):
        child = item // child_blocks
        return child, item % child_blocks, (child == half).astype(jnp.int32)

    slot_of = (iota(row_count)[:, None] * cap_pick + pick_rank).reshape(
        row_count, 2, child_blocks
    )
    slot_of = slot_of.transpose(1, 0, 2).reshape(2, col_count, col_blocks)
    match = col_key[:, :, None, :] == (group * cap_col + iota(cap_col))[:, None]
    place = jnp.sum(jnp.where(match, slot_of[:, :, None, :], 0), axis=-1)
    col_local = (
        jnp.sum(jnp.where(match, by_col[:, :, None, :] - group * group_cols + 1, 0), axis=-1) - 1
    )

    def chunked(table):
        table = table.reshape(2, col_count, chunks, width).transpose(2, 0, 1, 3)
        return table.reshape(chunks, 2, col_count * width)

    place = chunked(place)
    col_local = chunked(col_local)
    row_slot = (iota(row_count)[:, None] * cap_row + row_rank).reshape(row_count, 2, child_blocks)
    row_match = by_row[..., None] == prow * row_blocks + iota(row_blocks)
    row_slot = jnp.sum(
        jnp.where(row_match, row_slot.transpose(1, 0, 2)[..., None] + 1, 0), axis=(1, 2)
    )
    row_valid = (row_slot > 0).astype(jnp.int32).reshape(-1)
    row_slot = jnp.maximum(row_slot - 1, 0).reshape(-1)

    _, pick_block, pick_mine = to_child(pick_item)
    picked = pick_rows(own_panel, other_panel, pick_block, pick_mine)
    panel_blocks = lax.all_gather(picked, "prow", axis=0, tiled=True)

    columns = []
    for j in range(chunks):
        packed = pack_columns(child_update[0], chosen[:, j * width : (j + 1) * width])
        got = lax.all_to_all(packed, ("half", "pcol"), split_axis=0, concat_axis=0, tiled=True)
        columns.append(got.reshape(2, col_count, width, rows_dev, BLK))

    send_child, send_block, send_mine = to_child(send_item)
    parts = []
    for j in range(chunks):
        outgoing = schur_rows(
            own_panel,
            other_panel,
            columns[j],
            panel_blocks,
            send_child,
            send_block,
            send_mine,
            place[j].reshape(-1),
        )
        parts.append(lax.all_to_all(outgoing, "prow", split_axis=0, concat_axis=0, tiled=True))

    raw = first_panel(root_front, parts[0], row_slot, row_valid, col_local[0])

    def to_groups(value):
        span = 1
        while span < col_count:
            got = lax.ppermute(value, "pcol", [(i, i + span) for i in range(min(span, col_count - span))])
            value = jnp.where((pcol >= span) & (pcol < 2 * span), got, value)
            span *= 2
        got = lax.ppermute(value, "half", [(0, 1)])
        return jnp.where(half == 1, got, value)

    pivot = to_groups(raw[:RP])
    span = 1
    while span < row_count:
        got = lax.ppermute(pivot, "prow", [(i, i + span) for i in range(min(span, row_count - span))])
        pivot = jnp.where((prow >= span) & (prow < 2 * span), got, pivot)
        span *= 2
    factor = jnp.linalg.cholesky(pivot)
    inverse = lax.linalg.triangular_solve(
        factor, jnp.eye(RP, dtype=F32), left_side=True, lower=True
    )
    raw_rows = to_groups(raw)
    bands = row_count // ratio
    device = lambda g, r: ((g // col_count) * row_count + r) * col_count + g % col_count
    shift = (prow // ratio - group) % bands
    tile = jnp.where(shift == 0, raw_rows, 0.0)
    for k in range(1, bands):
        pairs = [
            (device(g, g * ratio + o), device(g, ((g + k) % bands) * ratio + o))
            for g in range(group_count)
            for o in range(ratio)
        ]
        got = lax.ppermute(raw_rows, ("half", "prow", "pcol"), pairs)
        tile = jnp.where(shift == k, got, tile)
    tiles = [tile]
    for o in range(1, ratio):
        pairs = [
            (r, (r // ratio) * ratio + (r % ratio + o) % ratio) for r in range(row_count)
        ]
        tiles.append(lax.ppermute(tile, "prow", pairs))
    offset = prow % ratio
    ordered = []
    for o in range(ratio):
        value = tiles[0]
        for k in range(1, ratio):
            value = jnp.where((offset - k) % ratio == o, tiles[k], value)
        ordered.append(value)
    raw_cols = jnp.concatenate(ordered, axis=0)
    solved = lax.dot_general(raw_rows, inverse, NT, precision=HIGHEST, preferred_element_type=F32)
    lower_cols = lax.dot_general(
        raw_cols, inverse, NT, precision=HIGHEST, preferred_element_type=F32
    )
    top = jnp.where(prow == 0, factor, solved[:RP])
    own_rows = jnp.concatenate([top, solved[RP:]], axis=0)
    flags = jnp.stack([(prow == 0), (group == 0)]).astype(jnp.int32)
    col_all = col_local.transpose(1, 0, 2).reshape(2, -1)
    return finish(root_front, parts, own_rows, lower_cols, row_slot, row_valid, col_all, flags)


def solution(mesh):
    return jax.shard_map(
        shards,
        mesh=mesh,
        in_specs=(
            P("half", "prow", "pcol"),
            P("half", "prow", None),
            P("prow", ("half", "pcol")),
            P(),
        ),
        out_specs=P("prow", ("half", "pcol")),
        check_vma=False,
    )
```

```python
import functools

import jax
import jax.numpy as jnp
from jax import lax
from jax.experimental import pallas as pl
from jax.experimental.pallas import tpu as pltpu
from jax.sharding import PartitionSpec as P

BLK = 128
RP = 256
F32 = jnp.float32
BF16 = jnp.bfloat16
HIGHEST = lax.Precision.HIGHEST
NT = (((1,), (1,)), ((), ()))
VMEM_LIMIT = 56 * 1024 * 1024


def split(x):
    hi = x.astype(BF16)
    lo = (x - hi.astype(F32)).astype(BF16)
    return hi, lo


def dot_nt(a, b):
    return lax.dot_general(a, b, NT, preferred_element_type=F32)


def params():
    return pltpu.CompilerParams(vmem_limit_bytes=VMEM_LIMIT)


def cost(flops, nbytes):
    return pl.CostEstimate(flops=int(flops), bytes_accessed=int(nbytes), transcendentals=0)


def pack_columns(update, chosen):
    rows = update.shape[0]
    groups, width = chosen.shape

    def body(chosen_ref, *refs):
        for d in range(groups):
            refs[groups + d][0] = refs[d][...]

    def source(d):
        return pl.BlockSpec((rows, BLK), lambda u, s: (0, s[d * width + u]))

    return pl.pallas_call(
        body,
        grid_spec=pltpu.PrefetchScalarGridSpec(
            num_scalar_prefetch=1,
            grid=(width,),
            in_specs=[source(d) for d in range(groups)],
            out_specs=[pl.BlockSpec((1, rows, BLK), lambda u, s: (u, 0, 0))] * groups,
        ),
        out_shape=[jax.ShapeDtypeStruct((width, rows, BLK), F32)] * groups,
        compiler_params=params(),
        cost_estimate=cost(0, 8 * groups * width * rows * BLK),
    )(chosen.reshape(-1), *([update] * groups))


def pick_rows(own, other, block, mine):
    count = block.shape[0]
    depth = own.shape[1]

    def body(block_ref, mine_ref, own_ref, other_ref, out_ref):
        s = pl.program_id(0)

        @pl.when(mine_ref[s] == 1)
        def _():
            out_ref[0] = own_ref[...]

        @pl.when(mine_ref[s] == 0)
        def _():
            out_ref[0] = other_ref[...]

    spec = pl.BlockSpec((BLK, depth), lambda s, b, m: (b[s], 0))
    return pl.pallas_call(
        body,
        grid_spec=pltpu.PrefetchScalarGridSpec(
            num_scalar_prefetch=2,
            grid=(count,),
            in_specs=[spec, spec],
            out_specs=pl.BlockSpec((1, BLK, depth), lambda s, b, m: (s, 0, 0)),
        ),
        out_shape=jax.ShapeDtypeStruct((count, BLK, depth), F32),
        compiler_params=params(),
        cost_estimate=cost(0, 12 * count * BLK * depth),
    )(block, mine, own, other)


def schur_rows(own, other, arrived, panels, half, item_slot, sources, places, origins, slots, col_count):
    groups = len(arrived)
    depth = own.shape[1]
    width, rows, _ = arrived[0].shape
    child_blocks = rows // BLK
    tall = 2 if child_blocks % 2 == 0 else 1
    steps = child_blocks // tall
    per_child = col_count * width
    wide = per_child * BLK
    count = len(panels)
    piece = next(w for w in (512, 384, 256, 128) if wide % w == 0)

    def body(half_ref, slot_ref, source_ref, place_ref, origin_ref, own_ref, other_ref, *rest):
        in_refs = rest[:groups]
        panel_refs = rest[groups : groups + count]
        out_ref, staged, hi_ref, lo_ref, total_ref, result, load_sem, store_sem = rest[groups + count :]
        c = pl.program_id(0)
        step = c * steps + pl.program_id(1)

        @pl.when(step == 0)
        def _():
            @pl.loop(0, 2 * per_child)
            def _(k):
                for a in range(count):

                    @pl.when(source_ref[k] == a)
                    def _():
                        pltpu.make_async_copy(
                            panel_refs[a].at[place_ref[k]], staged.at[k], load_sem.at[k]
                        ).start()

            @pl.loop(0, 2 * per_child)
            def _(k):
                pltpu.make_async_copy(panel_refs[0].at[0], staged.at[k], load_sem.at[k]).wait()
                hi, lo = split(staged[k])
                hi_ref[k] = hi
                lo_ref[k] = lo

        a_hi, a_lo = split(jnp.where(c == half_ref[0], own_ref[...], other_ref[...]))
        stacked = jnp.concatenate([a_hi, a_lo], axis=0)
        high = tall * BLK
        at_once = piece // BLK
        for n in range(0, per_child, at_once):
            at = pl.ds(c * per_child + n, at_once)
            both = dot_nt(stacked, hi_ref[at].reshape(piece, depth))
            total = both[:high] + both[high:] + dot_nt(a_hi, lo_ref[at].reshape(piece, depth))
            for k in range(at_once):
                total_ref[n + k] = total[:, k * BLK : (k + 1) * BLK]

        buffer = step % 2

        def store(m, at_step):
            item = at_step * tall + m
            return pltpu.make_async_copy(
                result.at[at_step % 2, m], out_ref.at[slot_ref[item]], store_sem.at[at_step % 2, m]
            )

        @pl.when(step >= 2)
        def _():
            for m in range(tall):
                store(m, step - 2).wait()

        for d in range(groups):

            @pl.when(origin_ref[d] // col_count == c)
            def _():
                q = origin_ref[d] % col_count
                for u in range(width):
                    for m in range(tall):
                        at = slice(m * BLK, (m + 1) * BLK)
                        result[buffer, m, q, u] = in_refs[d][u, at, :] - total_ref[q * width + u, at, :]

        for m in range(tall):
            store(m, step).start()

        @pl.when(step == 2 * steps - 1)
        def _():
            for m in range(tall):
                if steps > 0:
                    store(m, step - 1).wait()
                store(m, step).wait()

    def stay(c, i, mine):
        return jnp.where(c == mine, i, jnp.where(c < mine, 0, steps - 1))

    def arrival(d):
        return pl.BlockSpec(
            (width, tall * BLK, BLK),
            lambda c, i, h, t, s, p, o: (0, stay(c, i, o[d] // col_count), 0),
        )

    return pl.pallas_call(
        body,
        grid_spec=pltpu.PrefetchScalarGridSpec(
            num_scalar_prefetch=5,
            grid=(2, steps),
            in_specs=[
                pl.BlockSpec((tall * BLK, depth), lambda c, i, h, t, s, p, o: (stay(c, i, h[0]), 0)),
                pl.BlockSpec((tall * BLK, depth), lambda c, i, h, t, s, p, o: (stay(c, i, 1 - h[0]), 0)),
            ]
            + [arrival(d) for d in range(groups)]
            + [pl.BlockSpec(memory_space=pl.ANY)] * count,
            out_specs=pl.BlockSpec(memory_space=pl.ANY),
            scratch_shapes=[
                pltpu.VMEM((2 * per_child, BLK, depth), F32),
                pltpu.VMEM((2 * per_child, BLK, depth), BF16),
                pltpu.VMEM((2 * per_child, BLK, depth), BF16),
                pltpu.VMEM((per_child, tall * BLK, BLK), F32),
                pltpu.VMEM((2, tall, col_count, width, BLK, BLK), F32),
                pltpu.SemaphoreType.DMA((2 * per_child,)),
                pltpu.SemaphoreType.DMA((2, tall)),
            ],
        ),
        out_shape=jax.ShapeDtypeStruct((slots, col_count, width, BLK, BLK), F32),
        compiler_params=params(),
        cost_estimate=cost(
            12 * rows * wide * depth, 8 * rows * (depth + 2 * wide) + 8 * wide * depth
        ),
    )(half.reshape(1), item_slot, sources, places, origins, own, other, *arrived, *panels)


def first_panel(root, part, row_slot, row_valid, col_place):
    row_blocks = root.shape[0] // BLK
    _, col_count, width, _, _ = part.shape

    def body(slot_ref, valid_ref, place_ref, root_ref, a0_ref, a1_ref, out_ref):
        r = pl.program_id(0)
        out_ref[...] = root_ref[...]
        for c, a_ref in enumerate((a0_ref, a1_ref)):
            for q in range(col_count):
                for u in range(width):
                    col = place_ref[c, q * width + u]
                    ok = (valid_ref[c * row_blocks + r] == 1) & (col >= 0) & (col < RP // BLK)

                    @pl.when(ok)
                    def _():
                        at = pl.ds(pl.multiple_of(col * BLK, BLK), BLK)
                        out_ref[:, at] += a_ref[0, q, u]

    def arrived(c):
        return pl.BlockSpec(
            (1, col_count, width, BLK, BLK), lambda r, s, v, p: (s[c * row_blocks + r], 0, 0, 0, 0)
        )

    return pl.pallas_call(
        body,
        grid_spec=pltpu.PrefetchScalarGridSpec(
            num_scalar_prefetch=3,
            grid=(row_blocks,),
            in_specs=[pl.BlockSpec((BLK, RP), lambda r, s, v, p: (r, 0)), arrived(0), arrived(1)],
            out_specs=pl.BlockSpec((BLK, RP), lambda r, s, v, p: (r, 0)),
        ),
        out_shape=jax.ShapeDtypeStruct((root.shape[0], RP), F32),
        compiler_params=params(),
        cost_estimate=cost(0, 8 * root.shape[0] * RP + 4 * part.size),
    )(row_slot, row_valid, col_place, root, part, part)


def advance(root, parts, own_rows, columns, row_slot, row_valid, col_place, flags):
    rows, cols = root.shape
    row_blocks = rows // BLK
    count = len(parts)
    _, col_count, width, _, _ = parts[0].shape
    step = next(w for w in (512, 384, 256) if cols % w == 0)

    def body(slot_ref, valid_ref, place_ref, flag_ref, root_ref, *rest):
        a_refs = rest[: 2 * count]
        own_ref, col_ref, out_ref, hi_ref, lo_ref = rest[2 * count :]
        r = pl.program_id(0)

        @pl.when(r == 0)
        def _():
            hi, lo = split(col_ref[...])
            hi_ref[...] = hi
            lo_ref[...] = lo

        pivot_rows = (flag_ref[0] == 1) & (r < RP // BLK)

        @pl.when(pivot_rows)
        def _():
            out_ref[...] = root_ref[...]

        @pl.when(jnp.logical_not(pivot_rows))
        def _():
            a_hi, a_lo = split(own_ref[...])
            stacked = jnp.concatenate([a_hi, a_lo], axis=0)
            for n in range(0, cols, step):
                both = dot_nt(stacked, hi_ref[n : n + step, :])
                total = both[:BLK] + both[BLK:] + dot_nt(a_hi, lo_ref[n : n + step, :])
                out_ref[:, n : n + step] = root_ref[:, n : n + step] - total

        for c in range(2):
            for j in range(count):
                for q in range(col_count):
                    for u in range(width):
                        col = place_ref[c, (j * col_count + q) * width + u]

                        @pl.when((valid_ref[c * row_blocks + r] == 1) & (col >= 0))
                        def _():
                            at = pl.ds(pl.multiple_of(col * BLK, BLK), BLK)
                            out_ref[:, at] += a_refs[c * count + j][0, q, u]

        @pl.when(flag_ref[1] == 1)
        def _():
            out_ref[:, :RP] = own_ref[...]

    def arrived(c):
        return pl.BlockSpec(
            (1, col_count, width, BLK, BLK),
            lambda r, s, v, p, f: (s[c * row_blocks + r], 0, 0, 0, 0),
        )

    return pl.pallas_call(
        body,
        grid_spec=pltpu.PrefetchScalarGridSpec(
            num_scalar_prefetch=4,
            grid=(row_blocks,),
            in_specs=[pl.BlockSpec((BLK, cols), lambda r, s, v, p, f: (r, 0))]
            + [arrived(0)] * count
            + [arrived(1)] * count
            + [
                pl.BlockSpec((BLK, RP), lambda r, s, v, p, f: (r, 0)),
                pl.BlockSpec((cols, RP), lambda r, s, v, p, f: (0, 0)),
            ],
            out_specs=pl.BlockSpec((BLK, cols), lambda r, s, v, p, f: (r, 0)),
            scratch_shapes=[pltpu.VMEM((cols, RP), BF16), pltpu.VMEM((cols, RP), BF16)],
        ),
        out_shape=jax.ShapeDtypeStruct((rows, cols), F32),
        compiler_params=params(),
        cost_estimate=cost(6 * rows * cols * RP, 8 * rows * cols + 4 * sum(p.size for p in parts)),
    )(row_slot, row_valid, col_place, flags, root, *parts, *parts, own_rows, columns)


def deliver(root, part, row_slot, row_valid, col_place):
    rows, cols = root.shape
    row_blocks = rows // BLK
    _, col_count, width, _, _ = part.shape

    def body(slot_ref, valid_ref, place_ref, root_ref, a0_ref, a1_ref, out_ref):
        r = pl.program_id(0)
        out_ref[...] = root_ref[...]
        for c, a_ref in enumerate((a0_ref, a1_ref)):

            @pl.when(valid_ref[c * row_blocks + r] == 1)
            def _():
                for q in range(col_count):
                    for u in range(width):
                        col = place_ref[c, q * width + u]

                        @pl.when(col >= 0)
                        def _():
                            at = pl.ds(pl.multiple_of(col * BLK, BLK), BLK)
                            out_ref[:, at] += a_ref[0, q, u]

    def arrived(c):
        return pl.BlockSpec(
            (1, col_count, width, BLK, BLK), lambda r, s, v, p: (s[c * row_blocks + r], 0, 0, 0, 0)
        )

    whole = pl.BlockSpec((BLK, cols), lambda r, s, v, p: (r, 0))
    return pl.pallas_call(
        body,
        grid_spec=pltpu.PrefetchScalarGridSpec(
            num_scalar_prefetch=3,
            grid=(row_blocks,),
            in_specs=[whole, arrived(0), arrived(1)],
            out_specs=whole,
        ),
        out_shape=jax.ShapeDtypeStruct((rows, cols), F32),
        compiler_params=params(),
        cost_estimate=cost(0, 8 * rows * cols + 4 * part.size),
    )(row_slot, row_valid, col_place, root, part, part)


def shards(child_update, child_panel, root_front, index_map):
    col_count = lax.axis_size("pcol")
    row_count = lax.axis_size("prow")
    group_count = 2 * col_count
    half = lax.axis_index("half")
    pcol = lax.axis_index("pcol")
    prow = lax.axis_index("prow")
    group = half * col_count + pcol
    rows_dev = child_update.shape[1]
    root_rows, root_cols = root_front.shape
    child_blocks = rows_dev // BLK
    col_blocks = child_update.shape[2] // BLK
    row_blocks = root_rows // BLK
    group_cols = root_cols // BLK
    ratio = root_cols // root_rows
    cap_col = max(1, col_blocks // group_count)
    cap_row = max(1, 2 * child_blocks // row_count)
    cap_pick = cap_row * ratio
    widths = [cap_col] if cap_col <= 2 else [2, cap_col - 2]
    spans = [(sum(widths[:j]), w) for j, w in enumerate(widths)]
    band = 2 if row_count % 2 == 0 else 1
    iota = functools.partial(jnp.arange, dtype=jnp.int32)
    own_panel = child_panel[0]
    other_panel = lax.ppermute(own_panel, "half", [(0, 1), (1, 0)])

    by_col = index_map.reshape(2, col_count, col_blocks)
    col_group = by_col // group_cols
    before = (by_col[..., None, :] < by_col[..., :, None]) & (
        col_group[..., None, :] == col_group[..., :, None]
    )
    col_rank = jnp.sum(before.astype(jnp.int32), axis=-1)
    col_key = col_group * cap_col + col_rank
    own_key = lax.dynamic_index_in_dim(
        col_key.reshape(group_count, col_blocks), group, 0, keepdims=False
    )
    chosen = jnp.sum(
        jnp.where(own_key[None, :] == iota(group_count * cap_col)[:, None], iota(col_blocks), 0),
        axis=1,
    ).reshape(group_count, cap_col)

    by_row = index_map.reshape(2, row_count, child_blocks)
    joint = by_row.transpose(1, 0, 2).reshape(row_count, 2 * child_blocks)
    items = 2 * child_blocks
    earlier = iota(items)[None, :] < iota(items)[:, None]
    owner = joint // row_blocks
    row_rank = jnp.sum(
        ((owner[:, None, :] == owner[:, :, None]) & earlier).astype(jnp.int32), axis=-1
    )
    joint_group = joint // group_cols
    pick_rank = jnp.sum(
        ((joint_group[:, None, :] == joint_group[:, :, None]) & earlier).astype(jnp.int32), axis=-1
    )
    here = lax.dynamic_index_in_dim
    own_owner = here(owner, prow, 0, keepdims=False)
    own_row_rank = here(row_rank, prow, 0, keepdims=False)
    own_pick_group = here(joint_group, prow, 0, keepdims=False)
    own_pick_rank = here(pick_rank, prow, 0, keepdims=False)
    pick_item = jnp.sum(
        jnp.where(
            (own_pick_group[None, :] == group) & (own_pick_rank[None, :] == iota(cap_pick)[:, None]),
            iota(items),
            0,
        ),
        axis=1,
    )
    item_slot = own_owner * cap_row + own_row_rank

    spread_z, spread_x = iota(row_count) // band - prow // band, (iota(row_count) - prow) % band
    source = jnp.where(
        spread_z == 0,
        spread_x,
        band * (2 * jnp.abs(spread_z) - 1 + (spread_z > 0)) + spread_x,
    )
    code = (source[:, None] * cap_pick + pick_rank).reshape(row_count, 2, child_blocks)
    slot_of = code.transpose(1, 0, 2).reshape(2, col_count, col_blocks)
    match = col_key[:, :, None, :] == (group * cap_col + iota(cap_col))[:, None]
    place = jnp.sum(jnp.where(match, slot_of[:, :, None, :], 0), axis=-1)
    col_local = (
        jnp.sum(jnp.where(match, by_col[:, :, None, :] - group * group_cols + 1, 0), axis=-1) - 1
    )

    row_slot = (iota(row_count)[:, None] * cap_row + row_rank).reshape(row_count, 2, child_blocks)
    row_match = by_row[..., None] == prow * row_blocks + iota(row_blocks)
    row_slot = jnp.sum(
        jnp.where(row_match, row_slot.transpose(1, 0, 2)[..., None] + 1, 0), axis=(1, 2)
    )
    row_valid = (row_slot > 0).astype(jnp.int32).reshape(-1)
    row_slot = jnp.maximum(row_slot - 1, 0).reshape(-1)

    pick_mine = (pick_item // child_blocks == half).astype(jnp.int32)
    picked = pick_rows(own_panel, other_panel, pick_item % child_blocks, pick_mine)

    def across(value, rows_in):
        return [
            lax.ppermute(value, "prow", [(r, r - r % band + (r % band - o) % band) for r in rows_in])
            for o in range(1, band)
        ]

    rows_all = list(range(row_count))
    bands = row_count // band
    panels = [picked] + across(picked, rows_all)
    up = down = picked
    for k in range(1, bands):
        up = lax.ppermute(
            up, "prow", [(r, r + band) for r in rows_all if k - 1 <= r // band < bands - 1]
        )
        down = lax.ppermute(
            down, "prow", [(r, r - band) for r in rows_all if 0 < r // band <= bands - k]
        )
        panels += [up] + across(up, [r for r in rows_all if r // band >= k])
        panels += [down] + across(down, [r for r in rows_all if r // band < bands - k])

    device = lambda g, r: ((g // col_count) * row_count + r) * col_count + g % col_count
    everyone = ("half", "prow", "pcol")
    distance = (group + iota(group_count)) % group_count
    origins = (group - iota(group_count)) % group_count
    arrived = []
    for start, width in spans:
        packed = pack_columns(child_update[0], chosen[distance, start : start + width])
        got = [packed[0]]
        for d in range(1, group_count):
            pairs = [
                (device(g, r), device((g + d) % group_count, r))
                for g in range(group_count)
                for r in range(row_count)
            ]
            got.append(lax.ppermute(packed[d], everyone, pairs))
        arrived.append(got)

    parts, col_places = [], []
    for (start, width), got in zip(spans, arrived):
        codes = place[:, :, start : start + width].reshape(-1)
        col_places.append(col_local[:, :, start : start + width].reshape(2, -1))
        outgoing = schur_rows(
            own_panel,
            other_panel,
            got,
            panels,
            half,
            item_slot,
            codes // cap_pick,
            codes % cap_pick,
            origins,
            row_count * cap_row,
            col_count,
        )
        parts.append(lax.all_to_all(outgoing, "prow", split_axis=0, concat_axis=0, tiled=True))

    raw = first_panel(root_front, parts[0], row_slot, row_valid, col_places[0])

    def to_groups(value):
        total = jnp.where(group == 0, value, 0.0)
        for g in range(1, group_count):
            pairs = [(device(0, r), device(g, r)) for r in range(row_count)]
            total = total + lax.ppermute(value, everyone, pairs)
        return total

    corner = raw[:RP]
    first = jnp.where(group == 0, corner, 0.0)
    for g in range(1, group_count):
        first = first + lax.ppermute(corner, everyone, [(device(0, 0), device(g, 0))])
    pivot = jnp.where(prow == 0, first, 0.0)
    for r in range(1, row_count):
        pivot = pivot + lax.ppermute(first, "prow", [(0, r)])
    factor = jnp.linalg.cholesky(pivot)
    inverse = lax.linalg.triangular_solve(
        factor, jnp.eye(RP, dtype=F32), left_side=True, lower=True
    )
    raw_rows = to_groups(raw)
    groups_of = row_count // ratio
    shift = (prow // ratio - group) % groups_of
    tile = jnp.where(shift == 0, raw_rows, 0.0)
    for k in range(1, groups_of):
        pairs = [
            (device(g, g * ratio + o), device(g, ((g + k) % groups_of) * ratio + o))
            for g in range(group_count)
            for o in range(ratio)
        ]
        got = lax.ppermute(raw_rows, ("half", "prow", "pcol"), pairs)
        tile = jnp.where(shift == k, got, tile)
    tiles = [tile]
    for o in range(1, ratio):
        pairs = [
            (r, (r // ratio) * ratio + (r % ratio + o) % ratio) for r in range(row_count)
        ]
        tiles.append(lax.ppermute(tile, "prow", pairs))
    offset = prow % ratio
    ordered = []
    for o in range(ratio):
        value = tiles[0]
        for k in range(1, ratio):
            value = jnp.where((offset - k) % ratio == o, tiles[k], value)
        ordered.append(value)
    raw_cols = jnp.concatenate(ordered, axis=0)
    solved = lax.dot_general(raw_rows, inverse, NT, precision=HIGHEST, preferred_element_type=F32)
    lower_cols = lax.dot_general(
        raw_cols, inverse, NT, precision=HIGHEST, preferred_element_type=F32
    )
    top = jnp.where(prow == 0, factor, solved[:RP])
    own_rows = jnp.concatenate([top, solved[RP:]], axis=0)
    flags = jnp.stack([(prow == 0), (group == 0)]).astype(jnp.int32)
    root = advance(
        root_front, parts[:1], own_rows, lower_cols, row_slot, row_valid, col_places[0], flags
    )
    for part, col_place in zip(parts[1:], col_places[1:]):
        root = deliver(root, part, row_slot, row_valid, col_place)
    return root


def solution(mesh):
    return jax.shard_map(
        shards,
        mesh=mesh,
        in_specs=(
            P("half", "prow", "pcol"),
            P("half", "prow", None),
            P("prow", ("half", "pcol")),
            P(),
        ),
        out_specs=P("prow", ("half", "pcol")),
        check_vma=False,
    )
```

```python
import functools

import jax
import jax.numpy as jnp
from jax import lax
from jax.experimental import pallas as pl
from jax.experimental.pallas import tpu as pltpu
from jax.sharding import PartitionSpec as P

BLK = 128
RP = 256
F32 = jnp.float32
BF16 = jnp.bfloat16
HIGHEST = lax.Precision.HIGHEST
NT = (((1,), (1,)), ((), ()))
VMEM_LIMIT = 56 * 1024 * 1024


def split(x):
    hi = x.astype(BF16)
    lo = (x - hi.astype(F32)).astype(BF16)
    return hi, lo


def dot_nt(a, b):
    return lax.dot_general(a, b, NT, preferred_element_type=F32)


def params():
    return pltpu.CompilerParams(vmem_limit_bytes=VMEM_LIMIT)


def cost(flops, nbytes):
    return pl.CostEstimate(flops=int(flops), bytes_accessed=int(nbytes), transcendentals=0)


def pack_columns(update, chosen):
    rows = update.shape[0]
    groups, width = chosen.shape

    def body(chosen_ref, *refs):
        for d in range(groups):
            refs[groups + d][0] = refs[d][...]

    def source(d):
        return pl.BlockSpec((rows, BLK), lambda u, s: (0, s[d * width + u]))

    return pl.pallas_call(
        body,
        grid_spec=pltpu.PrefetchScalarGridSpec(
            num_scalar_prefetch=1,
            grid=(width,),
            in_specs=[source(d) for d in range(groups)],
            out_specs=[pl.BlockSpec((1, rows, BLK), lambda u, s: (u, 0, 0))] * groups,
        ),
        out_shape=[jax.ShapeDtypeStruct((width, rows, BLK), F32)] * groups,
        compiler_params=params(),
        cost_estimate=cost(0, 8 * groups * width * rows * BLK),
    )(chosen.reshape(-1), *([update] * groups))


def pick_rows(own, other, block, mine):
    count = block.shape[0]
    depth = own.shape[1]

    def body(block_ref, mine_ref, own_ref, other_ref, out_ref):
        s = pl.program_id(0)

        @pl.when(mine_ref[s] == 1)
        def _():
            out_ref[0] = own_ref[...]

        @pl.when(mine_ref[s] == 0)
        def _():
            out_ref[0] = other_ref[...]

    spec = pl.BlockSpec((BLK, depth), lambda s, b, m: (b[s], 0))
    return pl.pallas_call(
        body,
        grid_spec=pltpu.PrefetchScalarGridSpec(
            num_scalar_prefetch=2,
            grid=(count,),
            in_specs=[spec, spec],
            out_specs=pl.BlockSpec((1, BLK, depth), lambda s, b, m: (s, 0, 0)),
        ),
        out_shape=jax.ShapeDtypeStruct((count, BLK, depth), F32),
        compiler_params=params(),
        cost_estimate=cost(0, 12 * count * BLK * depth),
    )(block, mine, own, other)


def schur_rows(own, other, arrived, panels, half, item_slot, places, origins, slots, col_count, span):
    groups = len(arrived)
    depth = own.shape[1]
    first, width = span
    rows = arrived[0].shape[1]
    child_blocks = rows // BLK
    tall = 2 if child_blocks % 2 == 0 else 1
    steps = child_blocks // tall
    per_child = col_count * width
    wide = per_child * BLK
    piece = next(w for w in (512, 384, 256, 128) if wide % w == 0)

    def body(half_ref, slot_ref, place_ref, origin_ref, own_ref, other_ref, *rest):
        in_refs = rest[:groups]
        panel_ref, out_ref, staged, hi_ref, lo_ref, total_ref, result, load_sem, store_sem = rest[groups:]
        c = pl.program_id(0)
        step = c * steps + pl.program_id(1)

        @pl.when(step == 0)
        def _():
            @pl.loop(0, 2 * per_child)
            def _(k):
                pltpu.make_async_copy(panel_ref.at[place_ref[k]], staged.at[k], load_sem.at[k]).start()

            @pl.loop(0, 2 * per_child)
            def _(k):
                pltpu.make_async_copy(panel_ref.at[place_ref[k]], staged.at[k], load_sem.at[k]).wait()
                hi, lo = split(staged[k])
                hi_ref[k] = hi
                lo_ref[k] = lo

        a_hi, a_lo = split(jnp.where(c == half_ref[0], own_ref[...], other_ref[...]))
        stacked = jnp.concatenate([a_hi, a_lo], axis=0)
        high = tall * BLK
        at_once = piece // BLK
        for n in range(0, per_child, at_once):
            at = pl.ds(c * per_child + n, at_once)
            both = dot_nt(stacked, hi_ref[at].reshape(piece, depth))
            total = both[:high] + both[high:] + dot_nt(a_hi, lo_ref[at].reshape(piece, depth))
            for k in range(at_once):
                total_ref[n + k] = total[:, k * BLK : (k + 1) * BLK]

        buffer = step % 2

        def store(m, at_step):
            item = at_step * tall + m
            return pltpu.make_async_copy(
                result.at[at_step % 2, m], out_ref.at[slot_ref[item]], store_sem.at[at_step % 2, m]
            )

        @pl.when(step >= 2)
        def _():
            for m in range(tall):
                store(m, step - 2).wait()

        for d in range(groups):

            @pl.when(origin_ref[d] // col_count == c)
            def _():
                q = origin_ref[d] % col_count
                for u in range(width):
                    for m in range(tall):
                        at = slice(m * BLK, (m + 1) * BLK)
                        result[buffer, m, q, u] = in_refs[d][u, at, :] - total_ref[q * width + u, at, :]

        for m in range(tall):
            store(m, step).start()

        @pl.when(step == 2 * steps - 1)
        def _():
            for m in range(tall):
                if steps > 0:
                    store(m, step - 1).wait()
                store(m, step).wait()

    def stay(c, i, mine):
        return jnp.where(c == mine, i, jnp.where(c < mine, 0, steps - 1))

    def arrival(d):
        return pl.BlockSpec(
            (width, tall * BLK, BLK),
            lambda c, i, h, t, p, o: (first // width, stay(c, i, o[d] // col_count), 0),
        )

    return pl.pallas_call(
        body,
        grid_spec=pltpu.PrefetchScalarGridSpec(
            num_scalar_prefetch=4,
            grid=(2, steps),
            in_specs=[
                pl.BlockSpec((tall * BLK, depth), lambda c, i, h, t, p, o: (stay(c, i, h[0]), 0)),
                pl.BlockSpec((tall * BLK, depth), lambda c, i, h, t, p, o: (stay(c, i, 1 - h[0]), 0)),
            ]
            + [arrival(d) for d in range(groups)]
            + [pl.BlockSpec(memory_space=pl.ANY)],
            out_specs=pl.BlockSpec(memory_space=pl.ANY),
            scratch_shapes=[
                pltpu.VMEM((2 * per_child, BLK, depth), F32),
                pltpu.VMEM((2 * per_child, BLK, depth), BF16),
                pltpu.VMEM((2 * per_child, BLK, depth), BF16),
                pltpu.VMEM((per_child, tall * BLK, BLK), F32),
                pltpu.VMEM((2, tall, col_count, width, BLK, BLK), F32),
                pltpu.SemaphoreType.DMA((2 * per_child,)),
                pltpu.SemaphoreType.DMA((2, tall)),
            ],
        ),
        out_shape=jax.ShapeDtypeStruct((slots, col_count, width, BLK, BLK), F32),
        compiler_params=params(),
        cost_estimate=cost(
            12 * rows * wide * depth, 8 * rows * (depth + 2 * wide) + 8 * wide * depth
        ),
    )(half.reshape(1), item_slot, places, origins, own, other, *arrived, panels)


def first_panel(root, parts, row_slot, row_valid, col_places):
    row_blocks = root.shape[0] // BLK
    count = len(parts)
    _, col_count, width, _, _ = parts[0].shape

    def body(slot_ref, valid_ref, place_ref, root_ref, *rest):
        a_refs, out_ref = rest[:-1], rest[-1]
        r = pl.program_id(0)
        out_ref[...] = root_ref[...]
        for c in range(2):
            for k in range(count * col_count * width):
                j, q, u = k // (col_count * width), k // width % col_count, k % width
                col = place_ref[c, k]
                ok = (valid_ref[c * row_blocks + r] == 1) & (col >= 0) & (col < RP // BLK)

                @pl.when(ok)
                def _():
                    at = pl.ds(pl.multiple_of(col * BLK, BLK), BLK)
                    out_ref[:, at] += a_refs[c * count + j][0, q, u]

    def arrived(c):
        return pl.BlockSpec(
            (1, col_count, width, BLK, BLK), lambda r, s, v, p: (s[c * row_blocks + r], 0, 0, 0, 0)
        )

    panel = pl.BlockSpec((BLK, RP), lambda r, s, v, p: (r, 0))
    return pl.pallas_call(
        body,
        grid_spec=pltpu.PrefetchScalarGridSpec(
            num_scalar_prefetch=3,
            grid=(row_blocks,),
            in_specs=[panel] + [arrived(0)] * count + [arrived(1)] * count,
            out_specs=panel,
        ),
        out_shape=jax.ShapeDtypeStruct((root.shape[0], RP), F32),
        compiler_params=params(),
        cost_estimate=cost(0, 8 * root.shape[0] * RP + 4 * sum(p.size for p in parts)),
    )(row_slot, row_valid, jnp.concatenate(col_places, axis=1), root, *parts, *parts)


def advance(root, parts, own_rows, columns, row_slot, row_valid, col_places, flags):
    rows, cols = root.shape
    row_blocks = rows // BLK
    count = len(parts)
    _, col_count, width, _, _ = parts[0].shape
    step = next(w for w in (512, 384, 256) if cols % w == 0)

    def body(slot_ref, valid_ref, place_ref, flag_ref, root_ref, *rest):
        a_refs = rest[: 2 * count]
        own_ref, col_ref, out_ref, hi_ref, lo_ref = rest[2 * count :]
        r = pl.program_id(0)

        @pl.when(r == 0)
        def _():
            hi, lo = split(col_ref[...])
            hi_ref[...] = hi
            lo_ref[...] = lo

        pivot_rows = (flag_ref[0] == 1) & (r < RP // BLK)

        @pl.when(pivot_rows)
        def _():
            out_ref[...] = root_ref[...]

        @pl.when(jnp.logical_not(pivot_rows))
        def _():
            a_hi, a_lo = split(own_ref[...])
            stacked = jnp.concatenate([a_hi, a_lo], axis=0)
            for n in range(0, cols, step):
                both = dot_nt(stacked, hi_ref[n : n + step, :])
                total = both[:BLK] + both[BLK:] + dot_nt(a_hi, lo_ref[n : n + step, :])
                out_ref[:, n : n + step] = root_ref[:, n : n + step] - total

        for c in range(2):
            for j in range(count):
                for q in range(col_count):
                    for u in range(width):
                        col = place_ref[c, (j * col_count + q) * width + u]

                        @pl.when((valid_ref[c * row_blocks + r] == 1) & (col >= 0))
                        def _():
                            at = pl.ds(pl.multiple_of(col * BLK, BLK), BLK)
                            out_ref[:, at] += a_refs[c * count + j][0, q, u]

        @pl.when(flag_ref[1] == 1)
        def _():
            out_ref[:, :RP] = own_ref[...]

    def arrived(c):
        return pl.BlockSpec(
            (1, col_count, width, BLK, BLK),
            lambda r, s, v, p, f: (s[c * row_blocks + r], 0, 0, 0, 0),
        )

    return pl.pallas_call(
        body,
        grid_spec=pltpu.PrefetchScalarGridSpec(
            num_scalar_prefetch=4,
            grid=(row_blocks,),
            in_specs=[pl.BlockSpec((BLK, cols), lambda r, s, v, p, f: (r, 0))]
            + [arrived(0)] * count
            + [arrived(1)] * count
            + [
                pl.BlockSpec((BLK, RP), lambda r, s, v, p, f: (r, 0)),
                pl.BlockSpec((cols, RP), lambda r, s, v, p, f: (0, 0)),
            ],
            out_specs=pl.BlockSpec((BLK, cols), lambda r, s, v, p, f: (r, 0)),
            scratch_shapes=[pltpu.VMEM((cols, RP), BF16), pltpu.VMEM((cols, RP), BF16)],
        ),
        out_shape=jax.ShapeDtypeStruct((rows, cols), F32),
        compiler_params=params(),
        cost_estimate=cost(6 * rows * cols * RP, 8 * rows * cols + 4 * sum(p.size for p in parts)),
    )(
        row_slot,
        row_valid,
        jnp.concatenate(col_places, axis=1),
        flags,
        root,
        *parts,
        *parts,
        own_rows,
        columns,
    )


def deliver(root, part, row_slot, row_valid, col_place):
    rows, cols = root.shape
    row_blocks = rows // BLK
    _, col_count, width, _, _ = part.shape

    def body(slot_ref, valid_ref, place_ref, root_ref, a0_ref, a1_ref, out_ref):
        r = pl.program_id(0)
        out_ref[...] = root_ref[...]
        for c, a_ref in enumerate((a0_ref, a1_ref)):

            @pl.when(valid_ref[c * row_blocks + r] == 1)
            def _():
                for q in range(col_count):
                    for u in range(width):
                        col = place_ref[c, q * width + u]

                        @pl.when(col >= 0)
                        def _():
                            at = pl.ds(pl.multiple_of(col * BLK, BLK), BLK)
                            out_ref[:, at] += a_ref[0, q, u]

    def arrived(c):
        return pl.BlockSpec(
            (1, col_count, width, BLK, BLK), lambda r, s, v, p: (s[c * row_blocks + r], 0, 0, 0, 0)
        )

    whole = pl.BlockSpec((BLK, cols), lambda r, s, v, p: (r, 0))
    return pl.pallas_call(
        body,
        grid_spec=pltpu.PrefetchScalarGridSpec(
            num_scalar_prefetch=3,
            grid=(row_blocks,),
            in_specs=[whole, arrived(0), arrived(1)],
            out_specs=whole,
        ),
        out_shape=jax.ShapeDtypeStruct((rows, cols), F32),
        compiler_params=params(),
        cost_estimate=cost(0, 8 * rows * cols + 4 * part.size),
    )(row_slot, row_valid, col_place, root, part, part)


def shards(child_update, child_panel, root_front, index_map):
    col_count = lax.axis_size("pcol")
    row_count = lax.axis_size("prow")
    group_count = 2 * col_count
    half = lax.axis_index("half")
    pcol = lax.axis_index("pcol")
    prow = lax.axis_index("prow")
    group = half * col_count + pcol
    rows_dev = child_update.shape[1]
    root_rows, root_cols = root_front.shape
    child_blocks = rows_dev // BLK
    col_blocks = child_update.shape[2] // BLK
    row_blocks = root_rows // BLK
    group_cols = root_cols // BLK
    ratio = root_cols // root_rows
    cap_col = max(1, col_blocks // group_count)
    cap_row = max(1, 2 * child_blocks // row_count)
    cap_pick = cap_row * ratio
    even = col_blocks == group_count * cap_col and 2 * child_blocks == row_count * cap_row
    halves = 2 if even and cap_pick % 2 == 0 and cap_col % 2 == 0 else 1
    half_col, half_pick = cap_col // halves, cap_pick // halves
    width = half_col // 2 if half_col % 2 == 0 else half_col
    iota = functools.partial(jnp.arange, dtype=jnp.int32)
    own_panel = child_panel[0]
    other_panel = lax.ppermute(own_panel, "half", [(0, 1), (1, 0)])

    by_col = index_map.reshape(2, col_count, col_blocks)
    by_row = index_map.reshape(2, row_count, child_blocks)
    key = by_row // group_cols
    if halves == 2:
        in_group = key[..., None] == iota(group_count)
        named = jnp.sum(in_group.astype(jnp.int32), axis=2)
        leading = jnp.sum((in_group & (by_row[..., None] < RP // BLK)).astype(jnp.int32), axis=2)
        least = jnp.maximum(jnp.maximum(half_pick - named[1], leading[0]), 0)
        most = jnp.minimum(jnp.minimum(named[0], half_pick - leading[1]), half_pick)
        least = least.reshape(col_count, row_count // col_count, group_count)
        room = most.reshape(least.shape) - least
        rest = half_col - jnp.sum(least, axis=1, keepdims=True)
        taken = least + jnp.clip(rest - (jnp.cumsum(room, axis=1) - room), 0, room)
        taken = taken.reshape(row_count, group_count)
        taken = jnp.stack([taken, half_pick - taken])
        ahead = (by_row[..., None, :] < by_row[..., :, None]) & (key[..., None, :] == key[..., :, None])
        place_in = jnp.sum(ahead.astype(jnp.int32), axis=-1)
        limit = jnp.sum(jnp.where(in_group, taken[:, :, None, :], 0), axis=-1)
        key = 2 * key + (place_in >= limit).astype(jnp.int32)

    col_key = key.reshape(2, col_count, col_blocks)
    before = (col_key[..., None, :] == col_key[..., :, None]) & (
        iota(col_blocks)[None, :] < iota(col_blocks)[:, None]
    )
    col_key = col_key * half_col + jnp.sum(before.astype(jnp.int32), axis=-1)
    own_key = lax.dynamic_index_in_dim(
        col_key.reshape(group_count, col_blocks), group, 0, keepdims=False
    )
    chosen = jnp.sum(
        jnp.where(own_key[None, :] == iota(group_count * cap_col)[:, None], iota(col_blocks), 0),
        axis=1,
    ).reshape(group_count, halves, half_col)

    joint = by_row.transpose(1, 0, 2).reshape(row_count, 2 * child_blocks)
    items = 2 * child_blocks
    earlier = iota(items)[None, :] < iota(items)[:, None]
    owner = joint // row_blocks
    row_rank = jnp.sum(
        ((owner[:, None, :] == owner[:, :, None]) & earlier).astype(jnp.int32), axis=-1
    )
    joint_key = key.transpose(1, 0, 2).reshape(row_count, items)
    pick_rank = jnp.sum(
        ((joint_key[:, None, :] == joint_key[:, :, None]) & earlier).astype(jnp.int32), axis=-1
    )
    here = lax.dynamic_index_in_dim
    own_owner = here(owner, prow, 0, keepdims=False)
    own_row_rank = here(row_rank, prow, 0, keepdims=False)
    own_pick = here(joint_key * half_pick + pick_rank, prow, 0, keepdims=False)
    pick_item = jnp.sum(
        jnp.where(own_pick[None, :] == (group * cap_pick + iota(cap_pick))[:, None], iota(items), 0),
        axis=1,
    )
    item_slot = own_owner * cap_row + own_row_rank

    code = (iota(row_count)[:, None] * half_pick + pick_rank).reshape(row_count, 2, child_blocks)
    slot_of = code.transpose(1, 0, 2).reshape(2, col_count, col_blocks)
    match = col_key[:, :, None, :] == (group * cap_col + iota(cap_col))[:, None]
    place = jnp.sum(jnp.where(match, slot_of[:, :, None, :], 0), axis=-1)
    col_local = (
        jnp.sum(jnp.where(match, by_col[:, :, None, :] - group * group_cols + 1, 0), axis=-1) - 1
    )

    row_slot = (iota(row_count)[:, None] * cap_row + row_rank).reshape(row_count, 2, child_blocks)
    row_match = by_row[..., None] == prow * row_blocks + iota(row_blocks)
    row_slot = jnp.sum(
        jnp.where(row_match, row_slot.transpose(1, 0, 2)[..., None] + 1, 0), axis=(1, 2)
    )
    row_valid = (row_slot > 0).astype(jnp.int32).reshape(-1)
    row_slot = jnp.maximum(row_slot - 1, 0).reshape(-1)

    pick_mine = (pick_item // child_blocks == half).astype(jnp.int32)
    panels = []
    for h in range(halves):
        at = slice(h * half_pick, (h + 1) * half_pick)
        picked = pick_rows(own_panel, other_panel, pick_item[at] % child_blocks, pick_mine[at])
        panels.append(lax.all_gather(picked, "prow", axis=0, tiled=True))

    device = lambda g, r: ((g // col_count) * row_count + r) * col_count + g % col_count
    everyone = ("half", "prow", "pcol")
    distance = (group + iota(group_count)) % group_count
    origins = (group - iota(group_count)) % group_count
    arrived = []
    for h in range(halves):
        picks = chosen[distance, h]
        if arrived:
            picks, arrived[-1] = lax.optimization_barrier((picks, arrived[-1]))
        packed = pack_columns(child_update[0], picks)
        got = [packed[0]]
        for d in range(1, group_count):
            pairs = [
                (device(g, r), device((g + d) % group_count, r))
                for g in range(group_count)
                for r in range(row_count)
            ]
            got.append(lax.ppermute(packed[d], everyone, pairs))
        arrived.append(got)

    parts, col_places = [], []
    for h in range(halves):
        for first in range(0, half_col, width):
            at = slice(h * half_col + first, h * half_col + first + width)
            col_places.append(col_local[:, :, at].reshape(2, -1))
            outgoing = schur_rows(
                own_panel,
                other_panel,
                arrived[h],
                panels[h],
                half,
                item_slot,
                place[:, :, at].reshape(-1),
                origins,
                row_count * cap_row,
                col_count,
                (first, width),
            )
            parts.append(lax.all_to_all(outgoing, "prow", split_axis=0, concat_axis=0, tiled=True))

    early = max(1, len(parts) // halves)
    raw = first_panel(root_front, parts[:early], row_slot, row_valid, col_places[:early])

    def to_groups(value):
        total = jnp.where(group == 0, value, 0.0)
        for g in range(1, group_count):
            pairs = [(device(0, r), device(g, r)) for r in range(row_count)]
            total = total + lax.ppermute(value, everyone, pairs)
        return total

    corner = raw[:RP]
    first = jnp.where(group == 0, corner, 0.0)
    for g in range(1, group_count):
        first = first + lax.ppermute(corner, everyone, [(device(0, 0), device(g, 0))])
    pivot = jnp.where(prow == 0, first, 0.0)
    for r in range(1, row_count):
        pivot = pivot + lax.ppermute(first, "prow", [(0, r)])
    factor = jnp.linalg.cholesky(pivot)
    inverse = lax.linalg.triangular_solve(
        factor, jnp.eye(RP, dtype=F32), left_side=True, lower=True
    )
    raw_rows = to_groups(raw)
    groups_of = row_count // ratio
    shift = (prow // ratio - group) % groups_of
    tile = jnp.where(shift == 0, raw_rows, 0.0)
    for k in range(1, groups_of):
        pairs = [
            (device(g, g * ratio + o), device(g, ((g + k) % groups_of) * ratio + o))
            for g in range(group_count)
            for o in range(ratio)
        ]
        got = lax.ppermute(raw_rows, ("half", "prow", "pcol"), pairs)
        tile = jnp.where(shift == k, got, tile)
    tiles = [tile]
    for o in range(1, ratio):
        pairs = [
            (r, (r // ratio) * ratio + (r % ratio + o) % ratio) for r in range(row_count)
        ]
        tiles.append(lax.ppermute(tile, "prow", pairs))
    offset = prow % ratio
    ordered = []
    for o in range(ratio):
        value = tiles[0]
        for k in range(1, ratio):
            value = jnp.where((offset - k) % ratio == o, tiles[k], value)
        ordered.append(value)
    raw_cols = jnp.concatenate(ordered, axis=0)
    solved = lax.dot_general(raw_rows, inverse, NT, precision=HIGHEST, preferred_element_type=F32)
    lower_cols = lax.dot_general(
        raw_cols, inverse, NT, precision=HIGHEST, preferred_element_type=F32
    )
    top = jnp.where(prow == 0, factor, solved[:RP])
    own_rows = jnp.concatenate([top, solved[RP:]], axis=0)
    flags = jnp.stack([(prow == 0), (group == 0)]).astype(jnp.int32)
    late = max(1, len(parts) - 1)
    root = advance(
        root_front, parts[:late], own_rows, lower_cols, row_slot, row_valid, col_places[:late], flags
    )
    for part, col_place in zip(parts[late:], col_places[late:]):
        root = deliver(root, part, row_slot, row_valid, col_place)
    return root


def solution(mesh):
    return jax.shard_map(
        shards,
        mesh=mesh,
        in_specs=(
            P("half", "prow", "pcol"),
            P("half", "prow", None),
            P("prow", ("half", "pcol")),
            P(),
        ),
        out_specs=P("prow", ("half", "pcol")),
        check_vma=False,
    )
```

```python
import functools

import jax
import jax.numpy as jnp
from jax import lax
from jax.experimental import pallas as pl
from jax.experimental.pallas import tpu as pltpu
from jax.sharding import PartitionSpec as P

BLK = 128
RP = 256
F32 = jnp.float32
BF16 = jnp.bfloat16
HIGHEST = lax.Precision.HIGHEST
NT = (((1,), (1,)), ((), ()))
VMEM_LIMIT = 56 * 1024 * 1024


def split(x):
    hi = x.astype(BF16)
    lo = (x - hi.astype(F32)).astype(BF16)
    return hi, lo


def dot_nt(a, b):
    return lax.dot_general(a, b, NT, preferred_element_type=F32)


def params():
    return pltpu.CompilerParams(vmem_limit_bytes=VMEM_LIMIT)


def cost(flops, nbytes):
    return pl.CostEstimate(flops=int(flops), bytes_accessed=int(nbytes), transcendentals=0)


def pack_columns(update, chosen):
    rows = update.shape[0]
    groups, width = chosen.shape

    def body(chosen_ref, *refs):
        for d in range(groups):
            refs[groups + d][0] = refs[d][...]

    def source(d):
        return pl.BlockSpec((rows, BLK), lambda u, s: (0, s[d * width + u]))

    return pl.pallas_call(
        body,
        grid_spec=pltpu.PrefetchScalarGridSpec(
            num_scalar_prefetch=1,
            grid=(width,),
            in_specs=[source(d) for d in range(groups)],
            out_specs=[pl.BlockSpec((1, rows, BLK), lambda u, s: (u, 0, 0))] * groups,
        ),
        out_shape=[jax.ShapeDtypeStruct((width, rows, BLK), F32)] * groups,
        compiler_params=params(),
        cost_estimate=cost(0, 8 * groups * width * rows * BLK),
    )(chosen.reshape(-1), *([update] * groups))


def pick_rows(own, other, block, mine):
    count = block.shape[0]
    depth = own.shape[1]

    def body(block_ref, mine_ref, own_ref, other_ref, out_ref):
        s = pl.program_id(0)

        @pl.when(mine_ref[s] == 1)
        def _():
            out_ref[0] = own_ref[...]

        @pl.when(mine_ref[s] == 0)
        def _():
            out_ref[0] = other_ref[...]

    spec = pl.BlockSpec((BLK, depth), lambda s, b, m: (b[s], 0))
    return pl.pallas_call(
        body,
        grid_spec=pltpu.PrefetchScalarGridSpec(
            num_scalar_prefetch=2,
            grid=(count,),
            in_specs=[spec, spec],
            out_specs=pl.BlockSpec((1, BLK, depth), lambda s, b, m: (s, 0, 0)),
        ),
        out_shape=jax.ShapeDtypeStruct((count, BLK, depth), F32),
        compiler_params=params(),
        cost_estimate=cost(0, 12 * count * BLK * depth),
    )(block, mine, own, other)


def schur_rows(own, other, arrived, panels, half, item_slot, places, origins, slots, col_count, span):
    groups = len(arrived)
    depth = own.shape[1]
    first, width = span
    rows = arrived[0].shape[1]
    child_blocks = rows // BLK
    tall = 2 if child_blocks % 2 == 0 else 1
    steps = child_blocks // tall
    per_child = col_count * width
    wide = per_child * BLK
    piece = next(w for w in (512, 384, 256, 128) if wide % w == 0)

    def body(half_ref, slot_ref, place_ref, origin_ref, own_ref, other_ref, *rest):
        in_refs = rest[:groups]
        panel_ref, out_ref, staged, hi_ref, lo_ref, total_ref, result, load_sem, store_sem = rest[groups:]
        c = pl.program_id(0)
        step = c * steps + pl.program_id(1)

        @pl.when(step == 0)
        def _():
            @pl.loop(0, 2 * per_child)
            def _(k):
                pltpu.make_async_copy(panel_ref.at[place_ref[k]], staged.at[k], load_sem.at[k]).start()

            @pl.loop(0, 2 * per_child)
            def _(k):
                pltpu.make_async_copy(panel_ref.at[place_ref[k]], staged.at[k], load_sem.at[k]).wait()
                hi, lo = split(staged[k])
                hi_ref[k] = hi
                lo_ref[k] = lo

        a_hi, a_lo = split(jnp.where(c == half_ref[0], own_ref[...], other_ref[...]))
        stacked = jnp.concatenate([a_hi, a_lo], axis=0)
        high = tall * BLK
        at_once = piece // BLK
        for n in range(0, per_child, at_once):
            at = pl.ds(c * per_child + n, at_once)
            both = dot_nt(stacked, hi_ref[at].reshape(piece, depth))
            total = both[:high] + both[high:] + dot_nt(a_hi, lo_ref[at].reshape(piece, depth))
            for k in range(at_once):
                total_ref[n + k] = total[:, k * BLK : (k + 1) * BLK]

        buffer = step % 2

        def store(m, at_step):
            item = at_step * tall + m
            return pltpu.make_async_copy(
                result.at[at_step % 2, m], out_ref.at[slot_ref[item]], store_sem.at[at_step % 2, m]
            )

        @pl.when(step >= 2)
        def _():
            for m in range(tall):
                store(m, step - 2).wait()

        for d in range(groups):

            @pl.when(origin_ref[d] // col_count == c)
            def _():
                q = origin_ref[d] % col_count
                for u in range(width):
                    for m in range(tall):
                        at = slice(m * BLK, (m + 1) * BLK)
                        result[buffer, m, q, u] = in_refs[d][u, at, :] - total_ref[q * width + u, at, :]

        for m in range(tall):
            store(m, step).start()

        @pl.when(step == 2 * steps - 1)
        def _():
            for m in range(tall):
                if steps > 0:
                    store(m, step - 1).wait()
                store(m, step).wait()

    def stay(c, i, mine):
        return jnp.where(c == mine, i, jnp.where(c < mine, 0, steps - 1))

    def arrival(d):
        return pl.BlockSpec(
            (width, tall * BLK, BLK),
            lambda c, i, h, t, p, o: (first // width, stay(c, i, o[d] // col_count), 0),
        )

    return pl.pallas_call(
        body,
        grid_spec=pltpu.PrefetchScalarGridSpec(
            num_scalar_prefetch=4,
            grid=(2, steps),
            in_specs=[
                pl.BlockSpec((tall * BLK, depth), lambda c, i, h, t, p, o: (stay(c, i, h[0]), 0)),
                pl.BlockSpec((tall * BLK, depth), lambda c, i, h, t, p, o: (stay(c, i, 1 - h[0]), 0)),
            ]
            + [arrival(d) for d in range(groups)]
            + [pl.BlockSpec(memory_space=pl.ANY)],
            out_specs=pl.BlockSpec(memory_space=pl.ANY),
            scratch_shapes=[
                pltpu.VMEM((2 * per_child, BLK, depth), F32),
                pltpu.VMEM((2 * per_child, BLK, depth), BF16),
                pltpu.VMEM((2 * per_child, BLK, depth), BF16),
                pltpu.VMEM((per_child, tall * BLK, BLK), F32),
                pltpu.VMEM((2, tall, col_count, width, BLK, BLK), F32),
                pltpu.SemaphoreType.DMA((2 * per_child,)),
                pltpu.SemaphoreType.DMA((2, tall)),
            ],
        ),
        out_shape=jax.ShapeDtypeStruct((slots, col_count, width, BLK, BLK), F32),
        compiler_params=params(),
        cost_estimate=cost(
            12 * rows * wide * depth, 8 * rows * (depth + 2 * wide) + 8 * wide * depth
        ),
    )(half.reshape(1), item_slot, places, origins, own, other, *arrived, panels)


def first_panel(root, parts, row_slot, row_valid, col_places):
    row_blocks = root.shape[0] // BLK
    count = len(parts)
    _, col_count, width, _, _ = parts[0].shape

    def body(slot_ref, valid_ref, place_ref, root_ref, *rest):
        a_refs, out_ref = rest[:-1], rest[-1]
        r = pl.program_id(0)
        out_ref[...] = root_ref[...]
        for c in range(2):
            for k in range(count * col_count * width):
                j, q, u = k // (col_count * width), k // width % col_count, k % width
                col = place_ref[c, k]
                ok = (valid_ref[c * row_blocks + r] == 1) & (col >= 0) & (col < RP // BLK)

                @pl.when(ok)
                def _():
                    at = pl.ds(pl.multiple_of(col * BLK, BLK), BLK)
                    out_ref[:, at] += a_refs[c * count + j][0, q, u]

    def arrived(c):
        return pl.BlockSpec(
            (1, col_count, width, BLK, BLK), lambda r, s, v, p: (s[c * row_blocks + r], 0, 0, 0, 0)
        )

    panel = pl.BlockSpec((BLK, RP), lambda r, s, v, p: (r, 0))
    return pl.pallas_call(
        body,
        grid_spec=pltpu.PrefetchScalarGridSpec(
            num_scalar_prefetch=3,
            grid=(row_blocks,),
            in_specs=[panel] + [arrived(0)] * count + [arrived(1)] * count,
            out_specs=panel,
        ),
        out_shape=jax.ShapeDtypeStruct((root.shape[0], RP), F32),
        compiler_params=params(),
        cost_estimate=cost(0, 8 * root.shape[0] * RP + 4 * sum(p.size for p in parts)),
    )(row_slot, row_valid, jnp.concatenate(col_places, axis=1), root, *parts, *parts)


def pivot_part(root, outgoing, row_child, row_place, col_places, flag):
    count = len(outgoing)
    cap_row = row_child.shape[0]
    _, col_count, width, _, _ = outgoing[0].shape

    def body(child_ref, row_ref, place_ref, flag_ref, root_ref, *rest):
        a_refs, out_ref = rest[:-1], rest[-1]
        out_ref[...] = jnp.where(flag_ref[0] == 1, root_ref[...], 0.0)
        for w in range(cap_row):
            row = row_ref[w]
            for k in range(count * col_count * width):
                j, q, u = k // (col_count * width), k // width % col_count, k % width
                col = place_ref[child_ref[w], k]

                @pl.when((row >= 0) & (row < RP // BLK) & (col >= 0) & (col < RP // BLK))
                def _():
                    at_row = pl.ds(pl.multiple_of(row * BLK, BLK), BLK)
                    at_col = pl.ds(pl.multiple_of(col * BLK, BLK), BLK)
                    out_ref[at_row, at_col] += a_refs[j][w, q, u]

    corner = pl.BlockSpec((RP, RP), lambda i, c, r, p, f: (0, 0))
    leading = pl.BlockSpec((cap_row, col_count, width, BLK, BLK), lambda i, c, r, p, f: (0,) * 5)
    return pl.pallas_call(
        body,
        grid_spec=pltpu.PrefetchScalarGridSpec(
            num_scalar_prefetch=4,
            grid=(1,),
            in_specs=[corner] + [leading] * count,
            out_specs=corner,
        ),
        out_shape=jax.ShapeDtypeStruct((RP, RP), F32),
        compiler_params=params(),
        cost_estimate=cost(0, 8 * RP * RP + 4 * count * cap_row * col_count * width * BLK * BLK),
    )(row_child, row_place, jnp.concatenate(col_places, axis=1), flag.reshape(1), root, *outgoing)


def advance(root, parts, own_rows, columns, row_slot, row_valid, col_places, flags):
    rows, cols = root.shape
    row_blocks = rows // BLK
    count = len(parts)
    _, col_count, width, _, _ = parts[0].shape
    step = next(w for w in (512, 384, 256) if cols % w == 0)

    def body(slot_ref, valid_ref, place_ref, flag_ref, root_ref, *rest):
        a_refs = rest[: 2 * count]
        own_ref, col_ref, out_ref, hi_ref, lo_ref = rest[2 * count :]
        r = pl.program_id(0)

        @pl.when(r == 0)
        def _():
            hi, lo = split(col_ref[...])
            hi_ref[...] = hi
            lo_ref[...] = lo

        pivot_rows = (flag_ref[0] == 1) & (r < RP // BLK)

        @pl.when(pivot_rows)
        def _():
            out_ref[...] = root_ref[...]

        @pl.when(jnp.logical_not(pivot_rows))
        def _():
            a_hi, a_lo = split(own_ref[...])
            stacked = jnp.concatenate([a_hi, a_lo], axis=0)
            for n in range(0, cols, step):
                both = dot_nt(stacked, hi_ref[n : n + step, :])
                total = both[:BLK] + both[BLK:] + dot_nt(a_hi, lo_ref[n : n + step, :])
                out_ref[:, n : n + step] = root_ref[:, n : n + step] - total

        for c in range(2):
            for j in range(count):
                for q in range(col_count):
                    for u in range(width):
                        col = place_ref[c, (j * col_count + q) * width + u]

                        @pl.when((valid_ref[c * row_blocks + r] == 1) & (col >= 0))
                        def _():
                            at = pl.ds(pl.multiple_of(col * BLK, BLK), BLK)
                            out_ref[:, at] += a_refs[c * count + j][0, q, u]

        @pl.when(flag_ref[1] == 1)
        def _():
            out_ref[:, :RP] = own_ref[...]

    def arrived(c):
        return pl.BlockSpec(
            (1, col_count, width, BLK, BLK),
            lambda r, s, v, p, f: (s[c * row_blocks + r], 0, 0, 0, 0),
        )

    return pl.pallas_call(
        body,
        grid_spec=pltpu.PrefetchScalarGridSpec(
            num_scalar_prefetch=4,
            grid=(row_blocks,),
            in_specs=[pl.BlockSpec((BLK, cols), lambda r, s, v, p, f: (r, 0))]
            + [arrived(0)] * count
            + [arrived(1)] * count
            + [
                pl.BlockSpec((BLK, RP), lambda r, s, v, p, f: (r, 0)),
                pl.BlockSpec((cols, RP), lambda r, s, v, p, f: (0, 0)),
            ],
            out_specs=pl.BlockSpec((BLK, cols), lambda r, s, v, p, f: (r, 0)),
            scratch_shapes=[pltpu.VMEM((cols, RP), BF16), pltpu.VMEM((cols, RP), BF16)],
        ),
        out_shape=jax.ShapeDtypeStruct((rows, cols), F32),
        compiler_params=params(),
        cost_estimate=cost(6 * rows * cols * RP, 8 * rows * cols + 4 * sum(p.size for p in parts)),
    )(
        row_slot,
        row_valid,
        jnp.concatenate(col_places, axis=1),
        flags,
        root,
        *parts,
        *parts,
        own_rows,
        columns,
    )


def deliver(root, part, row_slot, row_valid, col_place):
    rows, cols = root.shape
    row_blocks = rows // BLK
    _, col_count, width, _, _ = part.shape

    def body(slot_ref, valid_ref, place_ref, root_ref, a0_ref, a1_ref, out_ref):
        r = pl.program_id(0)
        out_ref[...] = root_ref[...]
        for c, a_ref in enumerate((a0_ref, a1_ref)):

            @pl.when(valid_ref[c * row_blocks + r] == 1)
            def _():
                for q in range(col_count):
                    for u in range(width):
                        col = place_ref[c, q * width + u]

                        @pl.when(col >= 0)
                        def _():
                            at = pl.ds(pl.multiple_of(col * BLK, BLK), BLK)
                            out_ref[:, at] += a_ref[0, q, u]

    def arrived(c):
        return pl.BlockSpec(
            (1, col_count, width, BLK, BLK), lambda r, s, v, p: (s[c * row_blocks + r], 0, 0, 0, 0)
        )

    whole = pl.BlockSpec((BLK, cols), lambda r, s, v, p: (r, 0))
    return pl.pallas_call(
        body,
        grid_spec=pltpu.PrefetchScalarGridSpec(
            num_scalar_prefetch=3,
            grid=(row_blocks,),
            in_specs=[whole, arrived(0), arrived(1)],
            out_specs=whole,
        ),
        out_shape=jax.ShapeDtypeStruct((rows, cols), F32),
        compiler_params=params(),
        cost_estimate=cost(0, 8 * rows * cols + 4 * part.size),
    )(row_slot, row_valid, col_place, root, part, part)


def shards(child_update, child_panel, root_front, index_map):
    col_count = lax.axis_size("pcol")
    row_count = lax.axis_size("prow")
    group_count = 2 * col_count
    half = lax.axis_index("half")
    pcol = lax.axis_index("pcol")
    prow = lax.axis_index("prow")
    group = half * col_count + pcol
    rows_dev = child_update.shape[1]
    root_rows, root_cols = root_front.shape
    child_blocks = rows_dev // BLK
    col_blocks = child_update.shape[2] // BLK
    row_blocks = root_rows // BLK
    group_cols = root_cols // BLK
    ratio = root_cols // root_rows
    cap_col = max(1, col_blocks // group_count)
    cap_row = max(1, 2 * child_blocks // row_count)
    cap_pick = cap_row * ratio
    even = col_blocks == group_count * cap_col and 2 * child_blocks == row_count * cap_row
    halves = 2 if even and cap_pick % 2 == 0 and cap_col % 2 == 0 else 1
    half_col, half_pick = cap_col // halves, cap_pick // halves
    width = half_col // 2 if half_col % 2 == 0 else half_col
    iota = functools.partial(jnp.arange, dtype=jnp.int32)
    own_panel = child_panel[0]
    other_panel = lax.ppermute(own_panel, "half", [(0, 1), (1, 0)])

    by_col = index_map.reshape(2, col_count, col_blocks)
    by_row = index_map.reshape(2, row_count, child_blocks)
    key = by_row // group_cols
    if halves == 2:
        in_group = key[..., None] == iota(group_count)
        named = jnp.sum(in_group.astype(jnp.int32), axis=2)
        leading = jnp.sum((in_group & (by_row[..., None] < RP // BLK)).astype(jnp.int32), axis=2)
        least = jnp.maximum(jnp.maximum(half_pick - named[1], leading[0]), 0)
        most = jnp.minimum(jnp.minimum(named[0], half_pick - leading[1]), half_pick)
        least = least.reshape(col_count, row_count // col_count, group_count)
        room = most.reshape(least.shape) - least
        rest = half_col - jnp.sum(least, axis=1, keepdims=True)
        taken = least + jnp.clip(rest - (jnp.cumsum(room, axis=1) - room), 0, room)
        taken = taken.reshape(row_count, group_count)
        taken = jnp.stack([taken, half_pick - taken])
        ahead = (by_row[..., None, :] < by_row[..., :, None]) & (key[..., None, :] == key[..., :, None])
        place_in = jnp.sum(ahead.astype(jnp.int32), axis=-1)
        limit = jnp.sum(jnp.where(in_group, taken[:, :, None, :], 0), axis=-1)
        key = 2 * key + (place_in >= limit).astype(jnp.int32)

    col_key = key.reshape(2, col_count, col_blocks)
    before = (col_key[..., None, :] == col_key[..., :, None]) & (
        iota(col_blocks)[None, :] < iota(col_blocks)[:, None]
    )
    col_key = col_key * half_col + jnp.sum(before.astype(jnp.int32), axis=-1)
    own_key = lax.dynamic_index_in_dim(
        col_key.reshape(group_count, col_blocks), group, 0, keepdims=False
    )
    chosen = jnp.sum(
        jnp.where(own_key[None, :] == iota(group_count * cap_col)[:, None], iota(col_blocks), 0),
        axis=1,
    ).reshape(group_count, halves, half_col)

    joint = by_row.transpose(1, 0, 2).reshape(row_count, 2 * child_blocks)
    items = 2 * child_blocks
    earlier = iota(items)[None, :] < iota(items)[:, None]
    owner = joint // row_blocks
    row_rank = jnp.sum(
        ((owner[:, None, :] == owner[:, :, None]) & earlier).astype(jnp.int32), axis=-1
    )
    joint_key = key.transpose(1, 0, 2).reshape(row_count, items)
    pick_rank = jnp.sum(
        ((joint_key[:, None, :] == joint_key[:, :, None]) & earlier).astype(jnp.int32), axis=-1
    )
    here = lax.dynamic_index_in_dim
    own_owner = here(owner, prow, 0, keepdims=False)
    own_row_rank = here(row_rank, prow, 0, keepdims=False)
    own_pick = here(joint_key * half_pick + pick_rank, prow, 0, keepdims=False)
    pick_item = jnp.sum(
        jnp.where(own_pick[None, :] == (group * cap_pick + iota(cap_pick))[:, None], iota(items), 0),
        axis=1,
    )
    item_slot = own_owner * cap_row + own_row_rank

    code = (iota(row_count)[:, None] * half_pick + pick_rank).reshape(row_count, 2, child_blocks)
    slot_of = code.transpose(1, 0, 2).reshape(2, col_count, col_blocks)
    match = col_key[:, :, None, :] == (group * cap_col + iota(cap_col))[:, None]
    place = jnp.sum(jnp.where(match, slot_of[:, :, None, :], 0), axis=-1)
    col_local = (
        jnp.sum(jnp.where(match, by_col[:, :, None, :] - group * group_cols + 1, 0), axis=-1) - 1
    )

    row_slot = (iota(row_count)[:, None] * cap_row + row_rank).reshape(row_count, 2, child_blocks)
    row_match = by_row[..., None] == prow * row_blocks + iota(row_blocks)
    row_slot = jnp.sum(
        jnp.where(row_match, row_slot.transpose(1, 0, 2)[..., None] + 1, 0), axis=(1, 2)
    )
    row_valid = (row_slot > 0).astype(jnp.int32).reshape(-1)
    row_slot = jnp.maximum(row_slot - 1, 0).reshape(-1)

    pick_mine = (pick_item // child_blocks == half).astype(jnp.int32)
    picked = []
    for h in range(halves):
        at = slice(h * half_pick, (h + 1) * half_pick)
        picked.append(pick_rows(own_panel, other_panel, pick_item[at] % child_blocks, pick_mine[at]))

    device = lambda g, r: ((g // col_count) * row_count + r) * col_count + g % col_count
    everyone = ("half", "prow", "pcol")
    distance = (group + iota(group_count)) % group_count
    origins = (group - iota(group_count)) % group_count
    arrived = []
    packed = [pack_columns(child_update[0], chosen[distance, h]) for h in range(halves)]
    origins, picked[1:], packed[1:] = lax.optimization_barrier((origins, picked[1:], packed[1:]))
    panels = [lax.all_gather(value, "prow", axis=0, tiled=True) for value in picked]
    for h in range(halves):
        if arrived:
            packed[h], arrived[-1] = lax.optimization_barrier((packed[h], arrived[-1]))
        got = [packed[h][0]]
        for d in range(1, group_count):
            pairs = [
                (device(g, r), device((g + d) % group_count, r))
                for g in range(group_count)
                for r in range(row_count)
            ]
            got.append(lax.ppermute(packed[h][d], everyone, pairs))
        arrived.append(got)

    outgoing, parts, col_places = [], [], []
    for h in range(halves):
        for first in range(0, half_col, width):
            at = slice(h * half_col + first, h * half_col + first + width)
            col_places.append(col_local[:, :, at].reshape(2, -1))
            if len(outgoing) == 1:
                origins, outgoing[0], arrived = lax.optimization_barrier(
                    (origins, outgoing[0], arrived)
                )
            elif outgoing:
                origins, outgoing[-1] = lax.optimization_barrier((origins, outgoing[-1]))
            outgoing.append(
                schur_rows(
                    own_panel,
                    other_panel,
                    arrived[h],
                    panels[h],
                    half,
                    item_slot,
                    place[:, :, at].reshape(-1),
                    origins,
                    row_count * cap_row,
                    col_count,
                    (first, width),
                )
            )
            parts.append(
                lax.all_to_all(outgoing[-1], "prow", split_axis=0, concat_axis=0, tiled=True)
            )
    early = max(1, len(parts) // halves)

    to_first = (own_owner == 0)[None, :] & (own_row_rank[None, :] == iota(cap_row)[:, None])
    own_joint = here(joint, prow, 0, keepdims=False)
    row_child = jnp.sum(jnp.where(to_first, iota(items) // child_blocks, 0), axis=1)
    row_place = jnp.sum(jnp.where(to_first, own_joint + 1, 0), axis=1) - 1
    pivot = pivot_part(
        root_front,
        outgoing[:early],
        row_child,
        row_place,
        col_places[:early],
        ((prow == 0) & (group == 0)).astype(jnp.int32),
    )
    step = 1
    while step < row_count:
        pivot = pivot + lax.ppermute(pivot, "prow", [(r, r ^ step) for r in range(row_count)])
        step *= 2
    pivot, parts[0] = lax.optimization_barrier((pivot, parts[0]))
    factor = jnp.linalg.cholesky(pivot)
    inverse = lax.linalg.triangular_solve(
        factor, jnp.eye(RP, dtype=F32), left_side=True, lower=True
    )

    raw = first_panel(root_front, parts[:early], row_slot, row_valid, col_places[:early])
    solved = lax.dot_general(raw, inverse, NT, precision=HIGHEST, preferred_element_type=F32)
    top = jnp.where(prow == 0, factor, solved[:RP])
    solved = jnp.concatenate([top, solved[RP:]], axis=0)
    own_rows = jnp.where(group == 0, solved, 0.0)
    for g in range(1, group_count):
        pairs = [(device(0, r), device(g, r)) for r in range(row_count)]
        own_rows = own_rows + lax.ppermute(solved, everyone, pairs)
    groups_of = row_count // ratio
    shift = (prow // ratio - group) % groups_of
    tile = jnp.where(shift == 0, own_rows, 0.0)
    for k in range(1, groups_of):
        pairs = [
            (device(g, g * ratio + o), device(g, ((g + k) % groups_of) * ratio + o))
            for g in range(group_count)
            for o in range(ratio)
        ]
        got = lax.ppermute(own_rows, everyone, pairs)
        tile = jnp.where(shift == k, got, tile)
    tiles = [tile]
    for o in range(1, ratio):
        pairs = [
            (r, (r // ratio) * ratio + (r % ratio + o) % ratio) for r in range(row_count)
        ]
        tiles.append(lax.ppermute(tile, "prow", pairs))
    offset = prow % ratio
    ordered = []
    for o in range(ratio):
        value = tiles[0]
        for k in range(1, ratio):
            value = jnp.where((offset - k) % ratio == o, tiles[k], value)
        ordered.append(value)
    lower_cols = jnp.concatenate(ordered, axis=0)
    flags = jnp.stack([(prow == 0), (group == 0)]).astype(jnp.int32)
    late = max(1, len(parts) - 1)
    root = advance(
        root_front, parts[:late], own_rows, lower_cols, row_slot, row_valid, col_places[:late], flags
    )
    for part, col_place in zip(parts[late:], col_places[late:]):
        root = deliver(root, part, row_slot, row_valid, col_place)
    return root


def solution(mesh):
    return jax.shard_map(
        shards,
        mesh=mesh,
        in_specs=(
            P("half", "prow", "pcol"),
            P("half", "prow", None),
            P("prow", ("half", "pcol")),
            P(),
        ),
        out_specs=P("prow", ("half", "pcol")),
        check_vma=False,
    )
```

```python
import functools

import jax
import jax.numpy as jnp
from jax import lax
from jax.experimental import pallas as pl
from jax.experimental.pallas import tpu as pltpu
from jax.sharding import PartitionSpec as P

BLK = 128
RP = 256
F32 = jnp.float32
BF16 = jnp.bfloat16
HIGHEST = lax.Precision.HIGHEST
NT = (((1,), (1,)), ((), ()))
VMEM_LIMIT = 56 * 1024 * 1024


def split(x):
    hi = x.astype(BF16)
    lo = (x - hi.astype(F32)).astype(BF16)
    return hi, lo


def dot_nt(a, b):
    return lax.dot_general(a, b, NT, preferred_element_type=F32)


def params():
    return pltpu.CompilerParams(vmem_limit_bytes=VMEM_LIMIT)


def cost(flops, nbytes):
    return pl.CostEstimate(flops=int(flops), bytes_accessed=int(nbytes), transcendentals=0)


def pack_columns(update, chosen):
    rows = update.shape[0]
    groups, width = chosen.shape

    def body(chosen_ref, *refs):
        for d in range(groups):
            refs[groups + d][0] = refs[d][...]

    def source(d):
        return pl.BlockSpec((rows, BLK), lambda u, s: (0, s[d * width + u]))

    return pl.pallas_call(
        body,
        grid_spec=pltpu.PrefetchScalarGridSpec(
            num_scalar_prefetch=1,
            grid=(width,),
            in_specs=[source(d) for d in range(groups)],
            out_specs=[pl.BlockSpec((1, rows, BLK), lambda u, s: (u, 0, 0))] * groups,
        ),
        out_shape=[jax.ShapeDtypeStruct((width, rows, BLK), F32)] * groups,
        compiler_params=params(),
        cost_estimate=cost(0, 8 * groups * width * rows * BLK),
    )(chosen.reshape(-1), *([update] * groups))


def pick_rows(own, other, block, mine):
    count = block.shape[0]
    depth = own.shape[1]

    def body(block_ref, mine_ref, own_ref, other_ref, out_ref):
        s = pl.program_id(0)

        @pl.when(mine_ref[s] == 1)
        def _():
            out_ref[0] = own_ref[...]

        @pl.when(mine_ref[s] == 0)
        def _():
            out_ref[0] = other_ref[...]

    spec = pl.BlockSpec((BLK, depth), lambda s, b, m: (b[s], 0))
    return pl.pallas_call(
        body,
        grid_spec=pltpu.PrefetchScalarGridSpec(
            num_scalar_prefetch=2,
            grid=(count,),
            in_specs=[spec, spec],
            out_specs=pl.BlockSpec((1, BLK, depth), lambda s, b, m: (s, 0, 0)),
        ),
        out_shape=jax.ShapeDtypeStruct((count, BLK, depth), F32),
        compiler_params=params(),
        cost_estimate=cost(0, 12 * count * BLK * depth),
    )(block, mine, own, other)


def schur_rows(own, other, arrived, panels, half, item_slot, places, origins, slots, col_count, span):
    groups = len(arrived)
    depth = own.shape[1]
    first, width = span
    rows = arrived[0].shape[1]
    child_blocks = rows // BLK
    tall = 2 if child_blocks % 2 == 0 else 1
    steps = child_blocks // tall
    per_child = col_count * width
    wide = per_child * BLK
    piece = next(w for w in (512, 384, 256, 128) if wide % w == 0)

    def body(half_ref, slot_ref, place_ref, origin_ref, own_ref, other_ref, *rest):
        in_refs = rest[:groups]
        panel_ref, out_ref, staged, hi_ref, lo_ref, total_ref, result, load_sem, store_sem = rest[groups:]
        c = pl.program_id(0)
        step = c * steps + pl.program_id(1)

        @pl.when(step == 0)
        def _():
            @pl.loop(0, 2 * per_child)
            def _(k):
                pltpu.make_async_copy(panel_ref.at[place_ref[k]], staged.at[k], load_sem.at[k]).start()

            @pl.loop(0, 2 * per_child)
            def _(k):
                pltpu.make_async_copy(panel_ref.at[place_ref[k]], staged.at[k], load_sem.at[k]).wait()
                hi, lo = split(staged[k])
                hi_ref[k] = hi
                lo_ref[k] = lo

        a_hi, a_lo = split(jnp.where(c == half_ref[0], own_ref[...], other_ref[...]))
        stacked = jnp.concatenate([a_hi, a_lo], axis=0)
        high = tall * BLK
        at_once = piece // BLK
        for n in range(0, per_child, at_once):
            at = pl.ds(c * per_child + n, at_once)
            both = dot_nt(stacked, hi_ref[at].reshape(piece, depth))
            total = both[:high] + both[high:] + dot_nt(a_hi, lo_ref[at].reshape(piece, depth))
            for k in range(at_once):
                total_ref[n + k] = total[:, k * BLK : (k + 1) * BLK]

        buffer = step % 2

        def store(m, at_step):
            item = at_step * tall + m
            return pltpu.make_async_copy(
                result.at[at_step % 2, m], out_ref.at[slot_ref[item]], store_sem.at[at_step % 2, m]
            )

        @pl.when(step >= 2)
        def _():
            for m in range(tall):
                store(m, step - 2).wait()

        for d in range(groups):

            @pl.when(origin_ref[d] // col_count == c)
            def _():
                q = origin_ref[d] % col_count
                for u in range(width):
                    for m in range(tall):
                        at = slice(m * BLK, (m + 1) * BLK)
                        result[buffer, m, q, u] = in_refs[d][u, at, :] - total_ref[q * width + u, at, :]

        for m in range(tall):
            store(m, step).start()

        @pl.when(step == 2 * steps - 1)
        def _():
            for m in range(tall):
                if steps > 0:
                    store(m, step - 1).wait()
                store(m, step).wait()

    def stay(c, i, mine):
        return jnp.where(c == mine, i, jnp.where(c < mine, 0, steps - 1))

    def arrival(d):
        return pl.BlockSpec(
            (width, tall * BLK, BLK),
            lambda c, i, h, t, p, o: (first // width, stay(c, i, o[d] // col_count), 0),
        )

    return pl.pallas_call(
        body,
        grid_spec=pltpu.PrefetchScalarGridSpec(
            num_scalar_prefetch=4,
            grid=(2, steps),
            in_specs=[
                pl.BlockSpec((tall * BLK, depth), lambda c, i, h, t, p, o: (stay(c, i, h[0]), 0)),
                pl.BlockSpec((tall * BLK, depth), lambda c, i, h, t, p, o: (stay(c, i, 1 - h[0]), 0)),
            ]
            + [arrival(d) for d in range(groups)]
            + [pl.BlockSpec(memory_space=pl.ANY)],
            out_specs=pl.BlockSpec(memory_space=pl.ANY),
            scratch_shapes=[
                pltpu.VMEM((2 * per_child, BLK, depth), F32),
                pltpu.VMEM((2 * per_child, BLK, depth), BF16),
                pltpu.VMEM((2 * per_child, BLK, depth), BF16),
                pltpu.VMEM((per_child, tall * BLK, BLK), F32),
                pltpu.VMEM((2, tall, col_count, width, BLK, BLK), F32),
                pltpu.SemaphoreType.DMA((2 * per_child,)),
                pltpu.SemaphoreType.DMA((2, tall)),
            ],
        ),
        out_shape=jax.ShapeDtypeStruct((slots, col_count, width, BLK, BLK), F32),
        compiler_params=params(),
        cost_estimate=cost(
            12 * rows * wide * depth, 8 * rows * (depth + 2 * wide) + 8 * wide * depth
        ),
    )(half.reshape(1), item_slot, places, origins, own, other, *arrived, panels)


def first_panel(root, parts, row_slot, row_valid, col_places):
    row_blocks = root.shape[0] // BLK
    count = len(parts)
    _, col_count, width, _, _ = parts[0].shape

    def body(slot_ref, valid_ref, place_ref, root_ref, *rest):
        a_refs, out_ref = rest[:-1], rest[-1]
        r = pl.program_id(0)
        out_ref[...] = root_ref[...]
        for c in range(2):
            for k in range(count * col_count * width):
                j, q, u = k // (col_count * width), k // width % col_count, k % width
                col = place_ref[c, k]
                ok = (valid_ref[c * row_blocks + r] == 1) & (col >= 0) & (col < RP // BLK)

                @pl.when(ok)
                def _():
                    at = pl.ds(pl.multiple_of(col * BLK, BLK), BLK)
                    out_ref[:, at] += a_refs[c * count + j][0, q, u]

    def arrived(c):
        return pl.BlockSpec(
            (1, col_count, width, BLK, BLK), lambda r, s, v, p: (s[c * row_blocks + r], 0, 0, 0, 0)
        )

    panel = pl.BlockSpec((BLK, RP), lambda r, s, v, p: (r, 0))
    return pl.pallas_call(
        body,
        grid_spec=pltpu.PrefetchScalarGridSpec(
            num_scalar_prefetch=3,
            grid=(row_blocks,),
            in_specs=[panel] + [arrived(0)] * count + [arrived(1)] * count,
            out_specs=panel,
        ),
        out_shape=jax.ShapeDtypeStruct((root.shape[0], RP), F32),
        compiler_params=params(),
        cost_estimate=cost(0, 8 * root.shape[0] * RP + 4 * sum(p.size for p in parts)),
    )(row_slot, row_valid, jnp.concatenate(col_places, axis=1), root, *parts, *parts)


def pivot_part(root, outgoing, row_child, row_place, col_places, flag):
    count = len(outgoing)
    cap_row = row_child.shape[0]
    _, col_count, width, _, _ = outgoing[0].shape

    def body(child_ref, row_ref, place_ref, flag_ref, root_ref, *rest):
        a_refs, out_ref = rest[:-1], rest[-1]
        out_ref[...] = jnp.where(flag_ref[0] == 1, root_ref[...], 0.0)
        for w in range(cap_row):
            row = row_ref[w]
            for k in range(count * col_count * width):
                j, q, u = k // (col_count * width), k // width % col_count, k % width
                col = place_ref[child_ref[w], k]

                @pl.when((row >= 0) & (row < RP // BLK) & (col >= 0) & (col < RP // BLK))
                def _():
                    at_row = pl.ds(pl.multiple_of(row * BLK, BLK), BLK)
                    at_col = pl.ds(pl.multiple_of(col * BLK, BLK), BLK)
                    out_ref[at_row, at_col] += a_refs[j][w, q, u]

    corner = pl.BlockSpec((RP, RP), lambda i, c, r, p, f: (0, 0))
    leading = pl.BlockSpec((cap_row, col_count, width, BLK, BLK), lambda i, c, r, p, f: (0,) * 5)
    return pl.pallas_call(
        body,
        grid_spec=pltpu.PrefetchScalarGridSpec(
            num_scalar_prefetch=4,
            grid=(1,),
            in_specs=[corner] + [leading] * count,
            out_specs=corner,
        ),
        out_shape=jax.ShapeDtypeStruct((RP, RP), F32),
        compiler_params=params(),
        cost_estimate=cost(0, 8 * RP * RP + 4 * count * cap_row * col_count * width * BLK * BLK),
    )(row_child, row_place, jnp.concatenate(col_places, axis=1), flag.reshape(1), root, *outgoing)


def advance(root, parts, own_rows, columns, row_slot, row_valid, col_places, flags):
    rows, cols = root.shape
    row_blocks = rows // BLK
    count = len(parts)
    _, col_count, width, _, _ = parts[0].shape
    step = next(w for w in (512, 384, 256) if cols % w == 0)
    tall = 2 if row_blocks % 2 == 0 else 1
    high = tall * BLK

    def body(slot_ref, valid_ref, place_ref, flag_ref, root_ref, *rest):
        a_refs = rest[: 2 * tall * count]
        own_ref, col_ref, out_ref, hi_ref, lo_ref = rest[2 * tall * count :]
        r = pl.program_id(0)

        @pl.when(r == 0)
        def _():
            hi, lo = split(col_ref[...])
            hi_ref[...] = hi
            lo_ref[...] = lo

        pivot_rows = (flag_ref[0] == 1) & (r * high < RP)

        @pl.when(pivot_rows)
        def _():
            out_ref[...] = root_ref[...]

        @pl.when(jnp.logical_not(pivot_rows))
        def _():
            a_hi, a_lo = split(own_ref[...])
            stacked = jnp.concatenate([a_hi, a_lo], axis=0)
            for n in range(0, cols, step):
                both = dot_nt(stacked, hi_ref[n : n + step, :])
                total = both[:high] + both[high:] + dot_nt(a_hi, lo_ref[n : n + step, :])
                out_ref[:, n : n + step] = root_ref[:, n : n + step] - total

        for c in range(2):
            for m in range(tall):

                @pl.when(valid_ref[c * row_blocks + r * tall + m] == 1)
                def _():
                    for j in range(count):
                        for q in range(col_count):
                            for u in range(width):
                                col = place_ref[c, (j * col_count + q) * width + u]
                                a_ref = a_refs[(c * tall + m) * count + j]

                                @pl.when(col >= 0)
                                def _():
                                    at = pl.ds(pl.multiple_of(col * BLK, BLK), BLK)
                                    out_ref[m * BLK : (m + 1) * BLK, at] += a_ref[0, q, u]

        @pl.when(flag_ref[1] == 1)
        def _():
            out_ref[:, :RP] = own_ref[...]

    def arrived(c, m):
        return pl.BlockSpec(
            (1, col_count, width, BLK, BLK),
            lambda r, s, v, p, f: (s[c * row_blocks + r * tall + m], 0, 0, 0, 0),
        )

    return pl.pallas_call(
        body,
        grid_spec=pltpu.PrefetchScalarGridSpec(
            num_scalar_prefetch=4,
            grid=(row_blocks // tall,),
            in_specs=[pl.BlockSpec((high, cols), lambda r, s, v, p, f: (r, 0))]
            + [arrived(c, m) for c in range(2) for m in range(tall) for _ in range(count)]
            + [
                pl.BlockSpec((high, RP), lambda r, s, v, p, f: (r, 0)),
                pl.BlockSpec((cols, RP), lambda r, s, v, p, f: (0, 0)),
            ],
            out_specs=pl.BlockSpec((high, cols), lambda r, s, v, p, f: (r, 0)),
            scratch_shapes=[pltpu.VMEM((cols, RP), BF16), pltpu.VMEM((cols, RP), BF16)],
        ),
        out_shape=jax.ShapeDtypeStruct((rows, cols), F32),
        compiler_params=params(),
        cost_estimate=cost(6 * rows * cols * RP, 8 * rows * cols + 4 * sum(p.size for p in parts)),
    )(
        row_slot,
        row_valid,
        jnp.concatenate(col_places, axis=1),
        flags,
        root,
        *(parts * (2 * tall)),
        own_rows,
        columns,
    )


def deliver(root, part, row_slot, row_valid, col_place):
    rows, cols = root.shape
    row_blocks = rows // BLK
    _, col_count, width, _, _ = part.shape

    def body(slot_ref, valid_ref, place_ref, root_ref, a0_ref, a1_ref, out_ref):
        r = pl.program_id(0)
        out_ref[...] = root_ref[...]
        for c, a_ref in enumerate((a0_ref, a1_ref)):

            @pl.when(valid_ref[c * row_blocks + r] == 1)
            def _():
                for q in range(col_count):
                    for u in range(width):
                        col = place_ref[c, q * width + u]

                        @pl.when(col >= 0)
                        def _():
                            at = pl.ds(pl.multiple_of(col * BLK, BLK), BLK)
                            out_ref[:, at] += a_ref[0, q, u]

    def arrived(c):
        return pl.BlockSpec(
            (1, col_count, width, BLK, BLK), lambda r, s, v, p: (s[c * row_blocks + r], 0, 0, 0, 0)
        )

    whole = pl.BlockSpec((BLK, cols), lambda r, s, v, p: (r, 0))
    return pl.pallas_call(
        body,
        grid_spec=pltpu.PrefetchScalarGridSpec(
            num_scalar_prefetch=3,
            grid=(row_blocks,),
            in_specs=[whole, arrived(0), arrived(1)],
            out_specs=whole,
        ),
        out_shape=jax.ShapeDtypeStruct((rows, cols), F32),
        compiler_params=params(),
        cost_estimate=cost(0, 8 * rows * cols + 4 * part.size),
    )(row_slot, row_valid, col_place, root, part, part)


def shards(child_update, child_panel, root_front, index_map):
    col_count = lax.axis_size("pcol")
    row_count = lax.axis_size("prow")
    group_count = 2 * col_count
    half = lax.axis_index("half")
    pcol = lax.axis_index("pcol")
    prow = lax.axis_index("prow")
    group = half * col_count + pcol
    rows_dev = child_update.shape[1]
    root_rows, root_cols = root_front.shape
    child_blocks = rows_dev // BLK
    col_blocks = child_update.shape[2] // BLK
    row_blocks = root_rows // BLK
    group_cols = root_cols // BLK
    ratio = root_cols // root_rows
    cap_col = max(1, col_blocks // group_count)
    cap_row = max(1, 2 * child_blocks // row_count)
    cap_pick = cap_row * ratio
    even = col_blocks == group_count * cap_col and 2 * child_blocks == row_count * cap_row
    halves = 2 if even and cap_pick % 2 == 0 and cap_col % 2 == 0 else 1
    half_col, half_pick = cap_col // halves, cap_pick // halves
    width = half_col // 2 if half_col % 2 == 0 else half_col
    iota = functools.partial(jnp.arange, dtype=jnp.int32)
    own_panel = child_panel[0]
    other_panel = lax.ppermute(own_panel, "half", [(0, 1), (1, 0)])

    by_col = index_map.reshape(2, col_count, col_blocks)
    by_row = index_map.reshape(2, row_count, child_blocks)
    key = by_row // group_cols
    if halves == 2:
        in_group = key[..., None] == iota(group_count)
        named = jnp.sum(in_group.astype(jnp.int32), axis=2)
        leading = jnp.sum((in_group & (by_row[..., None] < RP // BLK)).astype(jnp.int32), axis=2)
        least = jnp.maximum(jnp.maximum(half_pick - named[1], leading[0]), 0)
        most = jnp.minimum(jnp.minimum(named[0], half_pick - leading[1]), half_pick)
        least = least.reshape(col_count, row_count // col_count, group_count)
        room = most.reshape(least.shape) - least
        rest = half_col - jnp.sum(least, axis=1, keepdims=True)
        taken = least + jnp.clip(rest - (jnp.cumsum(room, axis=1) - room), 0, room)
        taken = taken.reshape(row_count, group_count)
        taken = jnp.stack([taken, half_pick - taken])
        ahead = (by_row[..., None, :] < by_row[..., :, None]) & (key[..., None, :] == key[..., :, None])
        place_in = jnp.sum(ahead.astype(jnp.int32), axis=-1)
        limit = jnp.sum(jnp.where(in_group, taken[:, :, None, :], 0), axis=-1)
        key = 2 * key + (place_in >= limit).astype(jnp.int32)

    col_key = key.reshape(2, col_count, col_blocks)
    before = (col_key[..., None, :] == col_key[..., :, None]) & (
        iota(col_blocks)[None, :] < iota(col_blocks)[:, None]
    )
    col_key = col_key * half_col + jnp.sum(before.astype(jnp.int32), axis=-1)
    own_key = lax.dynamic_index_in_dim(
        col_key.reshape(group_count, col_blocks), group, 0, keepdims=False
    )
    chosen = jnp.sum(
        jnp.where(own_key[None, :] == iota(group_count * cap_col)[:, None], iota(col_blocks), 0),
        axis=1,
    ).reshape(group_count, halves, half_col)

    joint = by_row.transpose(1, 0, 2).reshape(row_count, 2 * child_blocks)
    items = 2 * child_blocks
    earlier = iota(items)[None, :] < iota(items)[:, None]
    owner = joint // row_blocks
    row_rank = jnp.sum(
        ((owner[:, None, :] == owner[:, :, None]) & earlier).astype(jnp.int32), axis=-1
    )
    joint_key = key.transpose(1, 0, 2).reshape(row_count, items)
    pick_rank = jnp.sum(
        ((joint_key[:, None, :] == joint_key[:, :, None]) & earlier).astype(jnp.int32), axis=-1
    )
    here = lax.dynamic_index_in_dim
    own_owner = here(owner, prow, 0, keepdims=False)
    own_row_rank = here(row_rank, prow, 0, keepdims=False)
    own_pick = here(joint_key * half_pick + pick_rank, prow, 0, keepdims=False)
    pick_item = jnp.sum(
        jnp.where(own_pick[None, :] == (group * cap_pick + iota(cap_pick))[:, None], iota(items), 0),
        axis=1,
    )
    item_slot = own_owner * cap_row + own_row_rank

    code = (iota(row_count)[:, None] * half_pick + pick_rank).reshape(row_count, 2, child_blocks)
    slot_of = code.transpose(1, 0, 2).reshape(2, col_count, col_blocks)
    match = col_key[:, :, None, :] == (group * cap_col + iota(cap_col))[:, None]
    place = jnp.sum(jnp.where(match, slot_of[:, :, None, :], 0), axis=-1)
    col_local = (
        jnp.sum(jnp.where(match, by_col[:, :, None, :] - group * group_cols + 1, 0), axis=-1) - 1
    )

    row_slot = (iota(row_count)[:, None] * cap_row + row_rank).reshape(row_count, 2, child_blocks)
    row_match = by_row[..., None] == prow * row_blocks + iota(row_blocks)
    row_slot = jnp.sum(
        jnp.where(row_match, row_slot.transpose(1, 0, 2)[..., None] + 1, 0), axis=(1, 2)
    )
    row_valid = (row_slot > 0).astype(jnp.int32).reshape(-1)
    row_slot = jnp.maximum(row_slot - 1, 0).reshape(-1)

    pick_mine = (pick_item // child_blocks == half).astype(jnp.int32)
    picked = []
    for h in range(halves):
        at = slice(h * half_pick, (h + 1) * half_pick)
        picked.append(pick_rows(own_panel, other_panel, pick_item[at] % child_blocks, pick_mine[at]))

    device = lambda g, r: ((g // col_count) * row_count + r) * col_count + g % col_count
    everyone = ("half", "prow", "pcol")
    distance = (group + iota(group_count)) % group_count
    origins = (group - iota(group_count)) % group_count
    arrived = []
    packed = [pack_columns(child_update[0], chosen[distance, h]) for h in range(halves)]
    origins, picked[1:], packed[1:] = lax.optimization_barrier((origins, picked[1:], packed[1:]))
    panels = [lax.all_gather(value, "prow", axis=0, tiled=True) for value in picked]
    for h in range(halves):
        if arrived:
            packed[h], arrived[-1][col_count] = lax.optimization_barrier(
                (packed[h], arrived[-1][col_count])
            )
        got = [packed[h][0]]
        for d in range(1, group_count):
            pairs = [
                (device(g, r), device((g + d) % group_count, r))
                for g in range(group_count)
                for r in range(row_count)
            ]
            got.append(lax.ppermute(packed[h][d], everyone, pairs))
        arrived.append(got)

    spans = [(h, first) for h in range(halves) for first in range(0, half_col, width)]
    early = max(1, len(spans) // halves)
    outgoing, parts, col_places = [], [], []
    to_first = (own_owner == 0)[None, :] & (own_row_rank[None, :] == iota(cap_row)[:, None])
    own_joint = here(joint, prow, 0, keepdims=False)
    row_child = jnp.sum(jnp.where(to_first, iota(items) // child_blocks, 0), axis=1)
    row_place = jnp.sum(jnp.where(to_first, own_joint + 1, 0), axis=1) - 1
    for h, first in spans:
        at = slice(h * half_col + first, h * half_col + first + width)
        col_places.append(col_local[:, :, at].reshape(2, -1))
        if outgoing:
            origins, outgoing[-1] = lax.optimization_barrier((origins, outgoing[-1]))
        outgoing.append(
            schur_rows(
                own_panel,
                other_panel,
                arrived[h],
                panels[h],
                half,
                item_slot,
                place[:, :, at].reshape(-1),
                origins,
                row_count * cap_row,
                col_count,
                (first, width),
            )
        )
        if len(outgoing) == early:
            pivot = pivot_part(
                root_front,
                outgoing,
                row_child,
                row_place,
                col_places,
                ((prow == 0) & (group == 0)).astype(jnp.int32),
            )
            step = 1
            while step < row_count:
                pairs = [(r, r ^ step) for r in range(row_count)]
                pivot = pivot + lax.ppermute(pivot, "prow", pairs)
                step *= 2
            factor = jnp.linalg.cholesky(pivot)
            inverse = lax.linalg.triangular_solve(
                factor, jnp.eye(RP, dtype=F32), left_side=True, lower=True
            )
            origins, inverse = lax.optimization_barrier((origins, inverse))
    row_slot, outgoing[-1] = lax.optimization_barrier((row_slot, outgoing[-1]))
    for value in outgoing:
        parts.append(lax.all_to_all(value, "prow", split_axis=0, concat_axis=0, tiled=True))

    raw = first_panel(root_front, parts[:early], row_slot, row_valid, col_places[:early])
    solved = lax.dot_general(raw, inverse, NT, precision=HIGHEST, preferred_element_type=F32)
    top = jnp.where(prow == 0, factor, solved[:RP])
    solved = jnp.concatenate([top, solved[RP:]], axis=0)
    own_rows = jnp.where(group == 0, solved, 0.0)
    for g in range(1, group_count):
        pairs = [(device(0, r), device(g, r)) for r in range(row_count)]
        own_rows = own_rows + lax.ppermute(solved, everyone, pairs)
    groups_of = row_count // ratio
    shift = (prow // ratio - group) % groups_of
    tile = jnp.where(shift == 0, own_rows, 0.0)
    for k in range(1, groups_of):
        pairs = [
            (device(g, g * ratio + o), device(g, ((g + k) % groups_of) * ratio + o))
            for g in range(group_count)
            for o in range(ratio)
        ]
        got = lax.ppermute(own_rows, everyone, pairs)
        tile = jnp.where(shift == k, got, tile)
    tiles = [tile]
    for o in range(1, ratio):
        pairs = [
            (r, (r // ratio) * ratio + (r % ratio + o) % ratio) for r in range(row_count)
        ]
        tiles.append(lax.ppermute(tile, "prow", pairs))
    offset = prow % ratio
    ordered = []
    for o in range(ratio):
        value = tiles[0]
        for k in range(1, ratio):
            value = jnp.where((offset - k) % ratio == o, tiles[k], value)
        ordered.append(value)
    lower_cols = jnp.concatenate(ordered, axis=0)
    flags = jnp.stack([(prow == 0), (group == 0)]).astype(jnp.int32)
    late = max(1, len(parts) - 1)
    root = advance(
        root_front, parts[:late], own_rows, lower_cols, row_slot, row_valid, col_places[:late], flags
    )
    for part, col_place in zip(parts[late:], col_places[late:]):
        root = deliver(root, part, row_slot, row_valid, col_place)
    return root


def solution(mesh):
    return jax.shard_map(
        shards,
        mesh=mesh,
        in_specs=(
            P("half", "prow", "pcol"),
            P("half", "prow", None),
            P("prow", ("half", "pcol")),
            P(),
        ),
        out_specs=P("prow", ("half", "pcol")),
        check_vma=False,
    )
```

```python
import functools

import jax
import jax.numpy as jnp
from jax import lax
from jax.experimental import pallas as pl
from jax.experimental.pallas import tpu as pltpu
from jax.sharding import PartitionSpec as P

BLK = 128
RP = 256
F32 = jnp.float32
BF16 = jnp.bfloat16
HIGHEST = lax.Precision.HIGHEST
NT = (((1,), (1,)), ((), ()))
VMEM_LIMIT = 56 * 1024 * 1024


def split(x):
    hi = x.astype(BF16)
    lo = (x - hi.astype(F32)).astype(BF16)
    return hi, lo


def dot_nt(a, b):
    return lax.dot_general(a, b, NT, preferred_element_type=F32)


def params():
    return pltpu.CompilerParams(vmem_limit_bytes=VMEM_LIMIT)


def cost(flops, nbytes):
    return pl.CostEstimate(flops=int(flops), bytes_accessed=int(nbytes), transcendentals=0)


def pack_columns(update, chosen):
    rows = update.shape[0]
    groups, width = chosen.shape

    def body(chosen_ref, *refs):
        for d in range(groups):
            refs[groups + d][0] = refs[d][...]

    def source(d):
        return pl.BlockSpec((rows, BLK), lambda u, s: (0, s[d * width + u]))

    return pl.pallas_call(
        body,
        grid_spec=pltpu.PrefetchScalarGridSpec(
            num_scalar_prefetch=1,
            grid=(width,),
            in_specs=[source(d) for d in range(groups)],
            out_specs=[pl.BlockSpec((1, rows, BLK), lambda u, s: (u, 0, 0))] * groups,
        ),
        out_shape=[jax.ShapeDtypeStruct((width, rows, BLK), F32)] * groups,
        compiler_params=params(),
        cost_estimate=cost(0, 8 * groups * width * rows * BLK),
    )(chosen.reshape(-1), *([update] * groups))


def pick_rows(own, other, block, mine):
    count = block.shape[0]
    depth = own.shape[1]

    def body(block_ref, mine_ref, own_ref, other_ref, out_ref):
        s = pl.program_id(0)

        @pl.when(mine_ref[s] == 1)
        def _():
            out_ref[0] = own_ref[...]

        @pl.when(mine_ref[s] == 0)
        def _():
            out_ref[0] = other_ref[...]

    spec = pl.BlockSpec((BLK, depth), lambda s, b, m: (b[s], 0))
    return pl.pallas_call(
        body,
        grid_spec=pltpu.PrefetchScalarGridSpec(
            num_scalar_prefetch=2,
            grid=(count,),
            in_specs=[spec, spec],
            out_specs=pl.BlockSpec((1, BLK, depth), lambda s, b, m: (s, 0, 0)),
        ),
        out_shape=jax.ShapeDtypeStruct((count, BLK, depth), F32),
        compiler_params=params(),
        cost_estimate=cost(0, 12 * count * BLK * depth),
    )(block, mine, own, other)


def schur_rows(own, other, arrived, panels, half, item_slot, places, origins, slots, col_count, span):
    groups = len(arrived)
    depth = own.shape[1]
    first, width = span
    rows = arrived[0].shape[1]
    child_blocks = rows // BLK
    tall = 2 if child_blocks % 2 == 0 else 1
    steps = child_blocks // tall
    per_child = col_count * width
    wide = per_child * BLK
    piece = next(w for w in (512, 384, 256, 128) if wide % w == 0)

    def body(half_ref, slot_ref, place_ref, origin_ref, own_ref, other_ref, *rest):
        in_refs = rest[:groups]
        panel_ref, out_ref, staged, hi_ref, lo_ref, total_ref, result, load_sem, store_sem = rest[groups:]
        c = pl.program_id(0)
        step = c * steps + pl.program_id(1)

        @pl.when(step == 0)
        def _():
            @pl.loop(0, 2 * per_child)
            def _(k):
                pltpu.make_async_copy(panel_ref.at[place_ref[k]], staged.at[k], load_sem.at[k]).start()

            @pl.loop(0, 2 * per_child)
            def _(k):
                pltpu.make_async_copy(panel_ref.at[place_ref[k]], staged.at[k], load_sem.at[k]).wait()
                hi, lo = split(staged[k])
                hi_ref[k] = hi
                lo_ref[k] = lo

        a_hi, a_lo = split(jnp.where(c == half_ref[0], own_ref[...], other_ref[...]))
        stacked = jnp.concatenate([a_hi, a_lo], axis=0)
        high = tall * BLK
        at_once = piece // BLK
        for n in range(0, per_child, at_once):
            at = pl.ds(c * per_child + n, at_once)
            both = dot_nt(stacked, hi_ref[at].reshape(piece, depth))
            total = both[:high] + both[high:] + dot_nt(a_hi, lo_ref[at].reshape(piece, depth))
            for k in range(at_once):
                total_ref[n + k] = total[:, k * BLK : (k + 1) * BLK]

        buffer = step % 2

        def store(m, at_step):
            item = at_step * tall + m
            return pltpu.make_async_copy(
                result.at[at_step % 2, m], out_ref.at[slot_ref[item]], store_sem.at[at_step % 2, m]
            )

        @pl.when(step >= 2)
        def _():
            for m in range(tall):
                store(m, step - 2).wait()

        for d in range(groups):

            @pl.when(origin_ref[d] // col_count == c)
            def _():
                q = origin_ref[d] % col_count
                for u in range(width):
                    for m in range(tall):
                        at = slice(m * BLK, (m + 1) * BLK)
                        result[buffer, m, q, u] = in_refs[d][u, at, :] - total_ref[q * width + u, at, :]

        for m in range(tall):
            store(m, step).start()

        @pl.when(step == 2 * steps - 1)
        def _():
            for m in range(tall):
                if steps > 0:
                    store(m, step - 1).wait()
                store(m, step).wait()

    def stay(c, i, mine):
        return jnp.where(c == mine, i, jnp.where(c < mine, 0, steps - 1))

    def arrival(d):
        return pl.BlockSpec(
            (width, tall * BLK, BLK),
            lambda c, i, h, t, p, o: (first // width, stay(c, i, o[d] // col_count), 0),
        )

    return pl.pallas_call(
        body,
        grid_spec=pltpu.PrefetchScalarGridSpec(
            num_scalar_prefetch=4,
            grid=(2, steps),
            in_specs=[
                pl.BlockSpec((tall * BLK, depth), lambda c, i, h, t, p, o: (stay(c, i, h[0]), 0)),
                pl.BlockSpec((tall * BLK, depth), lambda c, i, h, t, p, o: (stay(c, i, 1 - h[0]), 0)),
            ]
            + [arrival(d) for d in range(groups)]
            + [pl.BlockSpec(memory_space=pl.ANY)],
            out_specs=pl.BlockSpec(memory_space=pl.ANY),
            scratch_shapes=[
                pltpu.VMEM((2 * per_child, BLK, depth), F32),
                pltpu.VMEM((2 * per_child, BLK, depth), BF16),
                pltpu.VMEM((2 * per_child, BLK, depth), BF16),
                pltpu.VMEM((per_child, tall * BLK, BLK), F32),
                pltpu.VMEM((2, tall, col_count, width, BLK, BLK), F32),
                pltpu.SemaphoreType.DMA((2 * per_child,)),
                pltpu.SemaphoreType.DMA((2, tall)),
            ],
        ),
        out_shape=jax.ShapeDtypeStruct((slots, col_count, width, BLK, BLK), F32),
        compiler_params=params(),
        cost_estimate=cost(
            12 * rows * wide * depth, 8 * rows * (depth + 2 * wide) + 8 * wide * depth
        ),
    )(half.reshape(1), item_slot, places, origins, own, other, *arrived, panels)


def first_panel(root, parts, row_slot, row_valid, col_places):
    row_blocks = root.shape[0] // BLK
    count = len(parts)
    _, col_count, width, _, _ = parts[0].shape

    def body(slot_ref, valid_ref, place_ref, root_ref, *rest):
        a_refs, out_ref = rest[:-1], rest[-1]
        r = pl.program_id(0)
        out_ref[...] = root_ref[...]
        for c in range(2):
            for k in range(count * col_count * width):
                j, q, u = k // (col_count * width), k // width % col_count, k % width
                col = place_ref[c, k]
                ok = (valid_ref[c * row_blocks + r] == 1) & (col >= 0) & (col < RP // BLK)

                @pl.when(ok)
                def _():
                    at = pl.ds(pl.multiple_of(col * BLK, BLK), BLK)
                    out_ref[:, at] += a_refs[c * count + j][0, q, u]

    def arrived(c):
        return pl.BlockSpec(
            (1, col_count, width, BLK, BLK), lambda r, s, v, p: (s[c * row_blocks + r], 0, 0, 0, 0)
        )

    panel = pl.BlockSpec((BLK, RP), lambda r, s, v, p: (r, 0))
    return pl.pallas_call(
        body,
        grid_spec=pltpu.PrefetchScalarGridSpec(
            num_scalar_prefetch=3,
            grid=(row_blocks,),
            in_specs=[panel] + [arrived(0)] * count + [arrived(1)] * count,
            out_specs=panel,
        ),
        out_shape=jax.ShapeDtypeStruct((root.shape[0], RP), F32),
        compiler_params=params(),
        cost_estimate=cost(0, 8 * root.shape[0] * RP + 4 * sum(p.size for p in parts)),
    )(row_slot, row_valid, jnp.concatenate(col_places, axis=1), root, *parts, *parts)


def pivot_part(root, outgoing, row_child, row_place, col_places, flag):
    count = len(outgoing)
    cap_row = row_child.shape[0]
    _, col_count, width, _, _ = outgoing[0].shape

    def body(child_ref, row_ref, place_ref, flag_ref, root_ref, *rest):
        a_refs, out_ref = rest[:-1], rest[-1]
        out_ref[...] = jnp.where(flag_ref[0] == 1, root_ref[...], 0.0)
        for w in range(cap_row):
            row = row_ref[w]
            for k in range(count * col_count * width):
                j, q, u = k // (col_count * width), k // width % col_count, k % width
                col = place_ref[child_ref[w], k]

                @pl.when((row >= 0) & (row < RP // BLK) & (col >= 0) & (col < RP // BLK))
                def _():
                    at_row = pl.ds(pl.multiple_of(row * BLK, BLK), BLK)
                    at_col = pl.ds(pl.multiple_of(col * BLK, BLK), BLK)
                    out_ref[at_row, at_col] += a_refs[j][w, q, u]

    corner = pl.BlockSpec((RP, RP), lambda i, c, r, p, f: (0, 0))
    leading = pl.BlockSpec((cap_row, col_count, width, BLK, BLK), lambda i, c, r, p, f: (0,) * 5)
    return pl.pallas_call(
        body,
        grid_spec=pltpu.PrefetchScalarGridSpec(
            num_scalar_prefetch=4,
            grid=(1,),
            in_specs=[corner] + [leading] * count,
            out_specs=corner,
        ),
        out_shape=jax.ShapeDtypeStruct((RP, RP), F32),
        compiler_params=params(),
        cost_estimate=cost(0, 8 * RP * RP + 4 * count * cap_row * col_count * width * BLK * BLK),
    )(row_child, row_place, jnp.concatenate(col_places, axis=1), flag.reshape(1), root, *outgoing)


def advance(root, parts, own_rows, columns, row_slot, row_valid, col_places, flags):
    rows, cols = root.shape
    row_blocks = rows // BLK
    count = len(parts)
    _, col_count, width, _, _ = parts[0].shape
    step = next(w for w in (512, 384, 256) if cols % w == 0)
    tall = 2 if row_blocks % 2 == 0 else 1
    high = tall * BLK

    def body(slot_ref, valid_ref, place_ref, flag_ref, root_ref, *rest):
        a_refs = rest[: 2 * tall * count]
        own_ref, col_ref, out_ref, hi_ref, lo_ref = rest[2 * tall * count :]
        r = pl.program_id(0)

        @pl.when(r == 0)
        def _():
            hi, lo = split(col_ref[...])
            hi_ref[...] = hi
            lo_ref[...] = lo

        pivot_rows = (flag_ref[0] == 1) & (r * high < RP)

        @pl.when(pivot_rows)
        def _():
            out_ref[...] = root_ref[...]

        @pl.when(jnp.logical_not(pivot_rows))
        def _():
            a_hi, a_lo = split(own_ref[...])
            stacked = jnp.concatenate([a_hi, a_lo], axis=0)
            for n in range(0, cols, step):
                both = dot_nt(stacked, hi_ref[n : n + step, :])
                total = both[:high] + both[high:] + dot_nt(a_hi, lo_ref[n : n + step, :])
                out_ref[:, n : n + step] = root_ref[:, n : n + step] - total

        for c in range(2):
            for m in range(tall):

                @pl.when(valid_ref[c * row_blocks + r * tall + m] == 1)
                def _():
                    for j in range(count):
                        for q in range(col_count):
                            for u in range(width):
                                col = place_ref[c, (j * col_count + q) * width + u]
                                a_ref = a_refs[(c * tall + m) * count + j]

                                @pl.when(col >= 0)
                                def _():
                                    at = pl.ds(pl.multiple_of(col * BLK, BLK), BLK)
                                    out_ref[m * BLK : (m + 1) * BLK, at] += a_ref[0, q, u]

        @pl.when(flag_ref[1] == 1)
        def _():
            out_ref[:, :RP] = own_ref[...]

    def arrived(c, m):
        return pl.BlockSpec(
            (1, col_count, width, BLK, BLK),
            lambda r, s, v, p, f: (s[c * row_blocks + r * tall + m], 0, 0, 0, 0),
        )

    return pl.pallas_call(
        body,
        grid_spec=pltpu.PrefetchScalarGridSpec(
            num_scalar_prefetch=4,
            grid=(row_blocks // tall,),
            in_specs=[pl.BlockSpec((high, cols), lambda r, s, v, p, f: (r, 0))]
            + [arrived(c, m) for c in range(2) for m in range(tall) for _ in range(count)]
            + [
                pl.BlockSpec((high, RP), lambda r, s, v, p, f: (r, 0)),
                pl.BlockSpec((cols, RP), lambda r, s, v, p, f: (0, 0)),
            ],
            out_specs=pl.BlockSpec((high, cols), lambda r, s, v, p, f: (r, 0)),
            scratch_shapes=[pltpu.VMEM((cols, RP), BF16), pltpu.VMEM((cols, RP), BF16)],
        ),
        out_shape=jax.ShapeDtypeStruct((rows, cols), F32),
        compiler_params=params(),
        cost_estimate=cost(6 * rows * cols * RP, 8 * rows * cols + 4 * sum(p.size for p in parts)),
    )(
        row_slot,
        row_valid,
        jnp.concatenate(col_places, axis=1),
        flags,
        root,
        *(parts * (2 * tall)),
        own_rows,
        columns,
    )


def deliver(root, part, row_slot, row_valid, col_place):
    rows, cols = root.shape
    row_blocks = rows // BLK
    _, col_count, width, _, _ = part.shape

    def body(slot_ref, valid_ref, place_ref, root_ref, a0_ref, a1_ref, out_ref):
        r = pl.program_id(0)
        out_ref[...] = root_ref[...]
        for c, a_ref in enumerate((a0_ref, a1_ref)):

            @pl.when(valid_ref[c * row_blocks + r] == 1)
            def _():
                for q in range(col_count):
                    for u in range(width):
                        col = place_ref[c, q * width + u]

                        @pl.when(col >= 0)
                        def _():
                            at = pl.ds(pl.multiple_of(col * BLK, BLK), BLK)
                            out_ref[:, at] += a_ref[0, q, u]

    def arrived(c):
        return pl.BlockSpec(
            (1, col_count, width, BLK, BLK), lambda r, s, v, p: (s[c * row_blocks + r], 0, 0, 0, 0)
        )

    whole = pl.BlockSpec((BLK, cols), lambda r, s, v, p: (r, 0))
    return pl.pallas_call(
        body,
        grid_spec=pltpu.PrefetchScalarGridSpec(
            num_scalar_prefetch=3,
            grid=(row_blocks,),
            in_specs=[whole, arrived(0), arrived(1)],
            out_specs=whole,
        ),
        out_shape=jax.ShapeDtypeStruct((rows, cols), F32),
        compiler_params=params(),
        cost_estimate=cost(0, 8 * rows * cols + 4 * part.size),
    )(row_slot, row_valid, col_place, root, part, part)


def shards(child_update, child_panel, root_front, index_map):
    col_count = lax.axis_size("pcol")
    row_count = lax.axis_size("prow")
    group_count = 2 * col_count
    half = lax.axis_index("half")
    pcol = lax.axis_index("pcol")
    prow = lax.axis_index("prow")
    group = half * col_count + pcol
    rows_dev = child_update.shape[1]
    root_rows, root_cols = root_front.shape
    child_blocks = rows_dev // BLK
    col_blocks = child_update.shape[2] // BLK
    row_blocks = root_rows // BLK
    group_cols = root_cols // BLK
    ratio = root_cols // root_rows
    cap_col = max(1, col_blocks // group_count)
    cap_row = max(1, 2 * child_blocks // row_count)
    cap_pick = cap_row * ratio
    even = col_blocks == group_count * cap_col and 2 * child_blocks == row_count * cap_row
    halves = 2 if even and cap_pick % 2 == 0 and cap_col % 2 == 0 else 1
    half_col, half_pick = cap_col // halves, cap_pick // halves
    width = half_col // 2 if half_col % 2 == 0 else half_col
    iota = functools.partial(jnp.arange, dtype=jnp.int32)
    own_panel = child_panel[0]
    other_panel = lax.ppermute(own_panel, "half", [(0, 1), (1, 0)])

    by_col = index_map.reshape(2, col_count, col_blocks)
    by_row = index_map.reshape(2, row_count, child_blocks)
    key = by_row // group_cols
    if halves == 2:
        in_group = key[..., None] == iota(group_count)
        named = jnp.sum(in_group.astype(jnp.int32), axis=2)
        leading = jnp.sum((in_group & (by_row[..., None] < RP // BLK)).astype(jnp.int32), axis=2)
        least = jnp.maximum(jnp.maximum(half_pick - named[1], leading[0]), 0)
        most = jnp.minimum(jnp.minimum(named[0], half_pick - leading[1]), half_pick)
        least = least.reshape(col_count, row_count // col_count, group_count)
        room = most.reshape(least.shape) - least
        rest = half_col - jnp.sum(least, axis=1, keepdims=True)
        taken = least + jnp.clip(rest - (jnp.cumsum(room, axis=1) - room), 0, room)
        taken = taken.reshape(row_count, group_count)
        taken = jnp.stack([taken, half_pick - taken])
        ahead = (by_row[..., None, :] < by_row[..., :, None]) & (key[..., None, :] == key[..., :, None])
        place_in = jnp.sum(ahead.astype(jnp.int32), axis=-1)
        limit = jnp.sum(jnp.where(in_group, taken[:, :, None, :], 0), axis=-1)
        key = 2 * key + (place_in >= limit).astype(jnp.int32)

    col_key = key.reshape(2, col_count, col_blocks)
    before = (col_key[..., None, :] == col_key[..., :, None]) & (
        iota(col_blocks)[None, :] < iota(col_blocks)[:, None]
    )
    col_key = col_key * half_col + jnp.sum(before.astype(jnp.int32), axis=-1)
    own_key = lax.dynamic_index_in_dim(
        col_key.reshape(group_count, col_blocks), group, 0, keepdims=False
    )
    chosen = jnp.sum(
        jnp.where(own_key[None, :] == iota(group_count * cap_col)[:, None], iota(col_blocks), 0),
        axis=1,
    ).reshape(group_count, halves, half_col)

    joint = by_row.transpose(1, 0, 2).reshape(row_count, 2 * child_blocks)
    items = 2 * child_blocks
    earlier = iota(items)[None, :] < iota(items)[:, None]
    owner = joint // row_blocks
    row_rank = jnp.sum(
        ((owner[:, None, :] == owner[:, :, None]) & earlier).astype(jnp.int32), axis=-1
    )
    joint_key = key.transpose(1, 0, 2).reshape(row_count, items)
    pick_rank = jnp.sum(
        ((joint_key[:, None, :] == joint_key[:, :, None]) & earlier).astype(jnp.int32), axis=-1
    )
    here = lax.dynamic_index_in_dim
    own_owner = here(owner, prow, 0, keepdims=False)
    own_row_rank = here(row_rank, prow, 0, keepdims=False)
    own_pick = here(joint_key * half_pick + pick_rank, prow, 0, keepdims=False)
    pick_item = jnp.sum(
        jnp.where(own_pick[None, :] == (group * cap_pick + iota(cap_pick))[:, None], iota(items), 0),
        axis=1,
    )
    item_slot = own_owner * cap_row + own_row_rank

    code = (iota(row_count)[:, None] * half_pick + pick_rank).reshape(row_count, 2, child_blocks)
    slot_of = code.transpose(1, 0, 2).reshape(2, col_count, col_blocks)
    match = col_key[:, :, None, :] == (group * cap_col + iota(cap_col))[:, None]
    place = jnp.sum(jnp.where(match, slot_of[:, :, None, :], 0), axis=-1)
    col_local = (
        jnp.sum(jnp.where(match, by_col[:, :, None, :] - group * group_cols + 1, 0), axis=-1) - 1
    )

    row_slot = (iota(row_count)[:, None] * cap_row + row_rank).reshape(row_count, 2, child_blocks)
    row_match = by_row[..., None] == prow * row_blocks + iota(row_blocks)
    row_slot = jnp.sum(
        jnp.where(row_match, row_slot.transpose(1, 0, 2)[..., None] + 1, 0), axis=(1, 2)
    )
    row_valid = (row_slot > 0).astype(jnp.int32).reshape(-1)
    row_slot = jnp.maximum(row_slot - 1, 0).reshape(-1)

    pick_mine = (pick_item // child_blocks == half).astype(jnp.int32)
    picked = []
    for h in range(halves):
        at = slice(h * half_pick, (h + 1) * half_pick)
        picked.append(pick_rows(own_panel, other_panel, pick_item[at] % child_blocks, pick_mine[at]))

    device = lambda g, r: ((g // col_count) * row_count + r) * col_count + g % col_count
    everyone = ("half", "prow", "pcol")
    distance = (group + iota(group_count)) % group_count
    origins = (group - iota(group_count)) % group_count
    arrived = []
    packed = [pack_columns(child_update[0], chosen[distance, h]) for h in range(halves)]
    origins, picked[1:], packed[1:] = lax.optimization_barrier((origins, picked[1:], packed[1:]))
    panels = [lax.all_gather(value, "prow", axis=0, tiled=True) for value in picked]
    for h in range(halves):
        if arrived:
            packed[h], arrived[-1][col_count] = lax.optimization_barrier(
                (packed[h], arrived[-1][col_count])
            )
        got = [packed[h][0]]
        for d in range(1, group_count):
            pairs = [
                (device(g, r), device((g + d) % group_count, r))
                for g in range(group_count)
                for r in range(row_count)
            ]
            got.append(lax.ppermute(packed[h][d], everyone, pairs))
        arrived.append(got)

    spans = [(h, first) for h in range(halves) for first in range(0, half_col, width)]
    early = max(1, len(spans) // halves)
    outgoing, parts, col_places = [], [], []
    to_first = (own_owner == 0)[None, :] & (own_row_rank[None, :] == iota(cap_row)[:, None])
    own_joint = here(joint, prow, 0, keepdims=False)
    row_child = jnp.sum(jnp.where(to_first, iota(items) // child_blocks, 0), axis=1)
    row_place = jnp.sum(jnp.where(to_first, own_joint + 1, 0), axis=1) - 1
    for h, first in spans:
        at = slice(h * half_col + first, h * half_col + first + width)
        col_places.append(col_local[:, :, at].reshape(2, -1))
        if len(outgoing) == 1:
            origins, outgoing[0], arrived = lax.optimization_barrier((origins, outgoing[0], arrived))
        elif outgoing:
            origins, outgoing[-1] = lax.optimization_barrier((origins, outgoing[-1]))
        outgoing.append(
            schur_rows(
                own_panel,
                other_panel,
                arrived[h],
                panels[h],
                half,
                item_slot,
                place[:, :, at].reshape(-1),
                origins,
                row_count * cap_row,
                col_count,
                (first, width),
            )
        )
        if len(outgoing) == early:
            pivot = pivot_part(
                root_front,
                outgoing,
                row_child,
                row_place,
                col_places,
                ((prow == 0) & (group == 0)).astype(jnp.int32),
            )
            step = 1
            while step < row_count:
                pairs = [(r, r ^ step) for r in range(row_count)]
                pivot = pivot + lax.ppermute(pivot, "prow", pairs)
                step *= 2
            origins, pivot = lax.optimization_barrier((origins, pivot))
        elif len(outgoing) == early + 1:
            pivot, outgoing[-1] = lax.optimization_barrier((pivot, outgoing[-1]))
    factor = jnp.linalg.cholesky(pivot)
    inverse = lax.linalg.triangular_solve(
        factor, jnp.eye(RP, dtype=F32), left_side=True, lower=True
    )
    for value in outgoing:
        parts.append(lax.all_to_all(value, "prow", split_axis=0, concat_axis=0, tiled=True))

    raw = first_panel(root_front, parts[:early], row_slot, row_valid, col_places[:early])
    solved = lax.dot_general(raw, inverse, NT, precision=HIGHEST, preferred_element_type=F32)
    top = jnp.where(prow == 0, factor, solved[:RP])
    solved = jnp.concatenate([top, solved[RP:]], axis=0)
    own_rows = jnp.where(group == 0, solved, 0.0)
    for g in range(1, group_count):
        pairs = [(device(0, r), device(g, r)) for r in range(row_count)]
        own_rows = own_rows + lax.ppermute(solved, everyone, pairs)
    groups_of = row_count // ratio
    shift = (prow // ratio - group) % groups_of
    tile = jnp.where(shift == 0, own_rows, 0.0)
    for k in range(1, groups_of):
        pairs = [
            (device(g, g * ratio + o), device(g, ((g + k) % groups_of) * ratio + o))
            for g in range(group_count)
            for o in range(ratio)
        ]
        got = lax.ppermute(own_rows, everyone, pairs)
        tile = jnp.where(shift == k, got, tile)
    tiles = [tile]
    for o in range(1, ratio):
        pairs = [
            (r, (r // ratio) * ratio + (r % ratio + o) % ratio) for r in range(row_count)
        ]
        tiles.append(lax.ppermute(tile, "prow", pairs))
    offset = prow % ratio
    ordered = []
    for o in range(ratio):
        value = tiles[0]
        for k in range(1, ratio):
            value = jnp.where((offset - k) % ratio == o, tiles[k], value)
        ordered.append(value)
    lower_cols = jnp.concatenate(ordered, axis=0)
    flags = jnp.stack([(prow == 0), (group == 0)]).astype(jnp.int32)
    late = max(1, len(parts) - 1)
    root = advance(
        root_front, parts[:late], own_rows, lower_cols, row_slot, row_valid, col_places[:late], flags
    )
    for part, col_place in zip(parts[late:], col_places[late:]):
        root = deliver(root, part, row_slot, row_valid, col_place)
    return root


def solution(mesh):
    return jax.shard_map(
        shards,
        mesh=mesh,
        in_specs=(
            P("half", "prow", "pcol"),
            P("half", "prow", None),
            P("prow", ("half", "pcol")),
            P(),
        ),
        out_specs=P("prow", ("half", "pcol")),
        check_vma=False,
    )
```

```python
import functools

import jax
import jax.numpy as jnp
from jax import lax
from jax.experimental import pallas as pl
from jax.experimental.pallas import tpu as pltpu
from jax.sharding import PartitionSpec as P

BLK = 128
RP = 256
F32 = jnp.float32
BF16 = jnp.bfloat16
HIGHEST = lax.Precision.HIGHEST
NT = (((1,), (1,)), ((), ()))
VMEM_LIMIT = 56 * 1024 * 1024


def split(x):
    hi = x.astype(BF16)
    lo = (x - hi.astype(F32)).astype(BF16)
    return hi, lo


def dot_nt(a, b):
    return lax.dot_general(a, b, NT, preferred_element_type=F32)


def params():
    return pltpu.CompilerParams(vmem_limit_bytes=VMEM_LIMIT)


def cost(flops, nbytes):
    return pl.CostEstimate(flops=int(flops), bytes_accessed=int(nbytes), transcendentals=0)


def pack_columns(update, chosen):
    rows = update.shape[0]
    groups, width = chosen.shape

    def body(chosen_ref, *refs):
        for d in range(groups):
            refs[groups + d][0] = refs[d][...]

    def source(d):
        return pl.BlockSpec((rows, BLK), lambda u, s: (0, s[d * width + u]))

    return pl.pallas_call(
        body,
        grid_spec=pltpu.PrefetchScalarGridSpec(
            num_scalar_prefetch=1,
            grid=(width,),
            in_specs=[source(d) for d in range(groups)],
            out_specs=[pl.BlockSpec((1, rows, BLK), lambda u, s: (u, 0, 0))] * groups,
        ),
        out_shape=[jax.ShapeDtypeStruct((width, rows, BLK), F32)] * groups,
        compiler_params=params(),
        cost_estimate=cost(0, 8 * groups * width * rows * BLK),
    )(chosen.reshape(-1), *([update] * groups))


def pick_rows(own, other, block, mine):
    count = block.shape[0]
    depth = own.shape[1]

    def body(block_ref, mine_ref, own_ref, other_ref, out_ref):
        s = pl.program_id(0)

        @pl.when(mine_ref[s] == 1)
        def _():
            out_ref[0] = own_ref[...]

        @pl.when(mine_ref[s] == 0)
        def _():
            out_ref[0] = other_ref[...]

    spec = pl.BlockSpec((BLK, depth), lambda s, b, m: (b[s], 0))
    return pl.pallas_call(
        body,
        grid_spec=pltpu.PrefetchScalarGridSpec(
            num_scalar_prefetch=2,
            grid=(count,),
            in_specs=[spec, spec],
            out_specs=pl.BlockSpec((1, BLK, depth), lambda s, b, m: (s, 0, 0)),
        ),
        out_shape=jax.ShapeDtypeStruct((count, BLK, depth), F32),
        compiler_params=params(),
        cost_estimate=cost(0, 12 * count * BLK * depth),
    )(block, mine, own, other)


def schur_rows(own, other, arrived, panels, half, item_slot, places, origins, slots, col_count, span):
    groups = len(arrived)
    depth = own.shape[1]
    first, width = span
    rows = arrived[0].shape[1]
    child_blocks = rows // BLK
    tall = 2 if child_blocks % 2 == 0 else 1
    steps = child_blocks // tall
    per_child = col_count * width
    wide = per_child * BLK
    piece = next(w for w in (512, 384, 256, 128) if wide % w == 0)

    def body(half_ref, slot_ref, place_ref, origin_ref, own_ref, other_ref, *rest):
        in_refs = rest[:groups]
        panel_ref, out_ref, staged, hi_ref, lo_ref, total_ref, result, load_sem, store_sem = rest[groups:]
        c = pl.program_id(0)
        step = c * steps + pl.program_id(1)

        @pl.when(step == 0)
        def _():
            @pl.loop(0, 2 * per_child)
            def _(k):
                pltpu.make_async_copy(panel_ref.at[place_ref[k]], staged.at[k], load_sem.at[k]).start()

            @pl.loop(0, 2 * per_child)
            def _(k):
                pltpu.make_async_copy(panel_ref.at[place_ref[k]], staged.at[k], load_sem.at[k]).wait()
                hi, lo = split(staged[k])
                hi_ref[k] = hi
                lo_ref[k] = lo

        a_hi, a_lo = split(jnp.where(c == half_ref[0], own_ref[...], other_ref[...]))
        stacked = jnp.concatenate([a_hi, a_lo], axis=0)
        high = tall * BLK
        at_once = piece // BLK
        for n in range(0, per_child, at_once):
            at = pl.ds(c * per_child + n, at_once)
            both = dot_nt(stacked, hi_ref[at].reshape(piece, depth))
            total = both[:high] + both[high:] + dot_nt(a_hi, lo_ref[at].reshape(piece, depth))
            for k in range(at_once):
                total_ref[n + k] = total[:, k * BLK : (k + 1) * BLK]

        buffer = step % 2

        def store(m, at_step):
            item = at_step * tall + m
            return pltpu.make_async_copy(
                result.at[at_step % 2, m], out_ref.at[slot_ref[item]], store_sem.at[at_step % 2, m]
            )

        @pl.when(step >= 2)
        def _():
            for m in range(tall):
                store(m, step - 2).wait()

        for d in range(groups):

            @pl.when(origin_ref[d] // col_count == c)
            def _():
                q = origin_ref[d] % col_count
                for u in range(width):
                    for m in range(tall):
                        at = slice(m * BLK, (m + 1) * BLK)
                        result[buffer, m, q, u] = in_refs[d][u, at, :] - total_ref[q * width + u, at, :]

        for m in range(tall):
            store(m, step).start()

        @pl.when(step == 2 * steps - 1)
        def _():
            for m in range(tall):
                if steps > 0:
                    store(m, step - 1).wait()
                store(m, step).wait()

    def stay(c, i, mine):
        return jnp.where(c == mine, i, jnp.where(c < mine, 0, steps - 1))

    def arrival(d):
        return pl.BlockSpec(
            (width, tall * BLK, BLK),
            lambda c, i, h, t, p, o: (first // width, stay(c, i, o[d] // col_count), 0),
        )

    return pl.pallas_call(
        body,
        grid_spec=pltpu.PrefetchScalarGridSpec(
            num_scalar_prefetch=4,
            grid=(2, steps),
            in_specs=[
                pl.BlockSpec((tall * BLK, depth), lambda c, i, h, t, p, o: (stay(c, i, h[0]), 0)),
                pl.BlockSpec((tall * BLK, depth), lambda c, i, h, t, p, o: (stay(c, i, 1 - h[0]), 0)),
            ]
            + [arrival(d) for d in range(groups)]
            + [pl.BlockSpec(memory_space=pl.ANY)],
            out_specs=pl.BlockSpec(memory_space=pl.ANY),
            scratch_shapes=[
                pltpu.VMEM((2 * per_child, BLK, depth), F32),
                pltpu.VMEM((2 * per_child, BLK, depth), BF16),
                pltpu.VMEM((2 * per_child, BLK, depth), BF16),
                pltpu.VMEM((per_child, tall * BLK, BLK), F32),
                pltpu.VMEM((2, tall, col_count, width, BLK, BLK), F32),
                pltpu.SemaphoreType.DMA((2 * per_child,)),
                pltpu.SemaphoreType.DMA((2, tall)),
            ],
        ),
        out_shape=jax.ShapeDtypeStruct((slots, col_count, width, BLK, BLK), F32),
        compiler_params=params(),
        cost_estimate=cost(
            12 * rows * wide * depth, 8 * rows * (depth + 2 * wide) + 8 * wide * depth
        ),
    )(half.reshape(1), item_slot, places, origins, own, other, *arrived, panels)


def first_panel(root, parts, row_slot, row_valid, col_places):
    row_blocks = root.shape[0] // BLK
    count = len(parts)
    _, col_count, width, _, _ = parts[0].shape

    def body(slot_ref, valid_ref, place_ref, root_ref, *rest):
        a_refs, out_ref = rest[:-1], rest[-1]
        r = pl.program_id(0)
        out_ref[...] = root_ref[...]
        for c in range(2):
            for k in range(count * col_count * width):
                j, q, u = k // (col_count * width), k // width % col_count, k % width
                col = place_ref[c, k]
                ok = (valid_ref[c * row_blocks + r] == 1) & (col >= 0) & (col < RP // BLK)

                @pl.when(ok)
                def _():
                    at = pl.ds(pl.multiple_of(col * BLK, BLK), BLK)
                    out_ref[:, at] += a_refs[c * count + j][0, q, u]

    def arrived(c):
        return pl.BlockSpec(
            (1, col_count, width, BLK, BLK), lambda r, s, v, p: (s[c * row_blocks + r], 0, 0, 0, 0)
        )

    panel = pl.BlockSpec((BLK, RP), lambda r, s, v, p: (r, 0))
    return pl.pallas_call(
        body,
        grid_spec=pltpu.PrefetchScalarGridSpec(
            num_scalar_prefetch=3,
            grid=(row_blocks,),
            in_specs=[panel] + [arrived(0)] * count + [arrived(1)] * count,
            out_specs=panel,
        ),
        out_shape=jax.ShapeDtypeStruct((root.shape[0], RP), F32),
        compiler_params=params(),
        cost_estimate=cost(0, 8 * root.shape[0] * RP + 4 * sum(p.size for p in parts)),
    )(row_slot, row_valid, jnp.concatenate(col_places, axis=1), root, *parts, *parts)


def pivot_part(root, outgoing, row_child, row_place, col_places, flag):
    count = len(outgoing)
    cap_row = row_child.shape[0]
    _, col_count, width, _, _ = outgoing[0].shape

    def body(child_ref, row_ref, place_ref, flag_ref, root_ref, *rest):
        a_refs, out_ref = rest[:-1], rest[-1]
        out_ref[...] = jnp.where(flag_ref[0] == 1, root_ref[...], 0.0)
        for w in range(cap_row):
            row = row_ref[w]
            for k in range(count * col_count * width):
                j, q, u = k // (col_count * width), k // width % col_count, k % width
                col = place_ref[child_ref[w], k]

                @pl.when((row >= 0) & (row < RP // BLK) & (col >= 0) & (col < RP // BLK))
                def _():
                    at_row = pl.ds(pl.multiple_of(row * BLK, BLK), BLK)
                    at_col = pl.ds(pl.multiple_of(col * BLK, BLK), BLK)
                    out_ref[at_row, at_col] += a_refs[j][w, q, u]

    corner = pl.BlockSpec((RP, RP), lambda i, c, r, p, f: (0, 0))
    leading = pl.BlockSpec((cap_row, col_count, width, BLK, BLK), lambda i, c, r, p, f: (0,) * 5)
    return pl.pallas_call(
        body,
        grid_spec=pltpu.PrefetchScalarGridSpec(
            num_scalar_prefetch=4,
            grid=(1,),
            in_specs=[corner] + [leading] * count,
            out_specs=corner,
        ),
        out_shape=jax.ShapeDtypeStruct((RP, RP), F32),
        compiler_params=params(),
        cost_estimate=cost(0, 8 * RP * RP + 4 * count * cap_row * col_count * width * BLK * BLK),
    )(row_child, row_place, jnp.concatenate(col_places, axis=1), flag.reshape(1), root, *outgoing)


def advance(root, parts, own_rows, columns, row_slot, row_valid, col_places, flags):
    rows, cols = root.shape
    row_blocks = rows // BLK
    count = len(parts)
    _, col_count, width, _, _ = parts[0].shape
    step = next(w for w in (512, 384, 256) if cols % w == 0)
    tall = 2 if row_blocks % 2 == 0 else 1
    high = tall * BLK

    def body(slot_ref, valid_ref, place_ref, flag_ref, root_ref, *rest):
        a_refs = rest[: 2 * tall * count]
        own_ref, col_ref, out_ref, hi_ref, lo_ref = rest[2 * tall * count :]
        r = pl.program_id(0)

        @pl.when(r == 0)
        def _():
            hi, lo = split(col_ref[...])
            hi_ref[...] = hi
            lo_ref[...] = lo

        pivot_rows = (flag_ref[0] == 1) & (r * high < RP)

        @pl.when(pivot_rows)
        def _():
            out_ref[...] = root_ref[...]

        @pl.when(jnp.logical_not(pivot_rows))
        def _():
            a_hi, a_lo = split(own_ref[...])
            stacked = jnp.concatenate([a_hi, a_lo], axis=0)
            for n in range(0, cols, step):
                both = dot_nt(stacked, hi_ref[n : n + step, :])
                total = both[:high] + both[high:] + dot_nt(a_hi, lo_ref[n : n + step, :])
                out_ref[:, n : n + step] = root_ref[:, n : n + step] - total

        for c in range(2):
            for m in range(tall):

                @pl.when(valid_ref[c * row_blocks + r * tall + m] == 1)
                def _():
                    for j in range(count):
                        for q in range(col_count):
                            for u in range(width):
                                col = place_ref[c, (j * col_count + q) * width + u]
                                a_ref = a_refs[(c * tall + m) * count + j]

                                @pl.when(col >= 0)
                                def _():
                                    at = pl.ds(pl.multiple_of(col * BLK, BLK), BLK)
                                    out_ref[m * BLK : (m + 1) * BLK, at] += a_ref[0, q, u]

        @pl.when(flag_ref[1] == 1)
        def _():
            out_ref[:, :RP] = own_ref[...]

    def arrived(c, m):
        return pl.BlockSpec(
            (1, col_count, width, BLK, BLK),
            lambda r, s, v, p, f: (s[c * row_blocks + r * tall + m], 0, 0, 0, 0),
        )

    return pl.pallas_call(
        body,
        grid_spec=pltpu.PrefetchScalarGridSpec(
            num_scalar_prefetch=4,
            grid=(row_blocks // tall,),
            in_specs=[pl.BlockSpec((high, cols), lambda r, s, v, p, f: (r, 0))]
            + [arrived(c, m) for c in range(2) for m in range(tall) for _ in range(count)]
            + [
                pl.BlockSpec((high, RP), lambda r, s, v, p, f: (r, 0)),
                pl.BlockSpec((cols, RP), lambda r, s, v, p, f: (0, 0)),
            ],
            out_specs=pl.BlockSpec((high, cols), lambda r, s, v, p, f: (r, 0)),
            scratch_shapes=[pltpu.VMEM((cols, RP), BF16), pltpu.VMEM((cols, RP), BF16)],
        ),
        out_shape=jax.ShapeDtypeStruct((rows, cols), F32),
        compiler_params=params(),
        cost_estimate=cost(6 * rows * cols * RP, 8 * rows * cols + 4 * sum(p.size for p in parts)),
    )(
        row_slot,
        row_valid,
        jnp.concatenate(col_places, axis=1),
        flags,
        root,
        *(parts * (2 * tall)),
        own_rows,
        columns,
    )


def deliver(root, part, row_slot, row_valid, col_place):
    rows, cols = root.shape
    row_blocks = rows // BLK
    _, col_count, width, _, _ = part.shape

    def body(slot_ref, valid_ref, place_ref, root_ref, a0_ref, a1_ref, out_ref):
        r = pl.program_id(0)
        out_ref[...] = root_ref[...]
        for c, a_ref in enumerate((a0_ref, a1_ref)):

            @pl.when(valid_ref[c * row_blocks + r] == 1)
            def _():
                for q in range(col_count):
                    for u in range(width):
                        col = place_ref[c, q * width + u]

                        @pl.when(col >= 0)
                        def _():
                            at = pl.ds(pl.multiple_of(col * BLK, BLK), BLK)
                            out_ref[:, at] += a_ref[0, q, u]

    def arrived(c):
        return pl.BlockSpec(
            (1, col_count, width, BLK, BLK), lambda r, s, v, p: (s[c * row_blocks + r], 0, 0, 0, 0)
        )

    whole = pl.BlockSpec((BLK, cols), lambda r, s, v, p: (r, 0))
    return pl.pallas_call(
        body,
        grid_spec=pltpu.PrefetchScalarGridSpec(
            num_scalar_prefetch=3,
            grid=(row_blocks,),
            in_specs=[whole, arrived(0), arrived(1)],
            out_specs=whole,
        ),
        out_shape=jax.ShapeDtypeStruct((rows, cols), F32),
        compiler_params=params(),
        cost_estimate=cost(0, 8 * rows * cols + 4 * part.size),
    )(row_slot, row_valid, col_place, root, part, part)


def shards(child_update, child_panel, root_front, index_map):
    col_count = lax.axis_size("pcol")
    row_count = lax.axis_size("prow")
    group_count = 2 * col_count
    half = lax.axis_index("half")
    pcol = lax.axis_index("pcol")
    prow = lax.axis_index("prow")
    group = half * col_count + pcol
    rows_dev = child_update.shape[1]
    root_rows, root_cols = root_front.shape
    child_blocks = rows_dev // BLK
    col_blocks = child_update.shape[2] // BLK
    row_blocks = root_rows // BLK
    group_cols = root_cols // BLK
    ratio = root_cols // root_rows
    cap_col = max(1, col_blocks // group_count)
    cap_row = max(1, 2 * child_blocks // row_count)
    cap_pick = cap_row * ratio
    even = col_blocks == group_count * cap_col and 2 * child_blocks == row_count * cap_row
    halves = 2 if even and cap_pick % 2 == 0 and cap_col % 2 == 0 else 1
    half_col, half_pick = cap_col // halves, cap_pick // halves
    width = half_col // 2 if half_col % 2 == 0 else half_col
    iota = functools.partial(jnp.arange, dtype=jnp.int32)
    own_panel = child_panel[0]
    other_panel = lax.ppermute(own_panel, "half", [(0, 1), (1, 0)])

    by_col = index_map.reshape(2, col_count, col_blocks)
    by_row = index_map.reshape(2, row_count, child_blocks)
    key = by_row // group_cols
    if halves == 2:
        in_group = key[..., None] == iota(group_count)
        named = jnp.sum(in_group.astype(jnp.int32), axis=2)
        leading = jnp.sum((in_group & (by_row[..., None] < RP // BLK)).astype(jnp.int32), axis=2)
        least = jnp.maximum(jnp.maximum(half_pick - named[1], leading[0]), 0)
        most = jnp.minimum(jnp.minimum(named[0], half_pick - leading[1]), half_pick)
        least = least.reshape(col_count, row_count // col_count, group_count)
        room = most.reshape(least.shape) - least
        rest = half_col - jnp.sum(least, axis=1, keepdims=True)
        taken = least + jnp.clip(rest - (jnp.cumsum(room, axis=1) - room), 0, room)
        taken = taken.reshape(row_count, group_count)
        taken = jnp.stack([taken, half_pick - taken])
        ahead = (by_row[..., None, :] < by_row[..., :, None]) & (key[..., None, :] == key[..., :, None])
        place_in = jnp.sum(ahead.astype(jnp.int32), axis=-1)
        limit = jnp.sum(jnp.where(in_group, taken[:, :, None, :], 0), axis=-1)
        key = 2 * key + (place_in >= limit).astype(jnp.int32)

    col_key = key.reshape(2, col_count, col_blocks)
    before = (col_key[..., None, :] == col_key[..., :, None]) & (
        iota(col_blocks)[None, :] < iota(col_blocks)[:, None]
    )
    col_key = col_key * half_col + jnp.sum(before.astype(jnp.int32), axis=-1)
    own_key = lax.dynamic_index_in_dim(
        col_key.reshape(group_count, col_blocks), group, 0, keepdims=False
    )
    chosen = jnp.sum(
        jnp.where(own_key[None, :] == iota(group_count * cap_col)[:, None], iota(col_blocks), 0),
        axis=1,
    ).reshape(group_count, halves, half_col)

    joint = by_row.transpose(1, 0, 2).reshape(row_count, 2 * child_blocks)
    items = 2 * child_blocks
    earlier = iota(items)[None, :] < iota(items)[:, None]
    owner = joint // row_blocks
    row_rank = jnp.sum(
        ((owner[:, None, :] == owner[:, :, None]) & earlier).astype(jnp.int32), axis=-1
    )
    joint_key = key.transpose(1, 0, 2).reshape(row_count, items)
    pick_rank = jnp.sum(
        ((joint_key[:, None, :] == joint_key[:, :, None]) & earlier).astype(jnp.int32), axis=-1
    )
    here = lax.dynamic_index_in_dim
    own_owner = here(owner, prow, 0, keepdims=False)
    own_row_rank = here(row_rank, prow, 0, keepdims=False)
    own_pick = here(joint_key * half_pick + pick_rank, prow, 0, keepdims=False)
    pick_item = jnp.sum(
        jnp.where(own_pick[None, :] == (group * cap_pick + iota(cap_pick))[:, None], iota(items), 0),
        axis=1,
    )
    item_slot = own_owner * cap_row + own_row_rank

    code = (iota(row_count)[:, None] * half_pick + pick_rank).reshape(row_count, 2, child_blocks)
    slot_of = code.transpose(1, 0, 2).reshape(2, col_count, col_blocks)
    match = col_key[:, :, None, :] == (group * cap_col + iota(cap_col))[:, None]
    place = jnp.sum(jnp.where(match, slot_of[:, :, None, :], 0), axis=-1)
    col_local = (
        jnp.sum(jnp.where(match, by_col[:, :, None, :] - group * group_cols + 1, 0), axis=-1) - 1
    )

    row_slot = (iota(row_count)[:, None] * cap_row + row_rank).reshape(row_count, 2, child_blocks)
    row_match = by_row[..., None] == prow * row_blocks + iota(row_blocks)
    row_slot = jnp.sum(
        jnp.where(row_match, row_slot.transpose(1, 0, 2)[..., None] + 1, 0), axis=(1, 2)
    )
    row_valid = (row_slot > 0).astype(jnp.int32).reshape(-1)
    row_slot = jnp.maximum(row_slot - 1, 0).reshape(-1)

    pick_mine = (pick_item // child_blocks == half).astype(jnp.int32)
    picked = []
    for h in range(halves):
        at = slice(h * half_pick, (h + 1) * half_pick)
        picked.append(pick_rows(own_panel, other_panel, pick_item[at] % child_blocks, pick_mine[at]))

    device = lambda g, r: ((g // col_count) * row_count + r) * col_count + g % col_count
    everyone = ("half", "prow", "pcol")
    distance = (group + iota(group_count)) % group_count
    origins = (group - iota(group_count)) % group_count
    arrived = []
    packed = [pack_columns(child_update[0], chosen[distance, h]) for h in range(halves)]
    origins, picked[1:], packed[1:] = lax.optimization_barrier((origins, picked[1:], packed[1:]))
    panels = [lax.all_gather(value, "prow", axis=0, tiled=True) for value in picked]
    for h in range(halves):
        if arrived:
            packed[h], arrived[-1][col_count] = lax.optimization_barrier(
                (packed[h], arrived[-1][col_count])
            )
        got = [packed[h][0]]
        for d in range(1, group_count):
            pairs = [
                (device(g, r), device((g + d) % group_count, r))
                for g in range(group_count)
                for r in range(row_count)
            ]
            got.append(lax.ppermute(packed[h][d], everyone, pairs))
        arrived.append(got)

    exchange = functools.partial(
        lax.all_to_all, axis_name="prow", split_axis=0, concat_axis=0, tiled=True
    )
    spans = [(h, first) for h in range(halves) for first in range(0, half_col, width)]
    early = max(1, len(spans) // halves)
    outgoing, parts, col_places = [], [], []
    to_first = (own_owner == 0)[None, :] & (own_row_rank[None, :] == iota(cap_row)[:, None])
    own_joint = here(joint, prow, 0, keepdims=False)
    row_child = jnp.sum(jnp.where(to_first, iota(items) // child_blocks, 0), axis=1)
    row_place = jnp.sum(jnp.where(to_first, own_joint + 1, 0), axis=1) - 1
    for h, first in spans:
        at = slice(h * half_col + first, h * half_col + first + width)
        col_places.append(col_local[:, :, at].reshape(2, -1))
        if len(outgoing) == 1:
            origins, outgoing[0], arrived = lax.optimization_barrier((origins, outgoing[0], arrived))
        elif outgoing:
            origins, outgoing[-1] = lax.optimization_barrier((origins, outgoing[-1]))
        outgoing.append(
            schur_rows(
                own_panel,
                other_panel,
                arrived[h],
                panels[h],
                half,
                item_slot,
                place[:, :, at].reshape(-1),
                origins,
                row_count * cap_row,
                col_count,
                (first, width),
            )
        )
        if len(outgoing) == early:
            pivot = pivot_part(
                root_front,
                outgoing,
                row_child,
                row_place,
                col_places,
                ((prow == 0) & (group == 0)).astype(jnp.int32),
            )
            step = 1
            while step < row_count:
                pairs = [(r, r ^ step) for r in range(row_count)]
                pivot = pivot + lax.ppermute(pivot, "prow", pairs)
                step *= 2
            parts.append(exchange(outgoing[0]))
            pivot, parts[0] = lax.optimization_barrier((pivot, parts[0]))
            factor = jnp.linalg.cholesky(pivot)
            inverse = lax.linalg.triangular_solve(
                factor, jnp.eye(RP, dtype=F32), left_side=True, lower=True
            )
            origins, inverse = lax.optimization_barrier((origins, inverse))
    parts += [exchange(value) for value in outgoing[1:]]

    raw = first_panel(root_front, parts[:early], row_slot, row_valid, col_places[:early])
    solved = lax.dot_general(raw, inverse, NT, precision=HIGHEST, preferred_element_type=F32)
    top = jnp.where(prow == 0, factor, solved[:RP])
    solved = jnp.concatenate([top, solved[RP:]], axis=0)
    own_rows = jnp.where(group == 0, solved, 0.0)
    for g in range(1, group_count):
        pairs = [(device(0, r), device(g, r)) for r in range(row_count)]
        own_rows = own_rows + lax.ppermute(solved, everyone, pairs)
    groups_of = row_count // ratio
    shift = (prow // ratio - group) % groups_of
    tile = jnp.where(shift == 0, own_rows, 0.0)
    for k in range(1, groups_of):
        pairs = [
            (device(g, g * ratio + o), device(g, ((g + k) % groups_of) * ratio + o))
            for g in range(group_count)
            for o in range(ratio)
        ]
        got = lax.ppermute(own_rows, everyone, pairs)
        tile = jnp.where(shift == k, got, tile)
    tiles = [tile]
    for o in range(1, ratio):
        pairs = [
            (r, (r // ratio) * ratio + (r % ratio + o) % ratio) for r in range(row_count)
        ]
        tiles.append(lax.ppermute(tile, "prow", pairs))
    offset = prow % ratio
    ordered = []
    for o in range(ratio):
        value = tiles[0]
        for k in range(1, ratio):
            value = jnp.where((offset - k) % ratio == o, tiles[k], value)
        ordered.append(value)
    lower_cols = jnp.concatenate(ordered, axis=0)
    flags = jnp.stack([(prow == 0), (group == 0)]).astype(jnp.int32)
    late = max(1, len(parts) - 1)
    root = advance(
        root_front, parts[:late], own_rows, lower_cols, row_slot, row_valid, col_places[:late], flags
    )
    for part, col_place in zip(parts[late:], col_places[late:]):
        root = deliver(root, part, row_slot, row_valid, col_place)
    return root


def solution(mesh):
    return jax.shard_map(
        shards,
        mesh=mesh,
        in_specs=(
            P("half", "prow", "pcol"),
            P("half", "prow", None),
            P("prow", ("half", "pcol")),
            P(),
        ),
        out_specs=P("prow", ("half", "pcol")),
        check_vma=False,
    )
```

```python
import functools

import jax
import jax.numpy as jnp
from jax import lax
from jax.experimental import pallas as pl
from jax.experimental.pallas import tpu as pltpu
from jax.sharding import PartitionSpec as P

BLK = 128
RP = 256
F32 = jnp.float32
BF16 = jnp.bfloat16
HIGHEST = lax.Precision.HIGHEST
NT = (((1,), (1,)), ((), ()))
VMEM_LIMIT = 56 * 1024 * 1024


def split(x):
    hi = x.astype(BF16)
    lo = (x - hi.astype(F32)).astype(BF16)
    return hi, lo


def dot_nt(a, b):
    return lax.dot_general(a, b, NT, preferred_element_type=F32)


def params():
    return pltpu.CompilerParams(vmem_limit_bytes=VMEM_LIMIT)


def cost(flops, nbytes):
    return pl.CostEstimate(flops=int(flops), bytes_accessed=int(nbytes), transcendentals=0)


def pack_columns(update, chosen):
    rows = update.shape[0]
    groups, width = chosen.shape

    def body(chosen_ref, *refs):
        for d in range(groups):
            refs[groups + d][0] = refs[d][...]

    def source(d):
        return pl.BlockSpec((rows, BLK), lambda u, s: (0, s[d * width + u]))

    return pl.pallas_call(
        body,
        grid_spec=pltpu.PrefetchScalarGridSpec(
            num_scalar_prefetch=1,
            grid=(width,),
            in_specs=[source(d) for d in range(groups)],
            out_specs=[pl.BlockSpec((1, rows, BLK), lambda u, s: (u, 0, 0))] * groups,
        ),
        out_shape=[jax.ShapeDtypeStruct((width, rows, BLK), F32)] * groups,
        compiler_params=params(),
        cost_estimate=cost(0, 8 * groups * width * rows * BLK),
    )(chosen.reshape(-1), *([update] * groups))


def pick_rows(own, other, block, mine):
    count = block.shape[0]
    depth = own.shape[1]

    def body(block_ref, mine_ref, own_ref, other_ref, out_ref):
        s = pl.program_id(0)

        @pl.when(mine_ref[s] == 1)
        def _():
            out_ref[0] = own_ref[...]

        @pl.when(mine_ref[s] == 0)
        def _():
            out_ref[0] = other_ref[...]

    spec = pl.BlockSpec((BLK, depth), lambda s, b, m: (b[s], 0))
    return pl.pallas_call(
        body,
        grid_spec=pltpu.PrefetchScalarGridSpec(
            num_scalar_prefetch=2,
            grid=(count,),
            in_specs=[spec, spec],
            out_specs=pl.BlockSpec((1, BLK, depth), lambda s, b, m: (s, 0, 0)),
        ),
        out_shape=jax.ShapeDtypeStruct((count, BLK, depth), F32),
        compiler_params=params(),
        cost_estimate=cost(0, 12 * count * BLK * depth),
    )(block, mine, own, other)


def schur_rows(own, other, arrived, panels, half, item_slot, places, origins, slots, col_count, span):
    groups = len(arrived)
    depth = own.shape[1]
    first, width = span
    rows = arrived[0].shape[1]
    child_blocks = rows // BLK
    tall = 2 if child_blocks % 2 == 0 else 1
    steps = child_blocks // tall
    per_child = col_count * width
    wide = per_child * BLK
    piece = next(w for w in (512, 384, 256, 128) if wide % w == 0)

    def body(half_ref, slot_ref, place_ref, origin_ref, own_ref, other_ref, *rest):
        in_refs = rest[:groups]
        panel_ref, out_ref, staged, hi_ref, lo_ref, total_ref, result, load_sem, store_sem = rest[groups:]
        c = pl.program_id(0)
        step = c * steps + pl.program_id(1)

        @pl.when(step == 0)
        def _():
            @pl.loop(0, 2 * per_child)
            def _(k):
                pltpu.make_async_copy(panel_ref.at[place_ref[k]], staged.at[k], load_sem.at[k]).start()

            @pl.loop(0, 2 * per_child)
            def _(k):
                pltpu.make_async_copy(panel_ref.at[place_ref[k]], staged.at[k], load_sem.at[k]).wait()
                hi, lo = split(staged[k])
                hi_ref[k] = hi
                lo_ref[k] = lo

        a_hi, a_lo = split(jnp.where(c == half_ref[0], own_ref[...], other_ref[...]))
        stacked = jnp.concatenate([a_hi, a_lo], axis=0)
        high = tall * BLK
        at_once = piece // BLK
        for n in range(0, per_child, at_once):
            at = pl.ds(c * per_child + n, at_once)
            both = dot_nt(stacked, hi_ref[at].reshape(piece, depth))
            total = both[:high] + both[high:] + dot_nt(a_hi, lo_ref[at].reshape(piece, depth))
            for k in range(at_once):
                total_ref[n + k] = total[:, k * BLK : (k + 1) * BLK]

        buffer = step % 2

        def store(m, at_step):
            item = at_step * tall + m
            return pltpu.make_async_copy(
                result.at[at_step % 2, m], out_ref.at[slot_ref[item]], store_sem.at[at_step % 2, m]
            )

        @pl.when(step >= 2)
        def _():
            for m in range(tall):
                store(m, step - 2).wait()

        for d in range(groups):

            @pl.when(origin_ref[d] // col_count == c)
            def _():
                q = origin_ref[d] % col_count
                for u in range(width):
                    for m in range(tall):
                        at = slice(m * BLK, (m + 1) * BLK)
                        result[buffer, m, q, u] = in_refs[d][u, at, :] - total_ref[q * width + u, at, :]

        for m in range(tall):
            store(m, step).start()

        @pl.when(step == 2 * steps - 1)
        def _():
            for m in range(tall):
                if steps > 0:
                    store(m, step - 1).wait()
                store(m, step).wait()

    def stay(c, i, mine):
        return jnp.where(c == mine, i, jnp.where(c < mine, 0, steps - 1))

    def arrival(d):
        return pl.BlockSpec(
            (width, tall * BLK, BLK),
            lambda c, i, h, t, p, o: (first // width, stay(c, i, o[d] // col_count), 0),
        )

    return pl.pallas_call(
        body,
        grid_spec=pltpu.PrefetchScalarGridSpec(
            num_scalar_prefetch=4,
            grid=(2, steps),
            in_specs=[
                pl.BlockSpec((tall * BLK, depth), lambda c, i, h, t, p, o: (stay(c, i, h[0]), 0)),
                pl.BlockSpec((tall * BLK, depth), lambda c, i, h, t, p, o: (stay(c, i, 1 - h[0]), 0)),
            ]
            + [arrival(d) for d in range(groups)]
            + [pl.BlockSpec(memory_space=pl.ANY)],
            out_specs=pl.BlockSpec(memory_space=pl.ANY),
            scratch_shapes=[
                pltpu.VMEM((2 * per_child, BLK, depth), F32),
                pltpu.VMEM((2 * per_child, BLK, depth), BF16),
                pltpu.VMEM((2 * per_child, BLK, depth), BF16),
                pltpu.VMEM((per_child, tall * BLK, BLK), F32),
                pltpu.VMEM((2, tall, col_count, width, BLK, BLK), F32),
                pltpu.SemaphoreType.DMA((2 * per_child,)),
                pltpu.SemaphoreType.DMA((2, tall)),
            ],
        ),
        out_shape=jax.ShapeDtypeStruct((slots, col_count, width, BLK, BLK), F32),
        compiler_params=params(),
        cost_estimate=cost(
            12 * rows * wide * depth, 8 * rows * (depth + 2 * wide) + 8 * wide * depth
        ),
    )(half.reshape(1), item_slot, places, origins, own, other, *arrived, panels)


def first_panel(root, parts, row_slot, row_valid, col_places):
    row_blocks = root.shape[0] // BLK
    count = len(parts)
    _, col_count, width, _, _ = parts[0].shape

    def body(slot_ref, valid_ref, place_ref, root_ref, *rest):
        a_refs, out_ref = rest[:-1], rest[-1]
        r = pl.program_id(0)
        out_ref[...] = root_ref[...]
        for c in range(2):
            for k in range(count * col_count * width):
                j, q, u = k // (col_count * width), k // width % col_count, k % width
                col = place_ref[c, k]
                ok = (valid_ref[c * row_blocks + r] == 1) & (col >= 0) & (col < RP // BLK)

                @pl.when(ok)
                def _():
                    at = pl.ds(pl.multiple_of(col * BLK, BLK), BLK)
                    out_ref[:, at] += a_refs[c * count + j][0, q, u]

    def arrived(c):
        return pl.BlockSpec(
            (1, col_count, width, BLK, BLK), lambda r, s, v, p: (s[c * row_blocks + r], 0, 0, 0, 0)
        )

    panel = pl.BlockSpec((BLK, RP), lambda r, s, v, p: (r, 0))
    return pl.pallas_call(
        body,
        grid_spec=pltpu.PrefetchScalarGridSpec(
            num_scalar_prefetch=3,
            grid=(row_blocks,),
            in_specs=[panel] + [arrived(0)] * count + [arrived(1)] * count,
            out_specs=panel,
        ),
        out_shape=jax.ShapeDtypeStruct((root.shape[0], RP), F32),
        compiler_params=params(),
        cost_estimate=cost(0, 8 * root.shape[0] * RP + 4 * sum(p.size for p in parts)),
    )(row_slot, row_valid, jnp.concatenate(col_places, axis=1), root, *parts, *parts)


def pivot_part(root, outgoing, row_child, row_place, col_places, flag):
    count = len(outgoing)
    cap_row = row_child.shape[0]
    _, col_count, width, _, _ = outgoing[0].shape

    def body(child_ref, row_ref, place_ref, flag_ref, root_ref, *rest):
        a_refs, out_ref = rest[:-1], rest[-1]
        out_ref[...] = jnp.where(flag_ref[0] == 1, root_ref[...], 0.0)
        for w in range(cap_row):
            row = row_ref[w]
            for k in range(count * col_count * width):
                j, q, u = k // (col_count * width), k // width % col_count, k % width
                col = place_ref[child_ref[w], k]

                @pl.when((row >= 0) & (row < RP // BLK) & (col >= 0) & (col < RP // BLK))
                def _():
                    at_row = pl.ds(pl.multiple_of(row * BLK, BLK), BLK)
                    at_col = pl.ds(pl.multiple_of(col * BLK, BLK), BLK)
                    out_ref[at_row, at_col] += a_refs[j][w, q, u]

    corner = pl.BlockSpec((RP, RP), lambda i, c, r, p, f: (0, 0))
    leading = pl.BlockSpec((cap_row, col_count, width, BLK, BLK), lambda i, c, r, p, f: (0,) * 5)
    return pl.pallas_call(
        body,
        grid_spec=pltpu.PrefetchScalarGridSpec(
            num_scalar_prefetch=4,
            grid=(1,),
            in_specs=[corner] + [leading] * count,
            out_specs=corner,
        ),
        out_shape=jax.ShapeDtypeStruct((RP, RP), F32),
        compiler_params=params(),
        cost_estimate=cost(0, 8 * RP * RP + 4 * count * cap_row * col_count * width * BLK * BLK),
    )(row_child, row_place, jnp.concatenate(col_places, axis=1), flag.reshape(1), root, *outgoing)


def advance(root, parts, own_rows, columns, row_slot, row_valid, col_places, flags):
    rows, cols = root.shape
    row_blocks = rows // BLK
    count = len(parts)
    _, col_count, width, _, _ = parts[0].shape
    step = next(w for w in (512, 384, 256) if cols % w == 0)
    tall = 2 if row_blocks % 2 == 0 else 1
    high = tall * BLK

    def body(slot_ref, valid_ref, place_ref, flag_ref, root_ref, *rest):
        a_refs = rest[: 2 * tall * count]
        own_ref, col_ref, out_ref, hi_ref, lo_ref = rest[2 * tall * count :]
        r = pl.program_id(0)

        @pl.when(r == 0)
        def _():
            hi, lo = split(col_ref[...])
            hi_ref[...] = hi
            lo_ref[...] = lo

        pivot_rows = (flag_ref[0] == 1) & (r * high < RP)

        @pl.when(pivot_rows)
        def _():
            out_ref[...] = root_ref[...]

        @pl.when(jnp.logical_not(pivot_rows))
        def _():
            a_hi, a_lo = split(own_ref[...])
            stacked = jnp.concatenate([a_hi, a_lo], axis=0)
            for n in range(0, cols, step):
                both = dot_nt(stacked, hi_ref[n : n + step, :])
                total = both[:high] + both[high:] + dot_nt(a_hi, lo_ref[n : n + step, :])
                out_ref[:, n : n + step] = root_ref[:, n : n + step] - total

        for c in range(2):
            for m in range(tall):

                @pl.when(valid_ref[c * row_blocks + r * tall + m] == 1)
                def _():
                    for j in range(count):
                        for q in range(col_count):
                            for u in range(width):
                                col = place_ref[c, (j * col_count + q) * width + u]
                                a_ref = a_refs[(c * tall + m) * count + j]

                                @pl.when(col >= 0)
                                def _():
                                    at = pl.ds(pl.multiple_of(col * BLK, BLK), BLK)
                                    out_ref[m * BLK : (m + 1) * BLK, at] += a_ref[0, q, u]

        @pl.when(flag_ref[1] == 1)
        def _():
            out_ref[:, :RP] = own_ref[...]

    def arrived(c, m):
        return pl.BlockSpec(
            (1, col_count, width, BLK, BLK),
            lambda r, s, v, p, f: (s[c * row_blocks + r * tall + m], 0, 0, 0, 0),
        )

    return pl.pallas_call(
        body,
        grid_spec=pltpu.PrefetchScalarGridSpec(
            num_scalar_prefetch=4,
            grid=(row_blocks // tall,),
            in_specs=[pl.BlockSpec((high, cols), lambda r, s, v, p, f: (r, 0))]
            + [arrived(c, m) for c in range(2) for m in range(tall) for _ in range(count)]
            + [
                pl.BlockSpec((high, RP), lambda r, s, v, p, f: (r, 0)),
                pl.BlockSpec((cols, RP), lambda r, s, v, p, f: (0, 0)),
            ],
            out_specs=pl.BlockSpec((high, cols), lambda r, s, v, p, f: (r, 0)),
            scratch_shapes=[pltpu.VMEM((cols, RP), BF16), pltpu.VMEM((cols, RP), BF16)],
        ),
        out_shape=jax.ShapeDtypeStruct((rows, cols), F32),
        compiler_params=params(),
        cost_estimate=cost(6 * rows * cols * RP, 8 * rows * cols + 4 * sum(p.size for p in parts)),
    )(
        row_slot,
        row_valid,
        jnp.concatenate(col_places, axis=1),
        flags,
        root,
        *(parts * (2 * tall)),
        own_rows,
        columns,
    )


def deliver(root, part, row_slot, row_valid, col_place):
    rows, cols = root.shape
    row_blocks = rows // BLK
    _, col_count, width, _, _ = part.shape

    def body(slot_ref, valid_ref, place_ref, root_ref, a0_ref, a1_ref, out_ref):
        r = pl.program_id(0)
        out_ref[...] = root_ref[...]
        for c, a_ref in enumerate((a0_ref, a1_ref)):

            @pl.when(valid_ref[c * row_blocks + r] == 1)
            def _():
                for q in range(col_count):
                    for u in range(width):
                        col = place_ref[c, q * width + u]

                        @pl.when(col >= 0)
                        def _():
                            at = pl.ds(pl.multiple_of(col * BLK, BLK), BLK)
                            out_ref[:, at] += a_ref[0, q, u]

    def arrived(c):
        return pl.BlockSpec(
            (1, col_count, width, BLK, BLK), lambda r, s, v, p: (s[c * row_blocks + r], 0, 0, 0, 0)
        )

    whole = pl.BlockSpec((BLK, cols), lambda r, s, v, p: (r, 0))
    return pl.pallas_call(
        body,
        grid_spec=pltpu.PrefetchScalarGridSpec(
            num_scalar_prefetch=3,
            grid=(row_blocks,),
            in_specs=[whole, arrived(0), arrived(1)],
            out_specs=whole,
        ),
        out_shape=jax.ShapeDtypeStruct((rows, cols), F32),
        compiler_params=params(),
        cost_estimate=cost(0, 8 * rows * cols + 4 * part.size),
    )(row_slot, row_valid, col_place, root, part, part)


def shards(child_update, child_panel, root_front, index_map):
    col_count = lax.axis_size("pcol")
    row_count = lax.axis_size("prow")
    group_count = 2 * col_count
    half = lax.axis_index("half")
    pcol = lax.axis_index("pcol")
    prow = lax.axis_index("prow")
    group = half * col_count + pcol
    rows_dev = child_update.shape[1]
    root_rows, root_cols = root_front.shape
    child_blocks = rows_dev // BLK
    col_blocks = child_update.shape[2] // BLK
    row_blocks = root_rows // BLK
    group_cols = root_cols // BLK
    ratio = root_cols // root_rows
    cap_col = max(1, col_blocks // group_count)
    cap_row = max(1, 2 * child_blocks // row_count)
    cap_pick = cap_row * ratio
    even = col_blocks == group_count * cap_col and 2 * child_blocks == row_count * cap_row
    halves = 2 if even and cap_pick % 2 == 0 and cap_col % 2 == 0 else 1
    half_col, half_pick = cap_col // halves, cap_pick // halves
    width = half_col // 2 if half_col % 2 == 0 else half_col
    iota = functools.partial(jnp.arange, dtype=jnp.int32)
    own_panel = child_panel[0]
    other_panel = lax.ppermute(own_panel, "half", [(0, 1), (1, 0)])

    by_col = index_map.reshape(2, col_count, col_blocks)
    by_row = index_map.reshape(2, row_count, child_blocks)
    key = by_row // group_cols
    if halves == 2:
        in_group = key[..., None] == iota(group_count)
        named = jnp.sum(in_group.astype(jnp.int32), axis=2)
        leading = jnp.sum((in_group & (by_row[..., None] < RP // BLK)).astype(jnp.int32), axis=2)
        least = jnp.maximum(jnp.maximum(half_pick - named[1], leading[0]), 0)
        most = jnp.minimum(jnp.minimum(named[0], half_pick - leading[1]), half_pick)
        least = least.reshape(col_count, row_count // col_count, group_count)
        room = most.reshape(least.shape) - least
        rest = half_col - jnp.sum(least, axis=1, keepdims=True)
        taken = least + jnp.clip(rest - (jnp.cumsum(room, axis=1) - room), 0, room)
        taken = taken.reshape(row_count, group_count)
        taken = jnp.stack([taken, half_pick - taken])
        ahead = (by_row[..., None, :] < by_row[..., :, None]) & (key[..., None, :] == key[..., :, None])
        place_in = jnp.sum(ahead.astype(jnp.int32), axis=-1)
        limit = jnp.sum(jnp.where(in_group, taken[:, :, None, :], 0), axis=-1)
        key = 2 * key + (place_in >= limit).astype(jnp.int32)

    col_key = key.reshape(2, col_count, col_blocks)
    before = (col_key[..., None, :] == col_key[..., :, None]) & (
        iota(col_blocks)[None, :] < iota(col_blocks)[:, None]
    )
    col_key = col_key * half_col + jnp.sum(before.astype(jnp.int32), axis=-1)
    own_key = lax.dynamic_index_in_dim(
        col_key.reshape(group_count, col_blocks), group, 0, keepdims=False
    )
    chosen = jnp.sum(
        jnp.where(own_key[None, :] == iota(group_count * cap_col)[:, None], iota(col_blocks), 0),
        axis=1,
    ).reshape(group_count, halves, half_col)

    joint = by_row.transpose(1, 0, 2).reshape(row_count, 2 * child_blocks)
    items = 2 * child_blocks
    earlier = iota(items)[None, :] < iota(items)[:, None]
    owner = joint // row_blocks
    row_rank = jnp.sum(
        ((owner[:, None, :] == owner[:, :, None]) & earlier).astype(jnp.int32), axis=-1
    )
    joint_key = key.transpose(1, 0, 2).reshape(row_count, items)
    pick_rank = jnp.sum(
        ((joint_key[:, None, :] == joint_key[:, :, None]) & earlier).astype(jnp.int32), axis=-1
    )
    here = lax.dynamic_index_in_dim
    own_owner = here(owner, prow, 0, keepdims=False)
    own_row_rank = here(row_rank, prow, 0, keepdims=False)
    own_pick = here(joint_key * half_pick + pick_rank, prow, 0, keepdims=False)
    pick_item = jnp.sum(
        jnp.where(own_pick[None, :] == (group * cap_pick + iota(cap_pick))[:, None], iota(items), 0),
        axis=1,
    )
    item_slot = own_owner * cap_row + own_row_rank

    code = (iota(row_count)[:, None] * half_pick + pick_rank).reshape(row_count, 2, child_blocks)
    slot_of = code.transpose(1, 0, 2).reshape(2, col_count, col_blocks)
    match = col_key[:, :, None, :] == (group * cap_col + iota(cap_col))[:, None]
    place = jnp.sum(jnp.where(match, slot_of[:, :, None, :], 0), axis=-1)
    col_local = (
        jnp.sum(jnp.where(match, by_col[:, :, None, :] - group * group_cols + 1, 0), axis=-1) - 1
    )

    row_slot = (iota(row_count)[:, None] * cap_row + row_rank).reshape(row_count, 2, child_blocks)
    row_match = by_row[..., None] == prow * row_blocks + iota(row_blocks)
    row_slot = jnp.sum(
        jnp.where(row_match, row_slot.transpose(1, 0, 2)[..., None] + 1, 0), axis=(1, 2)
    )
    row_valid = (row_slot > 0).astype(jnp.int32).reshape(-1)
    row_slot = jnp.maximum(row_slot - 1, 0).reshape(-1)

    pick_mine = (pick_item // child_blocks == half).astype(jnp.int32)
    picked = []
    for h in range(halves):
        at = slice(h * half_pick, (h + 1) * half_pick)
        picked.append(pick_rows(own_panel, other_panel, pick_item[at] % child_blocks, pick_mine[at]))

    device = lambda g, r: ((g // col_count) * row_count + r) * col_count + g % col_count
    everyone = ("half", "prow", "pcol")
    distance = (group + iota(group_count)) % group_count
    origins = (group - iota(group_count)) % group_count
    arrived = []
    packed = [pack_columns(child_update[0], chosen[distance, h]) for h in range(halves)]
    origins, picked[1:], packed[1:] = lax.optimization_barrier((origins, picked[1:], packed[1:]))
    panels = [lax.all_gather(value, "prow", axis=0, tiled=True) for value in picked]
    for h in range(halves):
        if arrived:
            packed[h], arrived[-1][col_count] = lax.optimization_barrier(
                (packed[h], arrived[-1][col_count])
            )
        got = [packed[h][0]]
        for d in range(1, group_count):
            pairs = [
                (device(g, r), device((g + d) % group_count, r))
                for g in range(group_count)
                for r in range(row_count)
            ]
            got.append(lax.ppermute(packed[h][d], everyone, pairs))
        arrived.append(got)

    exchange = functools.partial(
        lax.all_to_all, axis_name="prow", split_axis=0, concat_axis=0, tiled=True
    )
    spans = [(h, first) for h in range(halves) for first in range(0, half_col, width)]
    early = max(1, len(spans) // halves)
    outgoing, parts, col_places = [], [], []
    to_first = (own_owner == 0)[None, :] & (own_row_rank[None, :] == iota(cap_row)[:, None])
    own_joint = here(joint, prow, 0, keepdims=False)
    row_child = jnp.sum(jnp.where(to_first, iota(items) // child_blocks, 0), axis=1)
    row_place = jnp.sum(jnp.where(to_first, own_joint + 1, 0), axis=1) - 1
    for h, first in spans:
        at = slice(h * half_col + first, h * half_col + first + width)
        col_places.append(col_local[:, :, at].reshape(2, -1))
        if len(outgoing) == 1:
            parts.append(exchange(outgoing[0]))
            origins, outgoing[0], arrived = lax.optimization_barrier((origins, outgoing[0], arrived))
        elif outgoing:
            origins, outgoing[-1] = lax.optimization_barrier((origins, outgoing[-1]))
        outgoing.append(
            schur_rows(
                own_panel,
                other_panel,
                arrived[h],
                panels[h],
                half,
                item_slot,
                place[:, :, at].reshape(-1),
                origins,
                row_count * cap_row,
                col_count,
                (first, width),
            )
        )
        if len(outgoing) == early:
            pivot = pivot_part(
                root_front,
                outgoing,
                row_child,
                row_place,
                col_places,
                ((prow == 0) & (group == 0)).astype(jnp.int32),
            )
            step = 1
            while step < row_count:
                pairs = [(r, r ^ step) for r in range(row_count)]
                pivot = pivot + lax.ppermute(pivot, "prow", pairs)
                step *= 2
            origins, pivot = lax.optimization_barrier((origins, pivot))
        elif len(outgoing) == early + 1:
            pivot, outgoing[-1] = lax.optimization_barrier((pivot, outgoing[-1]))
    factor = jnp.linalg.cholesky(pivot)
    inverse = lax.linalg.triangular_solve(
        factor, jnp.eye(RP, dtype=F32), left_side=True, lower=True
    )
    parts += [exchange(value) for value in outgoing[len(parts) :]]

    raw = first_panel(root_front, parts[:early], row_slot, row_valid, col_places[:early])
    solved = lax.dot_general(raw, inverse, NT, precision=HIGHEST, preferred_element_type=F32)
    top = jnp.where(prow == 0, factor, solved[:RP])
    solved = jnp.concatenate([top, solved[RP:]], axis=0)
    own_rows = jnp.where(group == 0, solved, 0.0)
    for g in range(1, group_count):
        pairs = [(device(0, r), device(g, r)) for r in range(row_count)]
        own_rows = own_rows + lax.ppermute(solved, everyone, pairs)
    groups_of = row_count // ratio
    shift = (prow // ratio - group) % groups_of
    tile = jnp.where(shift == 0, own_rows, 0.0)
    for k in range(1, groups_of):
        pairs = [
            (device(g, g * ratio + o), device(g, ((g + k) % groups_of) * ratio + o))
            for g in range(group_count)
            for o in range(ratio)
        ]
        got = lax.ppermute(own_rows, everyone, pairs)
        tile = jnp.where(shift == k, got, tile)
    tiles = [tile]
    for o in range(1, ratio):
        pairs = [
            (r, (r // ratio) * ratio + (r % ratio + o) % ratio) for r in range(row_count)
        ]
        tiles.append(lax.ppermute(tile, "prow", pairs))
    offset = prow % ratio
    ordered = []
    for o in range(ratio):
        value = tiles[0]
        for k in range(1, ratio):
            value = jnp.where((offset - k) % ratio == o, tiles[k], value)
        ordered.append(value)
    lower_cols = jnp.concatenate(ordered, axis=0)
    flags = jnp.stack([(prow == 0), (group == 0)]).astype(jnp.int32)
    late = max(1, len(parts) - 1)
    root = advance(
        root_front, parts[:late], own_rows, lower_cols, row_slot, row_valid, col_places[:late], flags
    )
    for part, col_place in zip(parts[late:], col_places[late:]):
        root = deliver(root, part, row_slot, row_valid, col_place)
    return root


def solution(mesh):
    return jax.shard_map(
        shards,
        mesh=mesh,
        in_specs=(
            P("half", "prow", "pcol"),
            P("half", "prow", None),
            P("prow", ("half", "pcol")),
            P(),
        ),
        out_specs=P("prow", ("half", "pcol")),
        check_vma=False,
    )
```
